32 devices in a mesh: clip: 8 (over z, y), head: 4 (over x, core).
Axes of the slice: x: 2, y: 2, z: 4, core: 2. Of those that a mesh axis runs over, the one named last changes fastest.
Arguments:
- patch_tokens: bfloat16 [8, 8, 196, 768], P('clip', 'head'), may hold values from -6 to 6
- class_token: bfloat16 [8, 768], P('clip'), may hold values from -6 to 6
- keep_mask: int32 [8, 8, 196], P('clip'), may hold values from 0 to 1, as said below
- patch_grad: bfloat16 [8, 8, 196, 768], P('clip', 'head'), may hold values from -6 to 6
- class_grad: bfloat16 [8, 768], P('clip'), may hold values from -6 to 6
- norm_gain: float32 [1, 3, 768], replicated, may hold values from 0.5 to 1.5
- norm_bias: float32 [1, 3, 768], replicated, may hold values from -1.75 to 1.75
- input_weight: bfloat16 [1, 2, 768, 3, 768], P(None, None, None, None, 'head'), may hold values from -0.21875 to 0.21875
- input_bias: float32 [1, 2, 2, 768], P(None, None, None, 'head'), may hold values from -1.75 to 1.75
- output_weight: bfloat16 [1, 2, 768, 768], P(None, None, 'head'), may hold values from -0.875 to 0.875
- time_mixer: bfloat16 [1, 768, 768], replicated, may hold values from -0.21875 to 0.21875
- output_bias: float32 [1, 4, 768], replicated, may hold values from -1.75 to 1.75
- hidden_weight: bfloat16 [1, 768, 3072], P(None, None, 'head'), may hold values from -0.21875 to 0.21875
- hidden_bias: float32 [1, 3072], P(None, 'head'), may hold values from -1.75 to 1.75
- return_weight: bfloat16 [1, 3072, 768], P(None, 'head'), may hold values from -0.109375 to 0.109375
Outputs:
- patch_out: float32 [8, 8, 196, 768], P('clip', 'head')
- class_out: float32 [8, 768], P('clip', 'head')
- patch_input_grad: float32 [8, 8, 196, 768], P('clip', 'head')
- class_input_grad: float32 [8, 768], P('clip', 'head')
- grad_norm_gain: float32 [1, 3, 768], P(None, None, ('clip', 'head'))
- grad_norm_bias: float32 [1, 3, 768], P(None, None, ('clip', 'head'))
- grad_input_weight: float32 [1, 2, 768, 3, 768], P(None, None, 'clip', None, 'head')
- grad_input_bias: float32 [1, 2, 2, 768], P(None, None, None, ('head', 'clip'))
- grad_output_weight: float32 [1, 2, 768, 768], P(None, None, 'head', 'clip')
- grad_time_mixer: float32 [1, 768, 768], P(None, ('clip', 'head'))
- grad_output_bias: float32 [1, 4, 768], P(None, None, ('clip', 'head'))
- grad_hidden_weight: float32 [1, 768, 3072], P(None, 'clip', 'head')
- grad_hidden_bias: float32 [1, 3072], P(None, ('head', 'clip'))
- grad_return_weight: float32 [1, 3072, 768], P(None, 'head', 'clip')
The draws below stay inside these ranges and needn't reach their ends.
Inputs may be any that keep to these rules, and one draw needn't show every extreme that they name: `keep_mask`: 1 keeps the patch token, 0 drops it; the share kept differs from clip to clip and from frame to frame.
All inputs are finite; a program needn't handle non-finite values.
Results may differ from the reference program's by a relative error of at most 0.03.
Values may be sent and summed in bfloat16 or wider, within the bound.
A program may use at most 192 MiB of HBM per device.

```python
import jax
import jax.numpy as jnp
from jax import lax

D = 768
HEADS = 12
HEAD_DIM = 64
MLP = 3072
FRAMES = 8
PATCHES = 196
LAYERS = 1
CLIPS = 8


def draw_keep_mask(key, part):
    key = jax.random.fold_in(key, 7)
    clip_key, frame_key, cell_key = jax.random.split(key, 3)
    clip_rate = jax.random.randint(clip_key, (CLIPS, 1, 1), 74, 107)
    frame_rate = clip_rate + jax.random.randint(frame_key, (CLIPS, FRAMES, 1), -10, 11)
    cell_draw = jax.random.randint(cell_key, (CLIPS, FRAMES, PATCHES), 0, 100)
    return (cell_draw < frame_rate).astype(jnp.int32)


def block_scale(stream_key, extent, cuts, smallest, top_value):
    level, own = 1.0, jax.random.fold_in(stream_key, 6)
    for position, parts in cuts:
        heights = jnp.exp(jax.random.uniform(jax.random.fold_in(own, position), (parts,), jnp.float32, smallest / len(cuts), top_value / len(cuts)))
        level = level * jnp.repeat(heights, extent[position] // parts).reshape([-1 if axis == position else 1 for axis in range(len(extent))])
    return level


def bell_draw(key, extent, scale, most, pieces=(), kind=jnp.bfloat16):
    entries = scale * jax.random.normal(key, extent, jnp.float32)
    if pieces:
        entries = entries * block_scale(key, extent, pieces, -0.22, 0.18)
    return jnp.clip(entries, -most, most).astype(kind)


def setup_inputs(seed: int = 0) -> dict:
    key_list = jax.random.split(jax.random.key(seed), 16)
    patch_tokens = bell_draw(key_list[0], (CLIPS, FRAMES, PATCHES, D), 1.0, 6.0, ((0, 8), (1, 4)))
    class_token = bell_draw(key_list[1], (CLIPS, D), 1.0, 6.0, ((0, 8),))
    keep_mask = draw_keep_mask(jax.random.fold_in(key_list[15], 71), 0)
    patch_grad = bell_draw(key_list[3], (CLIPS, FRAMES, PATCHES, D), 1.0, 6.0, ((0, 8), (1, 4)))
    class_grad = bell_draw(key_list[4], (CLIPS, D), 1.0, 6.0, ((0, 8),))
    norm_gain = jnp.clip(1.0 + 0.1 * jax.random.normal(key_list[5], (LAYERS, 3, D), jnp.float32), 0.5, 1.5)
    norm_bias = bell_draw(key_list[6], (LAYERS, 3, D), 0.3, 1.75, (), jnp.float32)
    input_weight = bell_draw(key_list[7], (LAYERS, 2, D, 3, D), D ** -0.5, 0.21875, ((4, 4),))
    input_bias = bell_draw(key_list[8], (LAYERS, 2, 2, D), 0.3, 1.75, ((3, 4),), jnp.float32)
    output_weight = bell_draw(key_list[9], (LAYERS, 2, D, D), (D // 16) ** -0.5, 0.875, ((2, 4),))
    time_mixer = bell_draw(key_list[10], (LAYERS, D, D), D ** -0.5, 0.21875)
    output_bias = bell_draw(key_list[11], (LAYERS, 4, D), 0.3, 1.75, (), jnp.float32)
    hidden_weight = bell_draw(key_list[12], (LAYERS, D, MLP), D ** -0.5, 0.21875, ((2, 4),))
    hidden_bias = bell_draw(key_list[13], (LAYERS, MLP), 0.3, 1.75, ((1, 4),), jnp.float32)
    return_weight = bell_draw(key_list[14], (LAYERS, MLP, D), MLP ** -0.5, 0.109375, ((1, 4),))
    return dict(patch_tokens=patch_tokens, class_token=class_token, keep_mask=keep_mask, patch_grad=patch_grad, class_grad=class_grad, norm_gain=norm_gain, norm_bias=norm_bias, input_weight=input_weight, input_bias=input_bias, output_weight=output_weight, time_mixer=time_mixer, output_bias=output_bias, hidden_weight=hidden_weight, hidden_bias=hidden_bias, return_weight=return_weight)


@jax.custom_vjp
def low(v):
    return lax.optimization_barrier(v.astype(jnp.bfloat16)).astype(jnp.float32)

@jax.custom_vjp
def low_back(v):
    return v

def low_keep(v):
    return (low(v), None)

def low_pass(kept, grad):
    return (grad,)

def back_keep(v):
    return (v, None)

def back_low(kept, grad):
    return (low(grad),)
low.defvjp(low_keep, low_pass)
low_back.defvjp(back_keep, back_low)
EPSILON = 1e-06
MASKED = -1e+30
HIGHEST = lax.Precision.HIGHEST

def layer_norm(values, gains, shifts):
    average = lax.optimization_barrier(jnp.mean(values, axis=-1, keepdims=True))
    centred = values - average
    spread = lax.optimization_barrier(jnp.mean(centred * centred, axis=-1, keepdims=True))
    return centred * lax.rsqrt(spread + EPSILON) * gains + shifts

def rounded_pair(values):
    return low(low_back(values))

def masked_softmax(scores, allowed):
    scores = jnp.where(allowed, low_back(scores), MASKED)
    row_max = lax.optimization_barrier(jnp.max(scores, axis=-1, keepdims=True))
    exponent = jnp.exp(scores - row_max)
    return low(exponent / lax.optimization_barrier(jnp.sum(exponent, axis=-1, keepdims=True)))

def project(normed, weight, biases):
    mixed = jnp.einsum('...d,dje->...je', normed, weight, precision=HIGHEST)
    return (rounded_pair(mixed[..., 0, :] + biases[0]), rounded_pair(mixed[..., 1, :]), rounded_pair(mixed[..., 2, :] + biases[1]))

def split_heads(values):
    return values.reshape(values.shape[:-1] + (HEADS, HEAD_DIM))

def time_attention(queries, keys, values, keep_frames):
    scores = jnp.einsum('fphd,gphd->phfg', queries, keys, precision=HIGHEST) * HEAD_DIM ** (-0.5)
    allowed = (keep_frames.T > 0)[:, None, None, :] | jnp.eye(FRAMES, dtype=jnp.bool_)
    weights = masked_softmax(scores, allowed)
    return jnp.einsum('phfg,gphd->fphd', weights, values, precision=HIGHEST)

def frames_of(patch_part, class_part):
    class_rows = jnp.broadcast_to(class_part[None, None], (FRAMES, 1, HEADS, HEAD_DIM))
    return jnp.concatenate([class_rows, patch_part], axis=1)

def space_attention(patch_q, patch_k, patch_v, class_q, class_k, class_v, keep_frames):
    queries = frames_of(patch_q, class_q)
    keys = frames_of(patch_k, class_k)
    values = frames_of(patch_v, class_v)
    scores = jnp.einsum('fqhd,fkhd->fhqk', queries, keys, precision=HIGHEST) * HEAD_DIM ** (-0.5)
    valid = jnp.concatenate([jnp.ones((FRAMES, 1), jnp.bool_), keep_frames > 0], axis=1)
    allowed = valid[:, None, None, :] | jnp.eye(PATCHES + 1, dtype=jnp.bool_)
    weights = masked_softmax(scores, allowed)
    outputs = jnp.einsum('fhqk,fkhd->fqhd', weights, values, precision=HIGHEST)
    return (outputs[:, 1:], lax.optimization_barrier(jnp.mean(outputs[:, 0], axis=0)))

def run_forward(weights, patch_state, class_state, keep_frames):
    norm_gain, norm_bias, input_weight, input_bias, output_weight, time_mixer, output_bias, hidden_weight, hidden_bias, return_weight = weights
    for layer_index in range(LAYERS):
        gains = norm_gain[layer_index]
        shifts = norm_bias[layer_index]
        biases = output_bias[layer_index]
        time_normed = low(layer_norm(patch_state, gains[0], shifts[0]))
        time_q, time_k, time_v = project(time_normed, input_weight[layer_index, 0], input_bias[layer_index, 0])
        time_out = time_attention(split_heads(time_q), split_heads(time_k), split_heads(time_v), keep_frames)
        time_mixed = rounded_pair(time_out.reshape(FRAMES, PATCHES, D))
        time_proj = rounded_pair(jnp.einsum('fpd,de->fpe', time_mixed, output_weight[layer_index, 0], precision=HIGHEST) + biases[0])
        patch_state = patch_state + (low_back(jnp.einsum('fpd,de->fpe', time_proj, time_mixer[layer_index], precision=HIGHEST)) + biases[1])
        space_normed = low(layer_norm(patch_state, gains[1], shifts[1]))
        class_normed = low(layer_norm(class_state, gains[1], shifts[1]))
        patch_q, patch_k, patch_v = project(space_normed, input_weight[layer_index, 1], input_bias[layer_index, 1])
        class_q, class_k, class_v = project(class_normed, input_weight[layer_index, 1], input_bias[layer_index, 1])
        patch_out, class_out = space_attention(split_heads(patch_q), split_heads(patch_k), split_heads(patch_v), split_heads(class_q), split_heads(class_k), split_heads(class_v), keep_frames)
        patch_mixed = rounded_pair(patch_out.reshape(FRAMES, PATCHES, D))
        class_mixed = rounded_pair(class_out.reshape(D))
        patch_state = patch_state + (low_back(jnp.einsum('fpd,de->fpe', patch_mixed, output_weight[layer_index, 1], precision=HIGHEST)) + biases[2])
        class_state = class_state + (low_back(jnp.einsum('d,de->e', class_mixed, output_weight[layer_index, 1], precision=HIGHEST)) + biases[2])
        mlp_normed = low(layer_norm(patch_state, gains[2], shifts[2]))
        class_mlp = low(layer_norm(class_state, gains[2], shifts[2]))
        hidden_rows = low_back(jnp.einsum('fpd,dm->fpm', mlp_normed, hidden_weight[layer_index], precision=HIGHEST) + hidden_bias[layer_index])
        hidden_class = low_back(jnp.einsum('d,dm->m', class_mlp, hidden_weight[layer_index], precision=HIGHEST) + hidden_bias[layer_index])
        active_rows = low(jax.nn.gelu(hidden_rows, approximate=False))
        active_class = low(jax.nn.gelu(hidden_class, approximate=False))
        patch_state = patch_state + (low_back(jnp.einsum('fpm,md->fpd', active_rows, return_weight[layer_index], precision=HIGHEST)) + biases[3])
        class_state = class_state + (low_back(jnp.einsum('m,md->d', active_class, return_weight[layer_index], precision=HIGHEST)) + biases[3])
    return (patch_state * (keep_frames > 0).astype(patch_state.dtype)[..., None], class_state)

def reference(patch_tokens, class_token, keep_mask, patch_grad, class_grad, norm_gain, norm_bias, input_weight, input_bias, output_weight, time_mixer, output_bias, hidden_weight, hidden_bias, return_weight):
    params = tuple((weight.astype(jnp.float32) for weight in (norm_gain, norm_bias, input_weight, input_bias, output_weight, time_mixer, output_bias, hidden_weight, hidden_bias, return_weight)))

    def per_clip(totals, clip_items):
        patch_part, class_part, keep_part, patch_back, class_back = clip_items

        def forward(weights, patch_state, class_state):
            return run_forward(weights, patch_state, class_state, keep_part)
        outputs, pullback = jax.vjp(forward, params, patch_part.astype(jnp.float32), class_part.astype(jnp.float32))
        weight_grads, patch_in_grad, class_in_grad = pullback((patch_back.astype(jnp.float32), class_back.astype(jnp.float32)))
        totals = jax.tree.map(jnp.add, totals, weight_grads)
        return (totals, (outputs[0], outputs[1], patch_in_grad, class_in_grad))
    zero_grads = jax.tree.map(jnp.zeros_like, params)
    totals, stacked = lax.scan(per_clip, zero_grads, (patch_tokens, class_token, keep_mask, patch_grad, class_grad))
    return (stacked[0], stacked[1], stacked[2], stacked[3], totals[0], totals[1], totals[2], totals[3], totals[4], totals[5], totals[6], totals[7], totals[8], totals[9])
```

```python
import functools

import jax
import jax.numpy as jnp
from jax import lax
from jax.experimental import pallas as pl
from jax.experimental.pallas import tpu as pltpu
from jax.sharding import PartitionSpec as P

HEAD_DIM = 64
PAIR = 2 * HEAD_DIM
TILE = 16
EPSILON = 1e-06
MASKED = -1e30
FLOAT = jnp.float32
HALF = jnp.bfloat16
ROW_ROW = (((1,), (1,)), ((), ()))
COL_COL = (((0,), (0,)), ((), ()))
ROOT_HALF = 0.7071067811865476
ROOT_TWO_PI = 0.3989422804014327


def round_up(value, unit):
    return -(-value // unit) * unit


def mm(left, right):
    return jnp.dot(left, right, preferred_element_type=FLOAT)


def mm_t(left, right):
    return lax.dot_general(left, right, ROW_ROW, preferred_element_type=FLOAT)


def t_mm(left, right):
    return lax.dot_general(left, right, COL_COL, preferred_element_type=FLOAT)


def normalize(values):
    average = jnp.mean(values, axis=-1, keepdims=True)
    centred = values - average
    spread = jnp.mean(centred * centred, axis=-1, keepdims=True)
    inverse = lax.rsqrt(spread + EPSILON)
    return centred * inverse, inverse


def normalize_back(scaled, unit, inverse):
    first = jnp.mean(scaled, axis=-1, keepdims=True)
    second = jnp.mean(scaled * unit, axis=-1, keepdims=True)
    return (scaled - first - unit * second) * inverse


def rows_iota(shape):
    return lax.broadcasted_iota(jnp.int32, shape, 0)


def lanes_iota(shape):
    return lax.broadcasted_iota(jnp.int32, shape, 1)


def half_masks():
    lanes = lanes_iota((1, PAIR))
    first = (lanes < HEAD_DIM).astype(HALF)
    return first, (1 - first).astype(HALF)


def softmax_columns(scores):
    top = jnp.max(scores, axis=0, keepdims=True)
    exponent = jnp.exp(scores - top)
    total = jnp.sum(exponent, axis=0, keepdims=True)
    return exponent * (1.0 / total)


def time_norm_kernel(tokens, gains, shifts, out):
    frames, patches, _ = tokens.shape
    rows = out.shape[1]
    for frame in range(frames):
        unit, _ = normalize(tokens[frame].astype(FLOAT))
        out[frame, :patches] = (unit * gains[...] + shifts[...]).astype(HALF)
        out[frame, patches:] = jnp.zeros((rows - patches, out.shape[2]), HALF)


def group_allowed(keep_columns, group):
    shape = (keep_columns.shape[0],) * 2
    key, query = rows_iota(shape), lanes_iota(shape)
    chosen = lanes_iota(keep_columns.shape) == group
    kept = jnp.sum(jnp.where(chosen, keep_columns, 0.0), axis=1, keepdims=True)
    same = lax.rem(key, TILE) == lax.rem(query, TILE)
    return same & ((kept > 0.5) | (key == query))


def time_forward_kernel(heads, blocks, *refs):
    normed = refs[:blocks]
    weight, query_bias, value_bias, keep = refs[blocks : blocks + 4]
    outs = refs[blocks + 4 : 2 * blocks + 4]
    qkv, weights_out = refs[2 * blocks + 4 :]
    frames, rows, width = normed[0].shape
    wide = query_bias.shape[1]
    group_rows = blocks * frames * TILE
    for block in range(blocks):
        mixed = mm_t(normed[block][...].reshape(frames * rows, width), weight[...])
        part = qkv.at[block * frames : (block + 1) * frames]
        query = (mixed[:, :wide] + query_bias[...]).astype(HALF) * (HEAD_DIM**-0.5)
        part[:, :, :wide] = query.astype(HALF).reshape(frames, rows, wide)
        part[:, :, wide : 2 * wide] = (
            mixed[:, wide : 2 * wide].astype(HALF).reshape(frames, rows, wide)
        )
        part[:, :, 2 * wide :] = (
            (mixed[:, 2 * wide :] + value_bias[...]).astype(HALF).reshape(frames, rows, wide)
        )
    keep_columns = keep[...].T
    masks = half_masks()

    def one_group(group, carry):
        spot = pl.ds(pl.multiple_of(group * TILE, TILE), TILE)
        piece = qkv[:, spot, :].reshape(group_rows, 3 * wide)
        allowed = group_allowed(keep_columns, group)
        found = []
        for pair in range(wide // PAIR):
            query = piece[:, pair * PAIR : (pair + 1) * PAIR]
            key = piece[:, wide + pair * PAIR : wide + (pair + 1) * PAIR]
            value = piece[:, 2 * wide + pair * PAIR : 2 * wide + (pair + 1) * PAIR]
            total = jnp.zeros((group_rows, PAIR), FLOAT)
            for side in range(2):
                head = 2 * pair + side
                if head >= heads:
                    continue
                scores = mm_t(key * masks[side], query)
                soft = softmax_columns(jnp.where(allowed, scores, MASKED)).astype(HALF)
                weights_out[group, head] = soft
                total = total + t_mm(soft, value * masks[side])
            found.append(total.astype(HALF))
        joined = jnp.concatenate(found, axis=1)[:, : heads * HEAD_DIM]
        joined = joined.reshape(blocks, frames, TILE, heads * HEAD_DIM)
        for block in range(blocks):
            outs[block][:, spot, :] = joined[block]
        return carry

    lax.fori_loop(0, rows // TILE, one_group, 0)


def gather_rows(dest, parts, first, count):
    for place, part in enumerate(parts):
        dest[place * count : (place + 1) * count, :] = part[first : first + count, :]


def space_forward_kernel(blocks, own_width, *refs):
    tokens, class_token = refs[:2]
    mixed = refs[2 : 2 + blocks]
    bundles = refs[2 + blocks : 2 + 2 * blocks]
    mixer, biases, gains, shifts, query_bias, value_bias, keep = refs[
        2 + 2 * blocks : 9 + 2 * blocks
    ]
    (state_out, proj_out, normed_out, query_out, key_out, value_out, weights_out, spread_out,
     next_out, class_out) = refs[9 + 2 * blocks : 19 + 2 * blocks]
    joint, blocked = refs[19 + 2 * blocks :]
    frames, patches, width = tokens.shape
    rows = state_out.shape[1]
    flat = (frames * rows, width)
    total = jnp.zeros(flat, FLOAT)
    for block in range(blocks):
        total = total + mm(
            mixed[block][...].reshape(frames * rows, own_width), bundles[block][:own_width, :]
        )
    proj = (total + biases[0:1, :]).astype(HALF)
    proj_out[...] = proj.reshape(frames, rows, width)
    added = (mm(proj, mixer[...]) + biases[1:2, :]).reshape(frames, rows, width)
    for frame in range(frames):
        state_out[frame, :patches] = tokens[frame].astype(FLOAT) + added[frame, :patches]
        state_out[frame, patches : patches + 1] = class_token[...].astype(FLOAT)
        state_out[frame, patches + 1 :] = jnp.zeros((rows - patches - 1, width), FLOAT)
    unit, _ = normalize(state_out[...].reshape(flat))
    real = lax.rem(rows_iota((frames * rows, 1)), rows) <= patches
    normed = jnp.where(real, unit * gains[1:2, :] + shifts[1:2, :], 0.0).astype(HALF)
    normed_out[...] = normed.reshape(frames, rows, width)
    for kind, (dest, bias) in enumerate(
        ((query_out, query_bias), (key_out, None), (value_out, value_bias))
    ):
        gather_rows(joint, bundles, (1 + kind) * own_width, own_width)
        raw = mm_t(normed, joint[...])
        if bias is not None:
            raw = raw + bias[...]
        raw = raw.astype(HALF)
        if kind == 0:
            raw = (raw * (HEAD_DIM**-0.5)).astype(HALF)
        dest[...] = raw.reshape(frames, rows, width)
    key_index, query_index = rows_iota((rows, rows)), lanes_iota((rows, rows))
    for frame in range(frames):
        allowed = (
            (keep[:, frame : frame + 1] > 0.5) | (key_index == patches) | (key_index == query_index)
        )
        blocked[frame] = jnp.where(allowed, 0.0, MASKED)
    masks = half_masks()
    for frame in range(frames):

        def one_pair(pair, carry):
            spot = pl.ds(pl.multiple_of(pair * PAIR, PAIR), PAIR)
            query, key, value = query_out[frame, :, spot], key_out[frame, :, spot], value_out[frame, :, spot]
            total = jnp.zeros((rows, PAIR), FLOAT)
            for side in range(2):
                scores = mm_t(key * masks[side], query) + blocked[frame]
                soft = softmax_columns(scores).astype(HALF)
                weights_out[frame, 2 * pair + side] = soft
                total = total + t_mm(soft, value * masks[side])
            spread_out[frame, :, spot] = total.astype(HALF)
            return carry

        lax.fori_loop(0, width // PAIR, one_pair, 0)
    gather_rows(joint, bundles, 4 * own_width, own_width)
    added = mm(spread_out[...].reshape(flat), joint[...]).reshape(frames, rows, width)
    next_out[...] = state_out[...] + added + biases[2:3, :]
    part = added[0, patches : patches + 1]
    for frame in range(1, frames):
        part = part + added[frame, patches : patches + 1]
    class_out[...] = part * (1.0 / (frames * blocks))


def gelu_parts(values):
    size = jnp.abs(values)
    density = jnp.exp(-0.5 * values * values)
    step = 1.0 / (1.0 + (0.3275911 * ROOT_HALF) * size)
    tail = step * (
        0.5 * 0.254829592
        + step
        * (
            0.5 * -0.284496736
            + step * (0.5 * 1.421413741 + step * (0.5 * -1.453152027 + step * (0.5 * 1.061405429)))
        )
    )
    tail = tail * density
    return jnp.where(values < 0.0, tail, 1.0 - tail), density * ROOT_TWO_PI


def mlp_kernel(order, steps_per, *refs):
    blocks = len(order)
    index, state, class_token = refs[:3]
    class_parts = refs[3 : 3 + blocks]
    grads, class_grad, keep, biases, gains, shifts = refs[3 + blocks : 9 + blocks]
    first_weights = refs[9 + blocks : 9 + 2 * blocks]
    second_weights = refs[9 + 2 * blocks : 9 + 3 * blocks]
    hidden_biases = refs[9 + 3 * blocks : 9 + 4 * blocks]
    patch_out, class_out, grad_out, sums_out, hidden_sums, sent, kept = refs[
        9 + 4 * blocks : 16 + 4 * blocks
    ]
    (full, normed, grads_half, normed_t, grads_t, first, second, bias, hidden, back, active,
     hidden_back, total, normed_back) = refs[16 + 4 * blocks :]
    frames, rows, width = state.shape
    patches = grads.shape[1]
    flat = (frames * rows, width)
    cuts, cut = normed_t.shape[:2]
    block_width = first.shape[2]
    step = pl.program_id(0)
    last = pl.num_programs(0) - 1
    lead = (index[1] == 0).astype(FLOAT)
    row = rows_iota((frames * rows, 1))
    is_class = row == patches
    is_real = (lax.rem(row, rows) < patches) | is_class

    @pl.when(step == 0)
    def _():
        full[...] = state[...]
        class_state = class_token[...].astype(FLOAT) + biases[2:3, :]
        for part in class_parts:
            class_state = class_state + part[...]
        full[0, patches : patches + 1] = class_state
        unit, _ = normalize(full[...].reshape(flat))
        values = jnp.where(is_real, unit * gains[2:3, :] + shifts[2:3, :], 0.0)
        normed[...] = values.astype(HALF)
        weighted = jnp.where(is_class, values * lead, values).astype(HALF).T
        for frame in range(frames):
            grad_out[frame, :patches] = grads[frame].astype(FLOAT) * keep[:patches, frame : frame + 1]
            grad_out[frame, patches:] = jnp.zeros((rows - patches, width), FLOAT)
        grad_out[0, patches : patches + 1] = class_grad[...].astype(FLOAT)
        values = grad_out[...].reshape(flat)
        grads_half[...] = values.astype(HALF)
        turned = jnp.where(is_class, values * lead, values)
        sums_out[2:3] = jnp.sum(turned, axis=0, keepdims=True)
        turned = turned.astype(HALF).T
        for part in range(cuts):
            place = jnp.bitwise_xor(part, index[0])
            normed_t[place] = weighted[part * cut : (part + 1) * cut]
            grads_t[place] = turned[part * cut : (part + 1) * cut]
        total[...] = jnp.zeros_like(total)
        normed_back[...] = jnp.zeros_like(normed_back)
        for scratch in (first, second, hidden, back, active, hidden_back):
            scratch[...] = jnp.zeros_like(scratch)

    for place, block in enumerate(order):

        @pl.when((step >= place * steps_per) & (step < (place + 1) * steps_per))
        def _():
            slot = lax.rem(step, 3)
            first[slot] = first_weights[block][...]
            second[slot] = second_weights[block][...]
            bias[...] = hidden_biases[block][...]

    now, before, oldest = lax.rem(step, 3), lax.rem(step + 2, 3), lax.rem(step + 1, 3)
    even, odd = lax.rem(step, 2), lax.rem(step + 1, 2)
    active_old, back_old = active[even], hidden_back[even]
    total[...] += mm(active_old, second[oldest])
    normed_back[...] += mm_t(back_old, first[oldest])
    first_grad = mm(normed_t[...].reshape(width, frames * rows), back_old)
    second_grad = mm(grads_t[...].reshape(width, frames * rows), active_old)
    joined = jnp.concatenate([first_grad.astype(HALF), second_grad.astype(HALF)], axis=1)
    joined = joined.reshape(cuts, cut, 2 * block_width)
    in_sent = step < 2 + (blocks // 2) * steps_per

    @pl.when(in_sent)
    def _():
        sent[0] = joined

    @pl.when(jnp.logical_not(in_sent))
    def _():
        kept[0] = joined

    weights_row = jnp.where(is_class, lead, 1.0)
    hidden_sums[...] = jnp.sum(back_old.astype(FLOAT) * weights_row, axis=0, keepdims=True)[None]
    inner = hidden[odd]
    chance, density = gelu_parts(inner)
    active[odd] = (inner * chance).astype(HALF)
    hidden_back[odd] = (back[odd] * (chance + inner * density)).astype(HALF)
    hidden[even] = mm(normed[...], first[now]) + bias[...]
    back[even] = mm_t(grads_half[...], second[now])

    @pl.when(step == last)
    def _():
        result = (full[...].reshape(flat) + total[...] + biases[3:4, :]).reshape(frames, rows, width)
        for frame in range(frames):
            patch_out[frame] = result[frame, :patches] * keep[:patches, frame : frame + 1]
        class_out[...] = result[0, patches : patches + 1]
        unit, inverse = normalize(full[...].reshape(flat))
        incoming = normed_back[...]
        weighted = jnp.where(is_class, incoming * lead, incoming)
        sums_out[0:1] = jnp.sum(weighted * unit, axis=0, keepdims=True)
        sums_out[1:2] = jnp.sum(weighted, axis=0, keepdims=True)
        sums_out[3:] = jnp.zeros((sums_out.shape[0] - 3, width), FLOAT)
        change = normalize_back(incoming * gains[2:3, :], unit, inverse)
        change = jnp.where(is_real, change, 0.0)
        grad_out[...] += change.reshape(frames, rows, width)


def space_backward_kernel(blocks, own_width, patches, *refs):
    (index, grads, state, query_in, key_in, value_in, weights_in, mixer, gains) = refs[:9]
    bundles = refs[9 : 9 + blocks]
    (grad_out, proj_back, spread_grad, query_back, key_back, value_back, time_grad, class_back,
     sums_out) = refs[9 + blocks : 18 + blocks]
    joint, mixed_back = refs[18 + blocks :]
    frames, rows, width = state.shape
    flat = (frames * rows, width)
    lead = (index[1] == 0).astype(FLOAT)
    row = lax.rem(rows_iota((frames * rows, 1)), rows)
    is_patch = row < patches
    share = 1.0 / (frames * blocks)
    class_grad = grads[0, patches : patches + 1]
    values = grads[...].reshape(flat)
    sums_out[2:3] = (
        jnp.sum(jnp.where(is_patch, values, 0.0), axis=0, keepdims=True) + lead * class_grad
    )
    values = jnp.where(is_patch, values, jnp.where(row == patches, class_grad * share, 0.0))
    half = values.astype(HALF)
    spread_grad[...] = half.reshape(frames, rows, width)
    gather_rows(joint, bundles, 4 * own_width, own_width)
    mixed_back[...] = mm_t(half, joint[...]).astype(HALF).reshape(frames, rows, width)
    masks = half_masks()
    for frame in range(frames):

        def one_pair(pair, carry):
            spot = pl.ds(pl.multiple_of(pair * PAIR, PAIR), PAIR)
            query, key, value = query_in[frame, :, spot], key_in[frame, :, spot], value_in[frame, :, spot]
            outer = mixed_back[frame, :, spot]
            sums = [jnp.zeros((rows, PAIR), FLOAT) for _ in range(3)]
            for side in range(2):
                soft = weights_in[frame, 2 * pair + side]
                mine = outer * masks[side]
                sums[2] = sums[2] + mm(soft, mine)
                weight_back = mm_t(value, mine)
                wide = soft.astype(FLOAT)
                product = wide * weight_back
                score_back = product - wide * jnp.sum(product, axis=0, keepdims=True)
                score_back = score_back.astype(HALF)
                sums[1] = sums[1] + mm(score_back, query * masks[side])
                sums[0] = sums[0] + t_mm(score_back, key * masks[side])
            query_back[frame, :, spot] = (sums[0] * (HEAD_DIM**-0.5)).astype(HALF)
            key_back[frame, :, spot] = sums[1].astype(HALF)
            value_back[frame, :, spot] = sums[2].astype(HALF)
            return carry

        lax.fori_loop(0, width // PAIR, one_pair, 0)
    incoming = jnp.zeros(flat, FLOAT)
    for kind, source in enumerate((query_back, key_back, value_back)):
        gather_rows(joint, bundles, (1 + kind) * own_width, own_width)
        piece = source[...].reshape(flat)
        incoming = incoming + mm(piece, joint[...])
        if kind != 1:
            sums_out[5 + kind // 2 : 6 + kind // 2] = jnp.sum(
                piece.astype(FLOAT), axis=0, keepdims=True
            )
    unit, inverse = normalize(state[...].reshape(flat))
    sums_out[0:1] = jnp.sum(incoming * unit, axis=0, keepdims=True)
    sums_out[1:2] = jnp.sum(incoming, axis=0, keepdims=True)
    shaped = incoming.reshape(frames, rows, width)
    part = shaped[0, patches : patches + 1]
    for frame in range(1, frames):
        part = part + shaped[frame, patches : patches + 1]
    class_back[...] = part
    change = normalize_back(incoming * gains[1:2, :], unit, inverse)
    result = jnp.where(is_patch, grads[...].reshape(flat) + change, 0.0)
    grad_out[...] = result.reshape(frames, rows, width)
    sums_out[3:4] = jnp.sum(result, axis=0, keepdims=True)
    half = result.astype(HALF)
    time_grad[...] = half.reshape(frames, rows, width)
    back = mm_t(half, mixer[...]).astype(HALF)
    proj_back[...] = back.reshape(frames, rows, width)
    sums_out[4:5] = jnp.sum(back.astype(FLOAT), axis=0, keepdims=True)
    sums_out[7:8] = jnp.zeros((1, width), FLOAT)


def space_weights_kernel(order, own_width, *refs):
    (index, normed, query_back, key_back, value_back, spread_grad, spread, proj, time_grad) = refs[:9]
    sent, kept, mixer_grad = refs[9:]
    frames, rows, width = normed.shape
    blocks = len(order)
    cuts, cut = mixer_grad.shape[:2]
    flat = (frames * rows, width)

    def store(found, kind):
        found = found.astype(HALF)
        for part in range(cuts):
            place = jnp.bitwise_xor(part, index[0])
            piece = found[part * cut : (part + 1) * cut]
            if kind is None:
                mixer_grad[place] = piece
                continue
            for spot, block in enumerate(order):
                dest = sent if spot < blocks // 2 else kept
                dest[spot % (blocks // 2), place, :, kind * own_width : (kind + 1) * own_width] = (
                    piece[:, block * own_width : (block + 1) * own_width]
                )

    turned = normed[...].reshape(flat).T
    for kind, source in enumerate((query_back, key_back, value_back)):
        store(mm(turned, source[...].reshape(flat)), kind)
    turned = spread_grad[...].reshape(flat).T
    store(mm(turned, spread[...].reshape(flat)), 3)
    turned = proj[...].reshape(flat).T
    store(mm(turned, time_grad[...].reshape(flat)), None)


def time_backward_kernel(heads, blocks, *refs):
    proj_back = refs[:blocks]
    normed = refs[blocks : 2 * blocks]
    qkv, weights_in, output_weight, weight, gain, shift = refs[2 * blocks : 2 * blocks + 6]
    outs = refs[2 * blocks + 6 : 3 * blocks + 6]
    qkv_back, sums_out, norm_sums, mixed_back = refs[3 * blocks + 6 :]
    frames, rows, width = proj_back[0].shape
    wide = qkv.shape[2] // 3
    own = heads * HEAD_DIM
    group_rows = blocks * frames * TILE
    for block in range(blocks):
        found = mm_t(proj_back[block][...].reshape(frames * rows, width), output_weight[...])
        mixed_back[block * frames : (block + 1) * frames, :, :own] = (
            found.astype(HALF).reshape(frames, rows, own)
        )
        mixed_back[block * frames : (block + 1) * frames, :, own:] = jnp.zeros(
            (frames, rows, wide - own), HALF
        )
    masks = half_masks()

    def one_group(group, carry):
        spot = pl.ds(pl.multiple_of(group * TILE, TILE), TILE)
        piece = qkv[:, spot, :].reshape(group_rows, 3 * wide)
        outer_all = mixed_back[:, spot, :].reshape(group_rows, wide)
        for pair in range(wide // PAIR):
            query = piece[:, pair * PAIR : (pair + 1) * PAIR]
            key = piece[:, wide + pair * PAIR : wide + (pair + 1) * PAIR]
            value = piece[:, 2 * wide + pair * PAIR : 2 * wide + (pair + 1) * PAIR]
            outer = outer_all[:, pair * PAIR : (pair + 1) * PAIR]
            sums = [jnp.zeros((group_rows, PAIR), FLOAT) for _ in range(3)]
            for side in range(2):
                head = 2 * pair + side
                if head >= heads:
                    continue
                soft = weights_in[group, head]
                mine = outer * masks[side]
                sums[2] = sums[2] + mm(soft, mine)
                weight_back = mm_t(value, mine)
                large = soft.astype(FLOAT)
                product = large * weight_back
                score_back = product - large * jnp.sum(product, axis=0, keepdims=True)
                score_back = score_back.astype(HALF)
                sums[1] = sums[1] + mm(score_back, query * masks[side])
                sums[0] = sums[0] + t_mm(score_back, key * masks[side])
            for kind, scale in enumerate((HEAD_DIM**-0.5, 1.0, 1.0)):
                value_out = (sums[kind] * scale).astype(HALF)
                start = kind * wide + pair * PAIR
                qkv_back[:, spot, start : start + PAIR] = value_out.reshape(
                    blocks * frames, TILE, PAIR
                )
        return carry

    lax.fori_loop(0, rows // TILE, one_group, 0)
    sums = jnp.zeros((1, 3 * wide), FLOAT)
    first = jnp.zeros((1, width), FLOAT)
    second = jnp.zeros((1, width), FLOAT)
    for block in range(blocks):
        piece = qkv_back[block * frames : (block + 1) * frames].reshape(frames * rows, 3 * wide)
        sums = sums + jnp.sum(piece.astype(FLOAT), axis=0, keepdims=True)
        found = mm(piece, weight[...])
        outs[block][...] = found.astype(HALF).reshape(frames, rows, width)
        values = normed[block][...].reshape(frames * rows, width).astype(FLOAT)
        first = first + jnp.sum(found * values, axis=0, keepdims=True)
        second = second + jnp.sum(found, axis=0, keepdims=True)
    sums_out[...] = sums
    norm_sums[0:1] = (first - second * shift[0:1, :]) / gain[0:1, :]
    norm_sums[1:2] = second


def time_weights_kernel(heads, blocks, *refs):
    index = refs[0]
    normed = refs[1 : 1 + blocks]
    proj_back = refs[1 + blocks : 1 + 2 * blocks]
    mixed = refs[1 + 2 * blocks : 1 + 3 * blocks]
    qkv_back, out = refs[1 + 3 * blocks :]
    frames, rows, width = normed[0].shape
    cuts, cut = out.shape[:2]
    wide = qkv_back.shape[2] // 3
    own = heads * HEAD_DIM
    tokens = frames * rows
    found = jnp.zeros((width, 3 * wide), FLOAT)
    for block in range(blocks):
        found = found + t_mm(
            normed[block][...].reshape(tokens, width),
            qkv_back[block * frames : (block + 1) * frames].reshape(tokens, 3 * wide),
        )
    other = jnp.zeros((width, own), FLOAT)
    for block in range(blocks):
        other = other + t_mm(
            proj_back[block][...].reshape(tokens, width), mixed[block][...].reshape(tokens, own)
        )
    joined = jnp.concatenate(
        [found[:, kind * wide : kind * wide + own].astype(HALF) for kind in range(3)]
        + [other.astype(HALF)],
        axis=1,
    )
    for part in range(cuts):
        out[jnp.bitwise_xor(part, index[0])] = joined[part * cut : (part + 1) * cut]


def finish_kernel(grads, tokens, back, own, other, gains, class_token, class_grad, *refs):
    class_parts, (patch_out, class_out) = refs[:-2], refs[-2:]
    frames, patches, width = tokens.shape
    for frame in range(frames):
        unit, inverse = normalize(tokens[frame].astype(FLOAT))
        incoming = (
            back[frame, :patches].astype(FLOAT)
            + own[frame, :patches].astype(FLOAT)
            + other[frame, :patches].astype(FLOAT)
        )
        patch_out[frame] = grads[frame, :patches] + normalize_back(
            incoming * gains[0:1, :], unit, inverse
        )
    unit, inverse = normalize(class_token[...].astype(FLOAT))
    incoming = class_parts[0][...]
    for part in class_parts[1:]:
        incoming = incoming + part[...]
    class_out[...] = class_grad[0, patches : patches + 1] + normalize_back(
        incoming * gains[1:2, :], unit, inverse
    )


VMEM = pl.BlockSpec(memory_space=pltpu.VMEM)
SMEM = pl.BlockSpec(memory_space=pltpu.SMEM)


def shape(dims, kind=HALF):
    return jax.ShapeDtypeStruct(tuple(dims), kind)


def call(kernel, outs, args, name, flops, scratch=(), scalars=0, **more):
    moved = sum(a.size * a.dtype.itemsize for a in args) + sum(
        o.size * o.dtype.itemsize for o in outs
    )
    return pl.pallas_call(
        kernel,
        out_shape=list(outs),
        in_specs=[SMEM] * scalars + [VMEM] * (len(args) - scalars),
        out_specs=[VMEM] * len(outs),
        scratch_shapes=list(scratch),
        cost_estimate=pl.CostEstimate(
            flops=int(flops), bytes_accessed=int(moved), transcendentals=0
        ),
        compiler_params=pltpu.CompilerParams(vmem_limit_bytes=56 * 2**20),
        name=name,
        **more,
    )(*args)


def swap(values, axis, mask):
    size = lax.axis_size(axis)
    return lax.ppermute(values, axis, [(i, i ^ mask) for i in range(size)])


def spread_blocks(values):
    near = swap(values, "head", 1)
    far = swap(values, "head", 2)
    return [values, near, far, swap(far, "head", 1)]


def halve(sent, kept, axis, mask):
    return kept.astype(FLOAT) + swap(sent, axis, mask).astype(FLOAT)


def scatter_clips(values):
    clips = values.shape[0]
    mask = 1
    while values.shape[0] > 1:
        pairs = values.reshape((values.shape[0] // 2, 2) + values.shape[1:])
        sent = pairs[:, 1].astype(HALF)
        values = halve(sent, pairs[:, 0], "clip", mask)
        mask *= 2
    assert mask == clips
    return values[0]


def scatter_heads(sent, kept):
    recv = swap(sent, "head", 1)
    near = kept[0].astype(FLOAT) + recv[0].astype(FLOAT)
    far = kept[1].astype(FLOAT) + recv[1].astype(FLOAT)
    return halve(far.astype(HALF), near, "head", 2)


def on_device(
    patch_tokens,
    class_token,
    keep_mask,
    patch_grad,
    class_grad,
    norm_gain,
    norm_bias,
    input_weight,
    input_bias,
    output_weight,
    time_mixer,
    output_bias,
    hidden_weight,
    hidden_bias,
    return_weight,
):
    blocks = lax.axis_size("head")
    clips = lax.axis_size("clip")
    head_index = lax.axis_index("head")
    clip_index = lax.axis_index("clip")
    _, frames, patches, width = patch_tokens.shape
    all_frames = keep_mask.shape[1]
    own_width = input_weight.shape[-1]
    heads = own_width // HEAD_DIM
    all_heads = heads * blocks
    hidden = hidden_weight.shape[-1]
    rows = round_up(patches + 1, TILE)
    groups = rows // TILE
    group_rows = all_frames * TILE
    wide = round_up(own_width, PAIR)
    cut = width // clips
    tokens = frames * rows
    index = jnp.stack([clip_index, head_index]).astype(jnp.int32)
    gains, shifts, biases = norm_gain[0], norm_bias[0], output_bias[0]
    patch_state, patch_back = patch_tokens[0], patch_grad[0]
    mixer = time_mixer[0]
    first_weight, second_weight = hidden_weight[0], return_weight[0]

    (time_normed,) = call(
        time_norm_kernel,
        [shape((frames, rows, width))],
        [patch_state, gains[0:1], shifts[0:1]],
        "time_norm",
        1e6,
    )
    time_blocks = spread_blocks(time_normed)

    turned = jnp.transpose(input_weight[0], (0, 2, 3, 1))
    time_weight = jnp.pad(turned[0], ((0, 0), (0, wide - own_width), (0, 0))).reshape(
        3 * wide, width
    )
    bundle = jnp.concatenate(
        [output_weight[0, 0], turned[1].reshape(3 * own_width, width), output_weight[0, 1]], axis=0
    )
    small = jnp.concatenate([input_bias[0].reshape(-1), hidden_bias[0]])[None]
    smalls = [small] + [swap(small, "head", mask) for mask in range(1, blocks)]
    bundles = spread_blocks(bundle)
    first_weights = spread_blocks(first_weight)
    second_weights = spread_blocks(second_weight)

    keep = keep_mask[0].astype(FLOAT)
    keep = jnp.pad(keep, ((0, 0), (0, rows - patches))).reshape(blocks, frames, groups, TILE)
    local_keep = lax.dynamic_index_in_dim(keep, head_index, 0, False).reshape(frames, rows).T
    order = jnp.bitwise_xor(jnp.arange(blocks), head_index)
    time_keep = jnp.transpose(jnp.take(keep, order, axis=0), (2, 0, 1, 3)).reshape(
        groups, group_rows
    )
    time_keep = jnp.pad(time_keep, ((0, round_up(groups, 8) - groups), (0, 0)))
    biases_wide = jnp.pad(input_bias[0, 0], ((0, 0), (0, wide - own_width)))

    found = call(
        functools.partial(time_forward_kernel, heads, blocks),
        [shape((frames, rows, own_width))] * blocks
        + [
            shape((all_frames, rows, 3 * wide)),
            shape((groups, heads, group_rows, group_rows)),
        ],
        [*time_blocks, time_weight, biases_wide[0:1], biases_wide[1:2], time_keep],
        "time_forward",
        6e9,
    )
    time_mixed, time_qkv, time_soft = found[:blocks], found[blocks], found[blocks + 1]
    mixed_here = [time_mixed[0]] + [
        swap(time_mixed[mask], "head", mask) for mask in range(1, blocks)
    ]

    split = 2 * own_width
    query_bias = jnp.concatenate([s[:, split : split + own_width] for s in smalls], axis=1)
    value_bias = jnp.concatenate(
        [s[:, split + own_width : 2 * split] for s in smalls], axis=1
    )
    full = (frames, rows, width)
    (state, proj, space_normed, query, key, value, space_soft, spread, next_state, class_part) = call(
        functools.partial(space_forward_kernel, blocks, own_width),
        [
            shape(full, FLOAT),
            shape(full),
            shape(full),
            shape(full),
            shape(full),
            shape(full),
            shape((frames, all_heads, rows, rows)),
            shape(full),
            shape(full, FLOAT),
            shape((1, width), FLOAT),
        ],
        [
            patch_state,
            class_token,
            *mixed_here,
            *bundles,
            mixer,
            biases,
            gains,
            shifts,
            query_bias,
            value_bias,
            local_keep,
        ],
        "space_forward",
        10e9,
        scratch=[pltpu.VMEM((width, width), HALF), pltpu.VMEM((frames, rows, rows), FLOAT)],
    )
    class_parts = [class_part] + [swap(class_part, "head", mask) for mask in range(1, blocks)]

    block_width = 256
    steps_per = hidden // block_width
    send_order = (1, 3, 0, 2)
    steps = blocks * steps_per + 2
    half_steps = (blocks // 2) * steps_per

    def fixed(dims):
        return pl.BlockSpec(dims, lambda j: (0,) * len(dims))

    def along(place, dims, axis):
        def where(j):
            spot = jnp.clip(j - place * steps_per, 0, steps_per - 1)
            return tuple(spot if a == axis else 0 for a in range(2))

        return pl.BlockSpec(dims, where)

    place_of = [send_order.index(block) for block in range(blocks)]

    def sent_at(j):
        spot = jnp.clip(j - 2, 0, half_steps - 1)
        return (spot // steps_per, 0, 0, spot % steps_per)

    def kept_at(j):
        spot = jnp.clip(j - 2 - half_steps, 0, half_steps - 1)
        return (spot // steps_per, 0, 0, spot % steps_per)

    def hidden_at(j):
        spot = jnp.clip(j - 2, 0, 2 * half_steps - 1)
        return (spot // steps_per, 0, spot % steps_per)

    hidden_biases = [s[:, 2 * split :] for s in smalls]
    piece = (1, clips, cut, 2 * block_width)
    mlp_args = [
        index,
        next_state,
        class_token,
        *class_parts,
        patch_back,
        class_grad,
        local_keep,
        biases,
        gains,
        shifts,
        *first_weights,
        *second_weights,
        *hidden_biases,
    ]
    (patch_out, class_out, grads, mlp_sums, hidden_sums, mlp_sent, mlp_kept) = pl.pallas_call(
        functools.partial(mlp_kernel, send_order, steps_per),
        grid=(steps,),
        out_shape=[
            shape((frames, patches, width), FLOAT),
            shape((1, width), FLOAT),
            shape(full, FLOAT),
            shape((8, width), FLOAT),
            shape((blocks, 1, hidden), FLOAT),
            shape((blocks // 2, clips, cut, 2 * hidden)),
            shape((blocks // 2, clips, cut, 2 * hidden)),
        ],
        in_specs=[SMEM]
        + [fixed(a.shape) for a in mlp_args[1 : 9 + blocks]]
        + [along(place_of[b], (width, block_width), 1) for b in range(blocks)]
        + [along(place_of[b], (block_width, width), 0) for b in range(blocks)]
        + [along(place_of[b], (1, block_width), 1) for b in range(blocks)],
        out_specs=[
            fixed((frames, patches, width)),
            fixed((1, width)),
            fixed(full),
            fixed((8, width)),
            pl.BlockSpec((1, 1, block_width), hidden_at),
            pl.BlockSpec(piece, sent_at),
            pl.BlockSpec(piece, kept_at),
        ],
        scratch_shapes=[
            pltpu.VMEM(full, FLOAT),
            pltpu.VMEM((tokens, width), HALF),
            pltpu.VMEM((tokens, width), HALF),
            pltpu.VMEM((clips, cut, tokens), HALF),
            pltpu.VMEM((clips, cut, tokens), HALF),
            pltpu.VMEM((3, width, block_width), HALF),
            pltpu.VMEM((3, block_width, width), HALF),
            pltpu.VMEM((1, block_width), FLOAT),
            pltpu.VMEM((2, tokens, block_width), FLOAT),
            pltpu.VMEM((2, tokens, block_width), FLOAT),
            pltpu.VMEM((2, tokens, block_width), HALF),
            pltpu.VMEM((2, tokens, block_width), HALF),
            pltpu.VMEM((tokens, width), FLOAT),
            pltpu.VMEM((tokens, width), FLOAT),
        ],
        cost_estimate=pl.CostEstimate(
            flops=int(12e9), bytes_accessed=int(40e6), transcendentals=0
        ),
        compiler_params=pltpu.CompilerParams(vmem_limit_bytes=56 * 2**20),
        name="feed_forward",
    )(*mlp_args)

    (grads_next, proj_back, spread_grad, query_back, key_back, value_back, time_grad, class_back,
     space_sums) = call(
        functools.partial(space_backward_kernel, blocks, own_width, patches),
        [
            shape(full, FLOAT),
            shape(full),
            shape(full),
            shape(full),
            shape(full),
            shape(full),
            shape(full),
            shape((1, width), FLOAT),
            shape((8, width), FLOAT),
        ],
        [index, grads, state, query, key, value, space_soft, mixer, gains, *bundles],
        "space_backward",
        12e9,
        scratch=[pltpu.VMEM((width, width), HALF), pltpu.VMEM(full, HALF)],
        scalars=1,
    )
    proj_blocks = spread_blocks(proj_back)
    class_backs = [class_back] + [swap(class_back, "head", mask) for mask in range(1, blocks)]
    half_shape = (blocks // 2, clips, cut, 4 * own_width)
    space_sent, space_kept, mixer_grad = call(
        functools.partial(space_weights_kernel, send_order, own_width),
        [shape(half_shape), shape(half_shape), shape((clips, cut, width))],
        [
            index,
            space_normed,
            query_back,
            key_back,
            value_back,
            spread_grad,
            spread,
            proj,
            time_grad,
        ],
        "space_weights",
        5e9,
        scalars=1,
    )

    found = call(
        functools.partial(time_backward_kernel, heads, blocks),
        [shape(full)] * blocks
        + [
            shape((all_frames, rows, 3 * wide)),
            shape((1, 3 * wide), FLOAT),
            shape((2, width), FLOAT),
        ],
        [
            *proj_blocks,
            *time_blocks,
            time_qkv,
            time_soft,
            output_weight[0, 0],
            time_weight,
            gains[0:1],
            shifts[0:1],
        ],
        "time_backward",
        6e9,
        scratch=[pltpu.VMEM((all_frames, rows, wide), HALF)],
    )
    normed_back = found[:blocks]
    time_qkv_back, time_bias_sums, time_norm_sums = found[blocks:]
    (time_weights,) = call(
        functools.partial(time_weights_kernel, heads, blocks),
        [shape((clips, cut, 4 * own_width))],
        [index, *time_blocks, *proj_blocks, *time_mixed, time_qkv_back],
        "time_weights",
        4e9,
        scalars=1,
    )
    near = swap(normed_back[1], "head", 1)
    across = normed_back[2].astype(FLOAT) + swap(normed_back[3], "head", 1).astype(FLOAT)
    far = swap(across.astype(HALF), "head", 2)
    patch_input_grad, class_input_grad = call(
        finish_kernel,
        [shape((frames, patches, width), FLOAT), shape((1, width), FLOAT)],
        [
            grads_next,
            patch_state,
            normed_back[0],
            near,
            far,
            gains,
            class_token,
            grads,
            *class_backs,
        ],
        "finish",
        1e6,
    )

    mlp_total = scatter_clips(scatter_heads(mlp_sent, mlp_kept))
    space_total = scatter_clips(scatter_heads(space_sent, space_kept))
    time_total = scatter_clips(time_weights)
    mixer_total = scatter_clips(mixer_grad)
    for mask in (1, 2):
        mixer_total = mixer_total + swap(mixer_total, "head", mask)
    share = cut // blocks
    mixer_total = lax.dynamic_slice_in_dim(mixer_total, head_index * share, share, 0)

    hidden_sums = jnp.stack([hidden_sums[send_order.index(b)] for b in range(blocks)])
    hidden_sums = jnp.take(hidden_sums[:, 0], order, axis=0)
    space_bias = jnp.take(space_sums[5:7].reshape(2, blocks, own_width), order, axis=1).reshape(
        2, width
    )
    time_bias = jnp.stack([time_bias_sums[0, :own_width], time_bias_sums[0, 2 * wide : 2 * wide + own_width]])
    time_bias = lax.dynamic_update_slice_in_dim(
        jnp.zeros((2, width), FLOAT), time_bias, head_index * own_width, 1
    )
    sums = jnp.concatenate(
        [
            time_norm_sums[0:1],
            space_sums[0:1],
            mlp_sums[0:1],
            time_norm_sums[1:2],
            space_sums[1:2],
            mlp_sums[1:2],
            space_sums[4:5],
            space_sums[3:4],
            space_sums[2:3],
            mlp_sums[2:3],
            time_bias,
            space_bias,
            hidden_sums.reshape(-1, width),
        ],
        axis=0,
    )
    for mask in (1, 2):
        sums = sums + swap(sums, "head", mask)
    mask = 1
    while mask < clips:
        sums = sums + swap(sums, "clip", mask)
        mask *= 2
    part = width // (clips * blocks)
    both = clip_index * blocks + head_index
    shared = lax.dynamic_slice_in_dim(sums[:10], both * part, part, 1)
    other = head_index * clips + clip_index
    input_bias_grad = lax.dynamic_slice_in_dim(
        sums[10:14].reshape(2, 2, width), other * part, part, 2
    )
    hidden_part = blocks * hidden // (clips * blocks)
    hidden_bias_grad = lax.dynamic_slice_in_dim(
        sums[14:].reshape(-1), other * hidden_part, hidden_part, 0
    )

    own = own_width
    joined = jnp.stack([time_total, space_total])
    input_weight_grad = joined[:, :, : 3 * own].reshape(2, cut, 3, own)
    output_weight_grad = jnp.transpose(joined[:, :, 3 * own :], (0, 2, 1))
    mlp_total = mlp_total.reshape(cut, steps_per, 2, block_width)
    hidden_weight_grad = mlp_total[:, :, 0].reshape(cut, hidden)
    return_weight_grad = mlp_total[:, :, 1].reshape(cut, hidden).T
    quarter = width // blocks
    return (
        patch_out[None],
        lax.dynamic_slice_in_dim(class_out, head_index * quarter, quarter, 1),
        patch_input_grad[None],
        lax.dynamic_slice_in_dim(class_input_grad, head_index * quarter, quarter, 1),
        shared[None, 0:3],
        shared[None, 3:6],
        input_weight_grad[None],
        input_bias_grad[None],
        output_weight_grad[None],
        mixer_total[None],
        shared[None, 6:10],
        hidden_weight_grad[None],
        hidden_bias_grad[None],
        return_weight_grad[None],
    )


def solution(mesh):
    in_specs = (
        P("clip", "head", None, None),
        P("clip", None),
        P("clip", None, None),
        P("clip", "head", None, None),
        P("clip", None),
        P(),
        P(),
        P(None, None, None, None, "head"),
        P(None, None, None, "head"),
        P(None, None, "head", None),
        P(),
        P(),
        P(None, None, "head"),
        P(None, "head"),
        P(None, "head", None),
    )
    out_specs = (
        P("clip", "head", None, None),
        P("clip", "head"),
        P("clip", "head", None, None),
        P("clip", "head"),
        P(None, None, ("clip", "head")),
        P(None, None, ("clip", "head")),
        P(None, None, "clip", None, "head"),
        P(None, None, None, ("head", "clip")),
        P(None, None, "head", "clip"),
        P(None, ("clip", "head"), None),
        P(None, None, ("clip", "head")),
        P(None, "clip", "head"),
        P(None, ("head", "clip")),
        P(None, "head", "clip"),
    )
    return jax.shard_map(
        on_device, mesh=mesh, in_specs=in_specs, out_specs=out_specs, check_vma=False
    )
```

```python
import functools

import jax
import jax.numpy as jnp
from jax import lax
from jax.experimental import pallas as pl
from jax.experimental.pallas import tpu as pltpu
from jax.sharding import PartitionSpec as P

HEAD_DIM = 64
PAIR = 2 * HEAD_DIM
TILE = 16
EPSILON = 1e-06
MASKED = -1e30
FLOAT = jnp.float32
HALF = jnp.bfloat16
ROW_ROW = (((1,), (1,)), ((), ()))
COL_COL = (((0,), (0,)), ((), ()))
ROOT_HALF = 0.7071067811865476
ROOT_TWO_PI = 0.3989422804014327


def round_up(value, unit):
    return -(-value // unit) * unit


def mm(left, right):
    return jnp.dot(left, right, preferred_element_type=FLOAT)


def mm_t(left, right):
    return lax.dot_general(left, right, ROW_ROW, preferred_element_type=FLOAT)


def t_mm(left, right):
    return lax.dot_general(left, right, COL_COL, preferred_element_type=FLOAT)


def normalize(values):
    average = jnp.mean(values, axis=-1, keepdims=True)
    centred = values - average
    spread = jnp.mean(centred * centred, axis=-1, keepdims=True)
    inverse = lax.rsqrt(spread + EPSILON)
    return centred * inverse, inverse


def normalize_back(scaled, unit, inverse):
    first = jnp.mean(scaled, axis=-1, keepdims=True)
    second = jnp.mean(scaled * unit, axis=-1, keepdims=True)
    return (scaled - first - unit * second) * inverse


def rows_iota(shape):
    return lax.broadcasted_iota(jnp.int32, shape, 0)


def lanes_iota(shape):
    return lax.broadcasted_iota(jnp.int32, shape, 1)


def half_masks():
    lanes = lanes_iota((1, PAIR))
    first = (lanes < HEAD_DIM).astype(HALF)
    return first, (1 - first).astype(HALF)


def softmax_columns(scores):
    top = jnp.max(scores, axis=0, keepdims=True)
    exponent = jnp.exp(scores - top)
    total = jnp.sum(exponent, axis=0, keepdims=True)
    return exponent * (1.0 / total)


def gelu_parts(values):
    size = jnp.abs(values)
    density = jnp.exp(-0.5 * values * values)
    step = 1.0 / (1.0 + (0.3275911 * ROOT_HALF) * size)
    tail = step * (
        0.5 * 0.254829592
        + step
        * (
            0.5 * -0.284496736
            + step * (0.5 * 1.421413741 + step * (0.5 * -1.453152027 + step * (0.5 * 1.061405429)))
        )
    )
    tail = tail * density
    return jnp.where(values < 0.0, tail, 1.0 - tail), density * ROOT_TWO_PI


def flip(value, mask):
    return value + mask - 2 * mask * lax.rem(lax.div(value, mask), 2)


def flip_all(value, number, size):
    total, bit = 0, 1
    while bit < size:
        mine = lax.rem(lax.div(value, bit), 2)
        total = total + bit * ((1 - mine) if number & bit else mine)
        bit *= 2
    return total


def spread_index(clip, part, cuts, rest, cut):
    bits = []
    bit = 1
    while bit < 4 * rest:
        mine = lax.rem(lax.div(clip, bit), 2)
        bits.append(1 - mine if part & bit else mine)
        bit *= 2
    inner = 0
    for value in bits[2:]:
        inner = 2 * inner + value
    outer = part // (4 * rest)
    return bits[0], bits[1], inner, pl.ds(outer * cut, cut)


class Wires:
    def __init__(self, send, recv, local):
        self.send, self.recv, self.local = send, recv, local
        self.sent, self.moved, self.done = [], [], []

    def to(self, peer, source, dest):
        slot = len(self.sent)
        copy = pltpu.make_async_remote_copy(
            src_ref=source,
            dst_ref=dest,
            send_sem=self.send.at[slot],
            recv_sem=self.recv.at[slot],
            device_id=peer,
            device_id_type=pl.DeviceIdType.MESH,
        )
        copy.start()
        self.sent.append(copy)
        return copy

    def move(self, source, dest):
        copy = pltpu.make_async_copy(source, dest, self.local.at[len(self.moved)])
        copy.start()
        self.moved.append(copy)
        return copy


def greet(peers):
    barrier = pltpu.get_barrier_semaphore()
    for peer in peers:
        pl.semaphore_signal(
            barrier, inc=1, device_id=peer, device_id_type=pl.DeviceIdType.MESH
        )
    pl.semaphore_wait(barrier, len(peers))


class Gather:
    def __init__(self, wires, peers, clip, head, source, dest):
        self.wires, self.peers, self.source, self.dest = wires, peers, source, dest
        self.head = head
        self.rows = source.shape[0]
        self.piece = self.rows // 4
        self.half = round_up(self.piece // 2, TILE)
        self.mine = lax.rem(clip, 4)
        self.far = flip(head, 2)
        self.own = wires.move(source, dest.at[head])

    def spot(self, piece, first=0, count=None):
        start = pl.multiple_of(piece * self.piece + first, TILE)
        return pl.ds(start, self.piece if count is None else count)

    def start_far(self):
        here = self.spot(self.mine)
        self.cross = self.wires.to(
            self.peers["far"], self.source.at[here], self.dest.at[self.head, here]
        )

    def start_near(self):
        self.near = self.wires.to(self.peers["near"], self.source, self.dest.at[self.head])

    def share(self):
        self.cross.wait_recv()
        here = self.dest.at[self.far, self.spot(self.mine)]
        self.first = self.wires.to(self.peers["one"], here, here)
        self.second = self.wires.to(self.peers["two"], here, here)

    def share_again(self):
        self.second.wait_recv()
        here = self.dest.at[self.far, self.spot(flip(self.mine, 2), 0, self.half)]
        third = self.wires.to(self.peers["one"], here, here)
        self.first.wait_recv()
        here = self.dest.at[
            self.far, self.spot(flip(self.mine, 1), self.half, self.piece - self.half)
        ]
        self.rest = [third, self.wires.to(self.peers["two"], here, here)]

    def pass_on(self):
        for copy in self.rest:
            copy.wait_recv()
        here = self.dest.at[self.far]
        self.last = self.wires.to(self.peers["near"], here, here)


def time_groups(heads, groups, qkv, keep_t, weights_out, out, masks, same, equal):
    frames = qkv.shape[0]
    wide = qkv.shape[2] // 3
    total_rows = frames * TILE
    work = []
    for group in groups:
        spot = pl.ds(pl.multiple_of(group * TILE, TILE), TILE)
        piece = qkv[:, spot, :].reshape(total_rows, 3 * wide)
        kept = keep_t[spot, :]
        kept = jnp.concatenate(
            [jnp.broadcast_to(kept[:, f : f + 1], (TILE, total_rows)) for f in range(frames)],
            axis=0,
        )
        blocked = jnp.where(same & ((kept > 0.5) | equal), 0.0, MASKED)
        scores = []
        for head in range(heads):
            left = (head // 2) * PAIR
            query = piece[:, left : left + PAIR]
            key = piece[:, wide + left : wide + left + PAIR]
            scores.append(mm_t(key * masks[head % 2], query) + blocked)
        work.append((group, spot, piece, scores))
    softs = []
    for group, spot, piece, scores in work:
        found = [softmax_columns(s).astype(HALF) for s in scores]
        for head in range(heads):
            weights_out[group, head] = found[head]
        softs.append(found)
    for (group, spot, piece, _), found in zip(work, softs):
        results = []
        for pair in range(wide // PAIR):
            left = 2 * wide + pair * PAIR
            value = piece[:, left : left + PAIR]
            total = t_mm(found[2 * pair], value * masks[0])
            if 2 * pair + 1 < heads:
                total = total + t_mm(found[2 * pair + 1], value * masks[1])
            results.append(total.astype(HALF))
        joined = jnp.concatenate(results, axis=1)[:, : heads * HEAD_DIM]
        out[:, spot, :] = joined.reshape(frames, TILE, heads * HEAD_DIM)


def forward_kernel(
    heads,
    cuts,
    tokens,
    class_token,
    class_grad,
    keep_t,
    small,
    gains,
    shifts,
    biases,
    grads_in,
    time_weight_in,
    mixer_in,
    bundle_in,
    first_in,
    second_in,
    normed_o,
    qkv_o,
    time_soft_o,
    mixed_o,
    state_o,
    proj_o,
    space_normed_o,
    space_qkv_o,
    space_soft_o,
    spread_o,
    bundles_o,
    grad_o,
    kept_o,
    recv_o,
    patch_out,
    class_out,
    sums_out,
    hidden_sums,
    normed,
    qkv,
    time_soft,
    mixed,
    mixed_here,
    state,
    proj,
    space_normed,
    space_qkv,
    space_soft,
    spread,
    joint,
    blocked,
    bundles,
    first,
    second,
    smalls,
    time_weight,
    mixer,
    grads,
    class_parts,
    full,
    grad,
    mlp_normed,
    grads_half,
    normed_t,
    grads_t,
    total,
    normed_back,
    found,
    send_sems,
    recv_sems,
    local_sems,
):
    clip, head = lax.axis_index("clip"), lax.axis_index("head")
    frames, patches, width = tokens.shape
    all_frames, rows, _ = normed.shape
    blocks = all_frames // frames
    own_width = mixed.shape[2]
    wide = qkv.shape[2] // 3
    flat = (frames * rows, width)
    shaped = (frames, rows, width)
    rest, block_rows = normed_t.shape[2:4]
    cut = width // cuts
    hidden = first.shape[2]
    peers = {
        "near": (clip, flip(head, 1)),
        "far": (clip, flip(head, 2)),
        "cross": (clip, flip(flip(head, 1), 2)),
        "one": (flip(clip, 1), head),
        "two": (flip(clip, 2), head),
    }
    others = [peers["near"], peers["far"], peers["cross"]]
    wires = Wires(send_sems, recv_sems, local_sems)
    weight_copy = wires.move(time_weight_in, time_weight)
    mixer_copy = wires.move(mixer_in, mixer)
    grads_copy = wires.move(grads_in, grads)
    smalls[head] = small[...]
    greet(list(peers.values()))

    bundle = Gather(wires, peers, clip, head, bundle_in, bundles)
    gather_first = Gather(wires, peers, clip, head, first_in, first)
    gather_second = Gather(wires, peers, clip, head, second_in, second)
    bundle.start_far()
    small_copies = [wires.to(peer, small, smalls.at[head]) for peer in others]

    mine = pl.multiple_of(head * frames, frames)
    for frame in range(frames):
        unit, _ = normalize(tokens[frame].astype(FLOAT))
        normed[mine + frame, :patches] = (unit * gains[0:1, :] + shifts[0:1, :]).astype(HALF)
        normed[mine + frame, patches:] = jnp.zeros((rows - patches, width), HALF)
    own_part = normed.at[pl.ds(mine, frames)]
    far_copies = [
        wires.to(peers["far"], normed.at[mine + frame], normed.at[mine + frame])
        for frame in range(frames)
    ]
    near_copy = wires.to(peers["near"], own_part, own_part)
    bundle.start_near()
    gather_first.start_far()
    gather_second.start_far()

    for copy in small_copies:
        copy.wait_recv()
    bias_row = smalls[head]
    bias_gap = jnp.zeros((1, wide - own_width), FLOAT)
    query_bias = jnp.concatenate([bias_row[:, :own_width], bias_gap], axis=1)
    value_bias = jnp.concatenate([bias_row[:, own_width : 2 * own_width], bias_gap], axis=1)
    weight_copy.wait()

    def project(block):
        start = pl.multiple_of(block * frames, frames)
        raw = mm_t(normed[pl.ds(start, frames)].reshape(flat), time_weight[...])
        query = (raw[:, :wide] + query_bias).astype(HALF) * (HEAD_DIM**-0.5)
        value = (raw[:, 2 * wide :] + value_bias).astype(HALF)
        joined = jnp.concatenate(
            [query.astype(HALF), raw[:, wide : 2 * wide].astype(HALF), value], axis=1
        )
        qkv[pl.ds(start, frames)] = joined.reshape(frames, rows, 3 * wide)

    project(head)
    near_copy.wait_recv()
    project(flip(head, 1))
    bundle.share()
    gather_first.start_near()
    gather_second.start_near()
    far_start = pl.multiple_of(flip(head, 2) * frames, frames)
    passed = []
    for frame in range(frames):
        far_copies[frame].wait_recv()
        here = normed.at[far_start + frame]
        passed.append(wires.to(peers["near"], here, here))
    project(flip(head, 2))
    bundle.share_again()
    for copy in passed:
        copy.wait_recv()
    project(flip(flip(head, 1), 2))
    saved = [wires.move(normed, normed_o), wires.move(qkv, qkv_o)]

    masks = half_masks()
    square = (all_frames * TILE,) * 2
    key_index, query_index = rows_iota(square), lanes_iota(square)
    same = lax.rem(key_index, TILE) == lax.rem(query_index, TILE)
    equal = key_index == query_index
    groups = rows // TILE
    batch = 3
    middle = (groups // batch) // 2

    def attend(start, stop):
        def body(step, carry):
            time_groups(
                heads,
                [step * batch + i for i in range(batch)],
                qkv,
                keep_t,
                time_soft,
                mixed,
                masks,
                same,
                equal,
            )
            return carry

        lax.fori_loop(start, stop, body, 0)

    def exchange(first_row, count):
        spot = pl.ds(first_row, count)
        copies = []
        for peer in others:
            theirs = pl.ds(pl.multiple_of(peer[1] * frames, frames), frames)
            copies.append(
                wires.to(peer, mixed.at[theirs, spot], mixed_here.at[head, :, spot])
            )
        return copies

    cut_row = middle * batch * TILE
    attend(0, middle)
    exchanged = exchange(0, cut_row)
    attend(middle, groups // batch)
    for group in range(groups // batch * batch, groups):
        time_groups(heads, [group], qkv, keep_t, time_soft, mixed, masks, same, equal)
    exchanged = exchanged + exchange(cut_row, rows - cut_row)
    mixed_here[head] = mixed[pl.ds(mine, frames)]
    saved = saved + [wires.move(time_soft, time_soft_o), wires.move(mixed, mixed_o)]
    bundle.pass_on()
    gather_first.share()
    gather_second.share()
    keep_all = keep_t[...]
    key_index, query_index = rows_iota((rows, rows)), lanes_iota((rows, rows))
    for frame in range(frames):
        chosen = lanes_iota(keep_all.shape) == mine + frame
        kept = jnp.sum(jnp.where(chosen, keep_all, 0.0), axis=1, keepdims=True)
        allowed = (kept > 0.5) | (key_index == patches) | (key_index == query_index)
        blocked[frame] = jnp.where(allowed, 0.0, MASKED)
    for copy in (bundle.own, bundle.near, bundle.last):
        copy.wait() if copy is bundle.own else copy.wait_recv()
    saved.append(wires.move(bundles, bundles_o))
    for place in range(blocks):
        joint[place * own_width : (place + 1) * own_width] = bundles[place, :own_width]
    mixer_copy.wait()
    for copy in exchanged:
        copy.wait_recv()
    sum_here = jnp.zeros(flat, FLOAT)
    for place in range(blocks):
        sum_here = sum_here + mm(
            mixed_here[place].reshape(frames * rows, own_width), bundles[place, :own_width]
        )
    half = (sum_here + biases[0:1, :]).astype(HALF)
    proj[...] = half.reshape(shaped)
    added = (mm(half, mixer[...]) + biases[1:2, :]).reshape(shaped)
    for frame in range(frames):
        state[frame, :patches] = tokens[frame].astype(FLOAT) + added[frame, :patches]
        state[frame, patches : patches + 1] = class_token[...].astype(FLOAT)
        state[frame, patches + 1 :] = jnp.zeros((rows - patches - 1, width), FLOAT)
    saved = saved + [wires.move(proj, proj_o), wires.move(state, state_o)]

    unit, _ = normalize(state[...].reshape(flat))
    row = rows_iota((frames * rows, 1))
    real = lax.rem(row, rows) <= patches
    half = jnp.where(real, unit * gains[1:2, :] + shifts[1:2, :], 0.0).astype(HALF)
    space_normed[...] = half.reshape(shaped)
    start_bias = 2 * own_width
    for kind in range(3):
        for place in range(blocks):
            joint[place * own_width : (place + 1) * own_width] = bundles[
                place, (1 + kind) * own_width : (2 + kind) * own_width
            ]
        raw = mm_t(space_normed[...].reshape(flat), joint[...])
        if kind != 1:
            begin = start_bias + (kind // 2) * own_width
            bias = jnp.concatenate(
                [smalls[place][:, begin : begin + own_width] for place in range(blocks)], axis=1
            )
            raw = raw + bias
        raw = raw.astype(HALF)
        if kind == 0:
            raw = (raw * (HEAD_DIM**-0.5)).astype(HALF)
        space_qkv[kind] = raw.reshape(shaped)
    saved = saved + [wires.move(space_normed, space_normed_o), wires.move(space_qkv, space_qkv_o)]
    gather_first.share_again()
    gather_second.share_again()

    def one_frame(frame, carry):
        softs = []
        for pair in range(width // PAIR):
            spot = slice(pair * PAIR, (pair + 1) * PAIR)
            query, key = space_qkv[0, frame, :, spot], space_qkv[1, frame, :, spot]
            for side in range(2):
                scores = mm_t(key * masks[side], query) + blocked[frame]
                softs.append(softmax_columns(scores).astype(HALF))
                space_soft[frame, 2 * pair + side] = softs[-1]
        for pair in range(width // PAIR):
            spot = slice(pair * PAIR, (pair + 1) * PAIR)
            value = space_qkv[2, frame, :, spot]
            result = t_mm(softs[2 * pair], value * masks[0]) + t_mm(
                softs[2 * pair + 1], value * masks[1]
            )
            spread[frame, :, spot] = result.astype(HALF)
        return carry

    lax.fori_loop(0, frames, one_frame, 0)
    saved = saved + [wires.move(space_soft, space_soft_o), wires.move(spread, spread_o)]
    for place in range(blocks):
        joint[place * own_width : (place + 1) * own_width] = bundles[place, 4 * own_width :]
    added = mm(spread[...].reshape(flat), joint[...]).reshape(shaped)
    part = added[0, patches : patches + 1]
    for frame in range(1, frames):
        part = part + added[frame, patches : patches + 1]
    class_parts[head] = part * (1.0 / all_frames)
    class_copies = [
        wires.to(peer, class_parts.at[head], class_parts.at[head]) for peer in others
    ]
    full[...] = state[...] + added + biases[2:3, :]
    gather_first.pass_on()
    gather_second.pass_on()

    lead = (head == 0).astype(FLOAT)
    is_class = row == patches
    is_real = (lax.rem(row, rows) < patches) | is_class
    grads_copy.wait()
    for frame in range(frames):
        chosen = lanes_iota(keep_all.shape) == mine + frame
        kept = jnp.sum(jnp.where(chosen, keep_all, 0.0), axis=1, keepdims=True)
        grad[frame, :patches] = grads[frame].astype(FLOAT) * kept[:patches]
        grad[frame, patches:] = jnp.zeros((rows - patches, width), FLOAT)
    grad[0, patches : patches + 1] = class_grad[...].astype(FLOAT)
    values = grad[...].reshape(flat)
    grads_half[...] = values.astype(HALF)
    turned = jnp.where(is_class, values * lead, values)
    sums_out[2:3] = jnp.sum(turned, axis=0, keepdims=True)
    turned = turned.astype(HALF).T
    for part in range(cuts):
        grads_t[spread_index(clip, part, cuts, rest, cut)] = turned[part * cut : (part + 1) * cut]
    for copy in class_copies:
        copy.wait_recv()
    class_state = class_token[...].astype(FLOAT) + biases[2:3, :]
    for place in range(blocks):
        class_state = class_state + class_parts[place]
    full[0, patches : patches + 1] = class_state
    unit, _ = normalize(full[...].reshape(flat))
    values = jnp.where(is_real, unit * gains[2:3, :] + shifts[2:3, :], 0.0)
    mlp_normed[...] = values.astype(HALF)
    turned = jnp.where(is_class, values * lead, values).astype(HALF).T
    for part in range(cuts):
        normed_t[spread_index(clip, part, cuts, rest, cut)] = turned[part * cut : (part + 1) * cut]
    class_row = jnp.where(is_class, lead, 1.0)
    for copy in (gather_first.own, gather_second.own):
        copy.wait()
    sends = []
    for block in range(blocks):
        place = flip_all(head, block, blocks)
        if block == 1:
            gather_first.near.wait_recv()
            gather_second.near.wait_recv()
        if block == 3:
            gather_first.last.wait_recv()
            gather_second.last.wait_recv()
        inner = mm(mlp_normed[...], first[place]) + smalls[place][:, 4 * own_width :]
        outer = mm_t(grads_half[...], second[place])
        chance, density = gelu_parts(inner)
        active = (inner * chance).astype(HALF)
        back = (outer * (chance + inner * density)).astype(HALF)
        hidden_sums[pl.ds(place, 1)] = jnp.sum(
            back.astype(FLOAT) * class_row, axis=0, keepdims=True
        )
        forward = mm(active, second[place])
        backward = mm_t(back, first[place])
        if block == 0:
            total[...] = forward
            normed_back[...] = backward
        else:
            total[...] += forward
            normed_back[...] += backward
        if block >= 2:
            sends[block - 2].wait() if block == 2 else sends[block - 2].wait_send()
        turned = mm(normed_t[...].reshape(width, frames * rows), back).astype(HALF)
        found[block % 2, :, :, :, :, :hidden] = turned.reshape(2, 2, rest, block_rows, hidden)
        turned = mm(grads_t[...].reshape(width, frames * rows), active).astype(HALF)
        found[block % 2, :, :, :, :, hidden:] = turned.reshape(2, 2, rest, block_rows, hidden)
        if block % 2 == 0:
            sends.append(wires.move(found.at[0], kept_o.at[block // 2]))
        else:
            sends.append(wires.to(peers["near"], found.at[1], recv_o.at[block // 2]))
    result = (full[...].reshape(flat) + total[...] + biases[3:4, :]).reshape(shaped)
    for frame in range(frames):
        chosen = lanes_iota(keep_all.shape) == mine + frame
        kept = jnp.sum(jnp.where(chosen, keep_all, 0.0), axis=1, keepdims=True)
        patch_out[frame] = result[frame, :patches] * kept[:patches]
    class_out[...] = result[0, patches : patches + 1]
    unit, inverse = normalize(full[...].reshape(flat))
    incoming = normed_back[...]
    weighted = jnp.where(is_class, incoming * lead, incoming)
    sums_out[0:1] = jnp.sum(weighted * unit, axis=0, keepdims=True)
    sums_out[1:2] = jnp.sum(weighted, axis=0, keepdims=True)
    sums_out[3:] = jnp.zeros((sums_out.shape[0] - 3, width), FLOAT)
    change = normalize_back(incoming * gains[2:3, :], unit, inverse)
    change = jnp.where(is_real, change, 0.0)
    grad[...] += change.reshape(shaped)
    saved.append(wires.move(grad, grad_o))
    for copy in sends[1], sends[3]:
        copy.wait_recv()
    for copy in wires.sent:
        if copy is not sends[1]:
            copy.wait_send()
    for copy in saved + [sends[2]]:
        copy.wait()


class Reduce:
    def __init__(self, wires, data, landings, hops, start=(2, 2, 2)):
        self.wires, self.data, self.landings, self.hops = wires, data, landings, hops
        self.extent = list(start) + [data.shape[3]]
        self.at = 0
        self.done = wires.done

    def launch(self):
        axis, peer = self.hops[self.at]
        places = [pl.ds(0, size) for size in self.extent]
        if axis is not None:
            half = self.extent[axis] // 2
            places[axis] = pl.ds(half, half)
            self.extent[axis] = half
        landing = self.landings[self.at]
        self.copy = self.wires.to(peer, self.data.at[tuple(places)], landing)

    def step(self, out=None):
        self.copy.wait_recv()
        if self.hops[self.at][0] is None:
            self.copy.wait_send()
            self.done.append(self.copy)
        landing = self.landings[self.at]
        self.at += 1
        if out is not None:
            out(self.data[0, 0, 0, 0].astype(FLOAT) + landing[0, 0, 0, 0].astype(FLOAT))
            return
        first, second, third, rest = self.extent
        for place in [(a, b, c) for a in range(first) for b in range(second) for c in range(third)]:

            def add(index, carry):
                spot = place + (index,)
                self.data[spot] = (
                    self.data[spot].astype(FLOAT) + landing[spot].astype(FLOAT)
                ).astype(HALF)
                return carry

            lax.fori_loop(0, rest, add, 0)
        self.launch()


def backward_kernel(
    heads,
    cuts,
    tokens,
    class_token,
    gains,
    shifts,
    mlp_sums,
    hidden_sums,
    grad_in,
    bundles_in,
    time_weight_in,
    mixer_in,
    normed_in,
    qkv_in,
    time_soft_in,
    mixed_in,
    state_in,
    proj_in,
    space_normed_in,
    space_qkv_in,
    space_soft_in,
    spread_in,
    kept_in,
    recv_in,
    patch_out,
    class_out,
    time_out,
    space_out,
    mixer_out,
    hidden_out,
    return_out,
    sums_out,
    space_landing,
    grad,
    bundles,
    time_output,
    weight,
    normed,
    qkv,
    time_soft,
    mixed,
    state,
    proj,
    space_normed,
    space_qkv,
    space_soft,
    spread,
    joint,
    outer_grad,
    mixed_back,
    proj_back,
    time_back,
    near_landing,
    far_landing,
    class_parts,
    mlp,
    loaded,
    space,
    time_data,
    mixer_data,
    mixer_sums,
    mixer_landing,
    vectors,
    vector_landing,
    *rest,
):
    send_sems, recv_sems, local_sems, load_sems = rest[-4:]
    landings = list(rest[:-4])
    clip, head = lax.axis_index("clip"), lax.axis_index("head")
    frames, patches, width = tokens.shape
    all_frames, rows, _ = normed.shape
    blocks = all_frames // frames
    own_width = mixed.shape[2]
    wide = qkv.shape[2] // 3
    flat = (frames * rows, width)
    shaped = (frames, rows, width)
    cut = width // cuts
    rest_size = mlp.shape[3]
    hidden = mlp.shape[5] // 2
    near, far = flip(head, 1), flip(head, 2)
    cross = flip(near, 2)
    near_peer, far_peer, cross_peer = (clip, near), (clip, far), (clip, cross)
    others = [near_peer, far_peer, cross_peer]
    clip_peers = []
    bit = 1
    while bit < cuts:
        clip_peers.append((flip(clip, bit), head))
        bit *= 2
    wires = Wires(send_sems, recv_sems, local_sems)
    order = [
        (grad_in, grad),
        (bundles_in.at[:, pl.ds(own_width, 4 * own_width)], bundles),
        (space_soft_in, space_soft),
        (space_qkv_in, space_qkv),
        (kept_in, mlp),
        (state_in, state),
        (mixer_in, weight),
        (space_normed_in, space_normed),
        (spread_in, spread),
        (proj_in, proj),
        (qkv_in, qkv),
        (time_soft_in, time_soft),
        (bundles_in.at[head, pl.ds(0, own_width)], time_output),
        (normed_in, normed),
        (mixed_in, mixed),
    ]
    ready = {id(dest): wires.move(source, dest) for source, dest in order}

    def need(*refs):
        for ref in refs:
            ready[id(ref)].wait()

    greet(others + clip_peers)
    clip_hops = [
        (3 if 1 << number < rest_size else None, peer)
        for number, peer in enumerate(clip_peers[2:])
    ]
    cross_hop, first_hop, second_hop = (0, far_peer), (1, clip_peers[0]), (2, clip_peers[1])
    per = 3 + len(clip_hops)
    lanes = [pl.ds(0, hidden), pl.ds(hidden, hidden)]
    halves = [mlp.at[:, :, :, :, :, lane] for lane in lanes]
    chain_one = Reduce(wires, halves[0], landings[0:per], [first_hop, cross_hop, second_hop] + clip_hops)
    chain_two = Reduce(wires, halves[1], landings[per : 2 * per], [second_hop, first_hop, cross_hop] + clip_hops)
    chain_space = Reduce(wires, space.at[0], landings[2 * per : 3 * per], [first_hop, cross_hop, second_hop] + clip_hops)
    chain_time = Reduce(wires, time_data, landings[3 * per : 4 * per - 1], [first_hop, second_hop] + clip_hops, (1, 2, 2))
    chain_mixer = Reduce(wires, mixer_data, landings[4 * per - 1 : 5 * per - 2], [second_hop, first_hop] + clip_hops, (1, 2, 2))

    need(grad)
    lead = (head == 0).astype(FLOAT)
    row = lax.rem(rows_iota((frames * rows, 1)), rows)
    is_patch = row < patches
    class_grad = grad[0, patches : patches + 1]
    values = grad[...].reshape(flat)
    sums = {}
    sums["bias2"] = (
        jnp.sum(jnp.where(is_patch, values, 0.0), axis=0, keepdims=True) + lead * class_grad
    )
    values = jnp.where(
        is_patch, values, jnp.where(row == patches, class_grad * (1.0 / all_frames), 0.0)
    )
    half = values.astype(HALF)
    outer_grad[...] = half.reshape(shaped)
    need(bundles)
    for place in range(blocks):
        joint[place * own_width : (place + 1) * own_width] = bundles[place, 3 * own_width :]
    mixed_back[...] = mm_t(outer_grad[...].reshape(flat), joint[...]).astype(HALF).reshape(shaped)

    need(mlp)
    spots = [
        (a, b, c) for a in range(2) for b in range(2) for c in range(2)
    ]

    def add_landed(source, dest, columns):
        def load(number):
            slot = number % 2
            return pltpu.make_async_copy(
                source.at[spots[number]],
                loaded.at[slot, :, :, pl.ds(0, columns)],
                load_sems.at[slot],
            )

        load(0).start()
        for number, place in enumerate(spots):
            if number + 1 < len(spots):
                load(number + 1).start()
            load(number).wait()

            def add(index, carry):
                dest[place + (index,)] = (
                    dest[place + (index,)].astype(FLOAT)
                    + loaded[number % 2, index, :, :columns].astype(FLOAT)
                ).astype(HALF)
                return carry

            lax.fori_loop(0, rest_size, add, 0)

    add_landed(recv_in, mlp, 2 * hidden)
    chain_one.launch()
    chain_two.launch()

    need(space_soft, space_qkv)
    masks = half_masks()

    def one_frame(frame, carry):
        pairs = width // PAIR
        for group in range(2):
            chosen = range(group * pairs // 2, (group + 1) * pairs // 2)
            backs, mines = [], []
            for pair in chosen:
                spot = slice(pair * PAIR, (pair + 1) * PAIR)
                value = space_qkv[2, frame, :, spot]
                for side in range(2):
                    mine = mixed_back[frame, :, spot] * masks[side]
                    mines.append(mine)
                    backs.append(mm_t(value, mine))
            scores = []
            for number, pair in enumerate(chosen):
                for side in range(2):
                    soft = space_soft[frame, 2 * pair + side].astype(FLOAT)
                    product = soft * backs[2 * number + side]
                    score = product - soft * jnp.sum(product, axis=0, keepdims=True)
                    scores.append(score.astype(HALF))
            for number, pair in enumerate(chosen):
                spot = slice(pair * PAIR, (pair + 1) * PAIR)
                query, key = space_qkv[0, frame, :, spot], space_qkv[1, frame, :, spot]
                left, right = scores[2 * number], scores[2 * number + 1]
                value_back = mm(space_soft[frame, 2 * pair], mines[2 * number]) + mm(
                    space_soft[frame, 2 * pair + 1], mines[2 * number + 1]
                )
                key_back = mm(left, query * masks[0]) + mm(right, query * masks[1])
                query_back = t_mm(left, key * masks[0]) + t_mm(right, key * masks[1])
                space_qkv[0, frame, :, spot] = (query_back * (HEAD_DIM**-0.5)).astype(HALF)
                space_qkv[1, frame, :, spot] = key_back.astype(HALF)
                space_qkv[2, frame, :, spot] = value_back.astype(HALF)
        return carry

    lax.fori_loop(0, frames, one_frame, 0)
    incoming = jnp.zeros(flat, FLOAT)
    for kind in range(3):
        for place in range(blocks):
            joint[place * own_width : (place + 1) * own_width] = bundles[
                place, kind * own_width : (1 + kind) * own_width
            ]
        piece = space_qkv[kind].reshape(flat)
        incoming = incoming + mm(piece, joint[...])
        if kind != 1:
            sums["space%d" % kind] = jnp.sum(piece.astype(FLOAT), axis=0, keepdims=True)
    need(state)
    unit, inverse = normalize(state[...].reshape(flat))
    sums["gain1"] = jnp.sum(incoming * unit, axis=0, keepdims=True)
    sums["shift1"] = jnp.sum(incoming, axis=0, keepdims=True)
    by_frame = incoming.reshape(shaped)
    part = by_frame[0, patches : patches + 1]
    for frame in range(1, frames):
        part = part + by_frame[frame, patches : patches + 1]
    class_parts[head] = part
    class_state_grad = class_grad
    change = normalize_back(incoming * gains[1:2, :], unit, inverse)
    result = jnp.where(is_patch, grad[...].reshape(flat) + change, 0.0)
    grad[...] = result.reshape(shaped)
    sums["bias1"] = jnp.sum(result, axis=0, keepdims=True)
    half = result.astype(HALF)
    time_grad = mixed_back
    time_grad[...] = half.reshape(shaped)
    need(weight)
    back = mm_t(time_grad[...].reshape(flat), weight[...]).astype(HALF)
    mine = pl.multiple_of(head * frames, frames)
    proj_back[pl.ds(mine, frames)] = back.reshape(shaped)
    far_copies = [
        wires.to(far_peer, proj_back.at[mine + frame], proj_back.at[mine + frame])
        for frame in range(frames)
    ]
    own_part = proj_back.at[pl.ds(mine, frames)]
    near_copy = wires.to(near_peer, own_part, own_part)
    class_copies = [
        wires.to(peer, class_parts.at[head], class_parts.at[head]) for peer in others
    ]
    sums["bias0"] = jnp.sum(back.astype(FLOAT), axis=0, keepdims=True)

    ready[id(weight)] = wires.move(time_weight_in, weight)

    need(space_normed, spread, proj)

    def place_rows(part, result):
        return result[part * cut : (part + 1) * cut]

    turned = space_normed[...].reshape(flat).T
    for kind in range(4):
        if kind == 3:
            turned = outer_grad[...].reshape(flat).T
            result = mm(turned, spread[...].reshape(flat)).astype(HALF)
        else:
            result = mm(turned, space_qkv[kind].reshape(flat)).astype(HALF)
        for block in range(blocks):
            relative = flip_all(head, block, blocks)
            core, across = lax.rem(relative, 2), lax.div(relative, 2)
            for part in range(cuts):
                space[
                    (core, across)
                    + spread_index(clip, part, cuts, rest_size, cut)
                    + (slice(kind * own_width, (kind + 1) * own_width),)
                ] = place_rows(part, result)[:, block * own_width : (block + 1) * own_width]
    core_copy = wires.to(near_peer, space.at[1], space_landing)
    turned = proj[...].reshape(flat).T
    result = mm(turned, time_grad[...].reshape(flat)).astype(HALF)
    for part in range(cuts):
        mixer_data[(0,) + spread_index(clip, part, cuts, rest_size, cut)] = place_rows(part, result)
    chain_mixer.launch()

    need(qkv, time_soft, time_output, weight)

    def outer(block):
        start = pl.multiple_of(block * frames, frames)
        back = mm_t(proj_back[pl.ds(start, frames)].reshape(flat), time_output[...])
        back = back.astype(HALF)
        gap = jnp.zeros((frames * rows, wide - own_width), HALF)
        time_back[pl.ds(start, frames)] = jnp.concatenate([back, gap], axis=1).reshape(
            frames, rows, wide
        )

    outer(head)
    near_copy.wait_recv()
    outer(near)
    passed = []
    for frame in range(frames):
        far_copies[frame].wait_recv()
        here = proj_back.at[far * frames + frame]
        passed.append(wires.to(near_peer, here, here))
    outer(far)
    core_copy.wait_recv()
    add_landed(space_landing, space.at[0], 4 * own_width)
    chain_space.launch()
    for copy in passed:
        copy.wait_recv()
    outer(cross)
    total_rows = all_frames * TILE
    groups = rows // TILE
    batch = 3

    def time_backward(chosen):
        work = []
        for group in chosen:
            spot = pl.ds(pl.multiple_of(group * TILE, TILE), TILE)
            piece = qkv[:, spot, :].reshape(total_rows, 3 * wide)
            outers = time_back[:, spot, :].reshape(total_rows, wide)
            backs, mines = [], []
            for number in range(heads):
                left = (number // 2) * PAIR
                own = outers[:, left : left + PAIR] * masks[number % 2]
                mines.append(own)
                backs.append(mm_t(piece[:, 2 * wide + left : 2 * wide + left + PAIR], own))
            work.append((group, spot, piece, mines, backs))
        for group, spot, piece, mines, backs in work:
            parts = [[], [], []]
            for pair in range(wide // PAIR):
                left = pair * PAIR
                query = piece[:, left : left + PAIR]
                key = piece[:, wide + left : wide + left + PAIR]
                found = None
                for side in range(2):
                    number = 2 * pair + side
                    if number >= heads:
                        continue
                    soft = time_soft[group, number]
                    large = soft.astype(FLOAT)
                    product = large * backs[number]
                    score = product - large * jnp.sum(product, axis=0, keepdims=True)
                    score = score.astype(HALF)
                    terms = [
                        t_mm(score, key * masks[side]),
                        mm(score, query * masks[side]),
                        mm(soft, mines[number]),
                    ]
                    found = terms if found is None else [x + y for x, y in zip(found, terms)]
                for kind, scale in enumerate((HEAD_DIM**-0.5, 1.0, 1.0)):
                    parts[kind].append((found[kind] * scale).astype(HALF))
            joined = jnp.concatenate(parts[0] + parts[1] + parts[2], axis=1)
            qkv[:, spot, :] = joined.reshape(all_frames, TILE, 3 * wide)

    def body(step, carry):
        time_backward([step * batch + i for i in range(batch)])
        return carry

    lax.fori_loop(0, groups // batch, body, 0)
    for group in range(groups // batch * batch, groups):
        time_backward([group])

    need(normed)
    norm_sums = [jnp.zeros((1, width), FLOAT), jnp.zeros((1, width), FLOAT)]
    bias_sums = jnp.zeros((1, 3 * wide), FLOAT)

    def inner(block):
        start = pl.multiple_of(block * frames, frames)
        piece = qkv[pl.ds(start, frames)].reshape(frames * rows, 3 * wide)
        result = mm(piece, weight[...])
        values = normed[pl.ds(start, frames)].reshape(flat).astype(FLOAT)
        norm_sums[0] = norm_sums[0] + jnp.sum(result * values, axis=0, keepdims=True)
        norm_sums[1] = norm_sums[1] + jnp.sum(result, axis=0, keepdims=True)
        return result, jnp.sum(piece.astype(FLOAT), axis=0, keepdims=True)

    result, more = inner(cross)
    bias_sums = bias_sums + more
    space_qkv[0] = result.astype(HALF).reshape(shaped)
    back_cross = wires.to(near_peer, space_qkv.at[0], near_landing.at[0])
    result, more = inner(far)
    bias_sums = bias_sums + more
    back_cross.wait_recv()
    result = result + near_landing[0].reshape(flat).astype(FLOAT)
    space_qkv[1] = result.astype(HALF).reshape(shaped)
    back_far = wires.to(far_peer, space_qkv.at[1], far_landing)
    result, more = inner(near)
    bias_sums = bias_sums + more
    space_qkv[2] = result.astype(HALF).reshape(shaped)
    back_near = wires.to(near_peer, space_qkv.at[2], near_landing.at[1])
    result, more = inner(head)
    bias_sums = bias_sums + more
    outer_grad[...] = result.astype(HALF).reshape(shaped)

    sums["gain0"] = (norm_sums[0] - norm_sums[1] * shifts[0:1, :]) / gains[0:1, :]
    sums["shift0"] = norm_sums[1]
    lane = lanes_iota((1, width))
    here = (lane >= head * own_width) & (lane < (head + 1) * own_width)
    for kind in (0, 2):
        own = bias_sums[:, kind * wide : kind * wide + own_width]
        repeated = jnp.concatenate([own] * blocks, axis=1)
        sums["time%d" % kind] = jnp.where(here, repeated, 0.0)
    names = [
        sums["gain0"],
        sums["gain1"],
        mlp_sums[0:1],
        sums["shift0"],
        sums["shift1"],
        mlp_sums[1:2],
        sums["bias0"],
        sums["bias1"],
        sums["bias2"],
        mlp_sums[2:3],
        sums["time0"],
        sums["time2"],
        sums["space0"],
        sums["space2"],
    ]
    for number, value in enumerate(names):
        vectors[0, number : number + 1] = value
    vectors[0, len(names) : len(names) + blocks] = hidden_sums[...]
    vectors[0, len(names) + blocks :] = jnp.zeros(
        (vectors.shape[1] - len(names) - blocks, width), FLOAT
    )
    vector_peers = [near_peer, far_peer] + clip_peers
    vector_copies = [wires.to(vector_peers[0], vectors.at[0], vector_landing.at[0])]

    def vector_step(out=None):
        number = len(vector_copies)
        vector_copies[-1].wait_recv()
        total = vectors[number - 1] + vector_landing[number - 1]
        if number == len(vector_peers):
            sums_out[...] = total
            return
        vectors[number] = total
        vector_copies.append(
            wires.to(vector_peers[number], vectors.at[number], vector_landing.at[number])
        )

    need(mixed)

    def over_blocks(left, right):
        total = None
        for block in range(blocks):
            spot = slice(block * frames, (block + 1) * frames)
            term = t_mm(
                left[spot].reshape(flat), right[spot].reshape(frames * rows, right.shape[2])
            )
            total = term if total is None else total + term
        return total

    result = over_blocks(normed, qkv)
    pieces = [result[:, kind * wide : kind * wide + own_width].astype(HALF) for kind in range(3)]
    result = over_blocks(proj_back, mixed)
    joined = jnp.concatenate(pieces + [result.astype(HALF)], axis=1)
    for part in range(cuts):
        time_data[(0,) + spread_index(clip, part, cuts, rest_size, cut)] = place_rows(part, joined)
    chain_time.launch()
    vector_step()
    chain_one.step()
    chain_two.step()
    vector_step()
    chain_mixer.step()

    back_near.wait_recv()
    back_far.wait_recv()
    for frame in range(frames):
        unit, inverse = normalize(tokens[frame].astype(FLOAT))
        incoming = (
            outer_grad[frame, :patches].astype(FLOAT)
            + near_landing[1, frame, :patches].astype(FLOAT)
            + far_landing[frame, :patches].astype(FLOAT)
        )
        patch_out[frame] = grad[frame, :patches] + normalize_back(
            incoming * gains[0:1, :], unit, inverse
        )
    for copy in class_copies:
        copy.wait_recv()
    unit, inverse = normalize(class_token[...].astype(FLOAT))
    incoming = class_parts[0]
    for place in range(1, blocks):
        incoming = incoming + class_parts[place]
    class_out[...] = class_state_grad + normalize_back(incoming * gains[1:2, :], unit, inverse)

    def put_hidden(value):
        hidden_out[...] = value

    def put_return(value):
        return_out[...] = value.T

    def put_space(value):
        space_out[...] = value

    def put_time(value):
        time_out[...] = value

    def put_mixer(value):
        mixer_sums[0] = value

    chain_space.step()
    queue = [
        (chain_one, put_hidden),
        (chain_two, put_return),
        (chain_mixer, put_mixer),
        (chain_space, put_space),
        (chain_time, put_time),
    ]
    while queue:
        left = []
        for chain, put in queue:
            last = chain.at == len(chain.hops) - 1
            chain.step(put if last else None)
            if not last:
                left.append((chain, put))
        queue = left
        if len(vector_copies) < len(vector_peers):
            vector_step()
    while len(vector_copies) < len(vector_peers):
        vector_step()
    vector_step()
    for number, peer in enumerate((near_peer, far_peer)):
        copy = wires.to(peer, mixer_sums.at[number], mixer_landing.at[number])
        copy.wait_recv()
        value = mixer_sums[number] + mixer_landing[number]
        if number == 0:
            mixer_sums[1] = value
        else:
            mixer_out[...] = value
    for copy in wires.sent:
        if all(copy is not other for other in wires.done):
            copy.wait_send()


VMEM = pl.BlockSpec(memory_space=pltpu.VMEM)
ANY = pl.BlockSpec(memory_space=pl.ANY)
WIRES = 64
LIMIT = 125 * 2**19


def shape(dims, kind=HALF):
    return jax.ShapeDtypeStruct(tuple(dims), kind)


def room(dims, kind=HALF):
    return pltpu.VMEM(tuple(dims), kind)


def landing_rooms(axes, start, rest, cut, columns):
    extent = list(start) + [rest]
    found = []
    for axis in axes:
        if axis is not None:
            extent[axis] //= 2
        found.append(room(extent + [cut, columns]))
    return found


def on_device(
    patch_tokens,
    class_token,
    keep_mask,
    patch_grad,
    class_grad,
    norm_gain,
    norm_bias,
    input_weight,
    input_bias,
    output_weight,
    time_mixer,
    output_bias,
    hidden_weight,
    hidden_bias,
    return_weight,
):
    blocks = lax.axis_size("head")
    clips = lax.axis_size("clip")
    head_index = lax.axis_index("head")
    clip_index = lax.axis_index("clip")
    _, frames, patches, width = patch_tokens.shape
    all_frames = keep_mask.shape[1]
    own_width = input_weight.shape[-1]
    heads = own_width // HEAD_DIM
    all_heads = heads * blocks
    hidden = hidden_weight.shape[-1]
    rows = round_up(patches + 1, TILE)
    groups = rows // TILE
    group_rows = all_frames * TILE
    wide = round_up(own_width, PAIR)
    cut = width // clips
    dense = 1
    while cut * dense % TILE:
        dense *= 2
    block_rows = cut * dense
    rest = clips // (4 * dense)
    tokens = frames * rows
    gains, shifts, biases = norm_gain[0], norm_bias[0], output_bias[0]
    patch_state = patch_tokens[0]

    turned = jnp.transpose(input_weight[0], (0, 2, 3, 1))
    time_weight = jnp.pad(turned[0], ((0, 0), (0, wide - own_width), (0, 0))).reshape(
        3 * wide, width
    )
    bundle = jnp.concatenate(
        [output_weight[0, 0], turned[1].reshape(3 * own_width, width), output_weight[0, 1]], axis=0
    )
    small = jnp.concatenate([input_bias[0].reshape(-1), hidden_bias[0]])[None]
    keep_t = jnp.pad(keep_mask[0].T.astype(FLOAT), ((0, rows - patches), (0, 0)))

    full = (frames, rows, width)
    everything = (all_frames, rows, width)
    qkv_dims = (all_frames, rows, 3 * wide)
    time_soft_dims = (groups, heads, group_rows, group_rows)
    mixed_dims = (all_frames, rows, own_width)
    space_soft_dims = (frames, all_heads, rows, rows)
    bundle_dims = (blocks,) + bundle.shape
    halves = (2, 2, 2, rest, block_rows, 2 * hidden)
    kept_outs = [
        shape(everything),
        shape(qkv_dims),
        shape(time_soft_dims),
        shape(mixed_dims),
        shape(full, FLOAT),
        shape(full),
        shape(full),
        shape((3,) + full),
        shape(space_soft_dims),
        shape(full),
        shape(bundle_dims),
        shape(full, FLOAT),
        shape(halves),
        shape(halves),
    ]
    direct_outs = [
        shape((frames, patches, width), FLOAT),
        shape((1, width), FLOAT),
        shape((8, width), FLOAT),
        shape((blocks, hidden), FLOAT),
    ]
    sems = [pltpu.SemaphoreType.DMA((WIRES,))] * 3
    (
        normed, qkv, time_soft, mixed, state, proj, space_normed, space_qkv, space_soft, spread,
        bundles, grads, kept, recv, patch_out, class_out, mlp_sums, hidden_sums,
    ) = pl.pallas_call(
        functools.partial(forward_kernel, heads, clips),
        out_shape=kept_outs + direct_outs,
        in_specs=[VMEM] * 8 + [ANY] * 6,
        out_specs=[ANY] * len(kept_outs) + [VMEM] * len(direct_outs),
        scratch_shapes=[
            room(everything),
            room(qkv_dims),
            room(time_soft_dims),
            room(mixed_dims),
            room((blocks, frames, rows, own_width)),
            room(full, FLOAT),
            room(full),
            room(full),
            room((3,) + full),
            room(space_soft_dims),
            room(full),
            room((width, width)),
            room((frames, rows, rows), FLOAT),
            room(bundle_dims),
            room((blocks, width, hidden)),
            room((blocks, hidden, width)),
            room((blocks,) + small.shape, FLOAT),
            room((3 * wide, width)),
            room((width, width)),
            room((frames, patches, width)),
            room((blocks, 1, width), FLOAT),
            room(full, FLOAT),
            room(full, FLOAT),
            room((tokens, width)),
            room((tokens, width)),
            room((2, 2, rest, block_rows, tokens)),
            room((2, 2, rest, block_rows, tokens)),
            room((tokens, width), FLOAT),
            room((tokens, width), FLOAT),
            room((2, 2, 2, rest, block_rows, 2 * hidden)),
        ]
        + sems,
        cost_estimate=pl.CostEstimate(
            flops=int(30e9), bytes_accessed=int(40e6), transcendentals=0
        ),
        compiler_params=pltpu.CompilerParams(
            vmem_limit_bytes=LIMIT, collective_id=0, has_side_effects=True
        ),
        name="forward",
    )(
        patch_state,
        class_token,
        class_grad,
        keep_t,
        small,
        gains,
        shifts,
        biases,
        patch_grad[0],
        time_weight,
        time_mixer[0],
        bundle,
        hidden_weight[0],
        return_weight[0],
    )

    clip_bits = clips.bit_length() - 1
    later = [3 if 1 << number < rest else None for number in range(clip_bits - 2)]
    vector_rows = round_up(14 + blocks, 8)
    vector_hops = 2 + clip_bits
    chains = [
        ([1, 0, 2] + later, (2, 2, 2), hidden),
        ([2, 1, 0] + later, (2, 2, 2), hidden),
        ([1, 0, 2] + later, (2, 2, 2), 4 * own_width),
        ([1, 2] + later, (1, 2, 2), 4 * own_width),
        ([2, 1] + later, (1, 2, 2), width),
    ]
    landings = []
    for axes, start, columns in chains:
        landings += landing_rooms(axes, start, rest, block_rows, columns)
    (
        patch_input_grad, class_input_grad, time_total, space_total, mixer_total, hidden_total,
        return_total, sums, _,
    ) = pl.pallas_call(
        functools.partial(backward_kernel, heads, clips),
        out_shape=[
            shape((frames, patches, width), FLOAT),
            shape((1, width), FLOAT),
            shape((block_rows, 4 * own_width), FLOAT),
            shape((block_rows, 4 * own_width), FLOAT),
            shape((block_rows, width), FLOAT),
            shape((block_rows, hidden), FLOAT),
            shape((hidden, block_rows), FLOAT),
            shape((vector_rows, width), FLOAT),
            shape((2, 2, 2, rest, block_rows, 4 * own_width)),
        ],
        in_specs=[VMEM] * 6 + [ANY] * 16,
        out_specs=[VMEM] * 8 + [ANY],
        scratch_shapes=[
            room(full, FLOAT),
            room((blocks, 4 * own_width, width)),
            room((own_width, width)),
            room((width, width)),
            room(everything),
            room(qkv_dims),
            room(time_soft_dims),
            room(mixed_dims),
            room(full, FLOAT),
            room(full),
            room(full),
            room((3,) + full),
            room(space_soft_dims),
            room(full),
            room((width, width)),
            room(full),
            room(full),
            room(everything),
            room((all_frames, rows, wide)),
            room((2,) + full),
            room(full),
            room((blocks, 1, width), FLOAT),
            room(halves),
            room((2, rest, block_rows, 2 * hidden)),
            room((2, 2, 2, 2, rest, block_rows, 4 * own_width)),
            room((1, 2, 2, rest, block_rows, 4 * own_width)),
            room((1, 2, 2, rest, block_rows, width)),
            room((2, block_rows, width), FLOAT),
            room((2, block_rows, width), FLOAT),
            room((vector_hops, vector_rows, width), FLOAT),
            room((vector_hops, vector_rows, width), FLOAT),
        ]
        + landings
        + sems
        + [pltpu.SemaphoreType.DMA((2,))],
        cost_estimate=pl.CostEstimate(
            flops=int(20e9), bytes_accessed=int(40e6), transcendentals=0
        ),
        compiler_params=pltpu.CompilerParams(
            vmem_limit_bytes=LIMIT, collective_id=1, has_side_effects=True
        ),
        name="backward",
    )(
        patch_state,
        class_token,
        gains,
        shifts,
        mlp_sums,
        hidden_sums,
        grads,
        bundles,
        time_weight,
        time_mixer[0],
        normed,
        qkv,
        time_soft,
        mixed,
        state,
        proj,
        space_normed,
        space_qkv,
        space_soft,
        spread,
        kept,
        recv,
    )

    if dense > 1:
        start = lax.div(clip_index, clips // dense) * cut
        time_total, space_total, mixer_total, hidden_total = [
            lax.dynamic_slice_in_dim(total, start, cut, 0)
            for total in (time_total, space_total, mixer_total, hidden_total)
        ]
        return_total = lax.dynamic_slice_in_dim(return_total, start, cut, 1)
    share = cut // blocks
    mixer_grad = lax.dynamic_slice_in_dim(mixer_total, head_index * share, share, 0)
    part = width // (clips * blocks)
    both = clip_index * blocks + head_index
    shared = lax.dynamic_slice_in_dim(sums[:10], both * part, part, 1)
    other = head_index * clips + clip_index
    input_bias_grad = lax.dynamic_slice_in_dim(
        sums[10:14].reshape(2, 2, width), other * part, part, 2
    )
    hidden_part = blocks * hidden // (clips * blocks)
    hidden_bias_grad = lax.dynamic_slice_in_dim(
        sums[14 : 14 + blocks].reshape(-1), other * hidden_part, hidden_part, 0
    )
    joined = jnp.stack([time_total, space_total])
    input_weight_grad = joined[:, :, : 3 * own_width].reshape(2, cut, 3, own_width)
    output_weight_grad = jnp.transpose(joined[:, :, 3 * own_width :], (0, 2, 1))
    quarter = width // blocks
    return (
        patch_out[None],
        lax.dynamic_slice_in_dim(class_out, head_index * quarter, quarter, 1),
        patch_input_grad[None],
        lax.dynamic_slice_in_dim(class_input_grad, head_index * quarter, quarter, 1),
        shared[None, 0:3],
        shared[None, 3:6],
        input_weight_grad[None],
        input_bias_grad[None],
        output_weight_grad[None],
        mixer_grad[None],
        shared[None, 6:10],
        hidden_total[None],
        hidden_bias_grad[None],
        return_total[None],
    )


def solution(mesh):
    in_specs = (
        P("clip", "head", None, None),
        P("clip", None),
        P("clip", None, None),
        P("clip", "head", None, None),
        P("clip", None),
        P(),
        P(),
        P(None, None, None, None, "head"),
        P(None, None, None, "head"),
        P(None, None, "head", None),
        P(),
        P(),
        P(None, None, "head"),
        P(None, "head"),
        P(None, "head", None),
    )
    out_specs = (
        P("clip", "head", None, None),
        P("clip", "head"),
        P("clip", "head", None, None),
        P("clip", "head"),
        P(None, None, ("clip", "head")),
        P(None, None, ("clip", "head")),
        P(None, None, "clip", None, "head"),
        P(None, None, None, ("head", "clip")),
        P(None, None, "head", "clip"),
        P(None, ("clip", "head"), None),
        P(None, None, ("clip", "head")),
        P(None, "clip", "head"),
        P(None, ("head", "clip")),
        P(None, "head", "clip"),
    )
    return jax.shard_map(
        on_device, mesh=mesh, in_specs=in_specs, out_specs=out_specs, check_vma=False
    )
```

```python
import functools

import jax
import jax.numpy as jnp
from jax import lax
from jax.experimental import pallas as pl
from jax.experimental.pallas import tpu as pltpu
from jax.sharding import PartitionSpec as P

HEAD_DIM = 64
PAIR = 2 * HEAD_DIM
TILE = 16
EPSILON = 1e-06
MASKED = -1e30
FLOAT = jnp.float32
HALF = jnp.bfloat16
ROW_ROW = (((1,), (1,)), ((), ()))
COL_COL = (((0,), (0,)), ((), ()))
ROOT_HALF = 0.7071067811865476
ROOT_TWO_PI = 0.3989422804014327


HOPS = {
    "A": "yzxw",
    "B": "zxyw",
    "C": "xyzw",
    "S": "yzxw",
    "R": "zxyw",
    "T": "yzw",
    "U": "yzw",
    "X": "yzw",
}
SHARES = (4, 6, 2)
SCHEDULE = {
    "begin": (
        "A+", "B+", "C+",
    ),
    "sw": (
        "A-", "A+", "C-", "C+",
    ),
    "X": (
        "X+",
    ),
    "x1": (
        "B-",
    ),
    "S": (
        "S+",
    ),
    "c2": (
        "C-", "C+",
    ),
    "R": (
        "R+",
    ),
    "c3": (
        "X-", "X+",
    ),
    "ag0": (
        "A-",
    ),
    "ag2": (
        "B+", "A+",
    ),
    "p0": (
        "C-", "C+",
    ),
    "rc0": (
        "C-",
    ),
    "rn": (
        "A-", "A+", "X-", "X+",
    ),
    "V": (
        "V+",
    ),
    "T": (
        "T+",
    ),
    "t1": (
        "V-", "V+", "S-", "S+", "R-", "R+",
    ),
    "U": (
        "U+",
    ),
    "rx": (
        "X-", "X+", "A-", "V-", "V+", "T-", "T+", "B-", "B+", "V-", "V+", "X-", "X+", "S-",
        "S+", "U-", "U+", "V-", "V+", "T-", "T+", "R-", "R+", "B-", "B+", "X-", "X+", "U-",
        "U+", "X-", "S-", "S+", "R-", "R+",
    ),
    "tail": (
        "V-", "T-", "U-", "S-", "R-", "B-",
    ),
}


def column_groups(total):
    found, start = {}, 0
    for name, share in zip("ABC", SHARES):
        count = total * share // sum(SHARES)
        if count:
            found[name] = (start, count)
        start += count
    return found


def round_up(value, unit):
    return -(-value // unit) * unit


def mm(left, right):
    return jnp.dot(left, right, preferred_element_type=FLOAT)


def mm_t(left, right):
    return lax.dot_general(left, right, ROW_ROW, preferred_element_type=FLOAT)


def t_mm(left, right):
    return lax.dot_general(left, right, COL_COL, preferred_element_type=FLOAT)


def normalize(values):
    average = jnp.mean(values, axis=-1, keepdims=True)
    centred = values - average
    spread = jnp.mean(centred * centred, axis=-1, keepdims=True)
    inverse = lax.rsqrt(spread + EPSILON)
    return centred * inverse, inverse


def normalize_back(scaled, unit, inverse):
    first = jnp.mean(scaled, axis=-1, keepdims=True)
    second = jnp.mean(scaled * unit, axis=-1, keepdims=True)
    return (scaled - first - unit * second) * inverse


def rows_iota(shape):
    return lax.broadcasted_iota(jnp.int32, shape, 0)


def lanes_iota(shape):
    return lax.broadcasted_iota(jnp.int32, shape, 1)


def half_masks():
    lanes = lanes_iota((1, PAIR))
    first = (lanes < HEAD_DIM).astype(HALF)
    return first, (1 - first).astype(HALF)


def softmax_columns(scores):
    top = jnp.max(scores, axis=0, keepdims=True)
    exponent = jnp.exp(scores - top)
    total = jnp.sum(exponent, axis=0, keepdims=True)
    return exponent * (1.0 / total)


def gelu_parts(values):
    size = jnp.abs(values)
    density = jnp.exp(-0.5 * values * values)
    step = 1.0 / (1.0 + (0.3275911 * ROOT_HALF) * size)
    tail = step * (
        0.5 * 0.254829592
        + step
        * (
            0.5 * -0.284496736
            + step * (0.5 * 1.421413741 + step * (0.5 * -1.453152027 + step * (0.5 * 1.061405429)))
        )
    )
    tail = tail * density
    return jnp.where(values < 0.0, tail, 1.0 - tail), density * ROOT_TWO_PI


def flip(value, mask):
    return value + mask - 2 * mask * lax.rem(lax.div(value, mask), 2)


def flip_all(value, number, size):
    total, bit = 0, 1
    while bit < size:
        mine = lax.rem(lax.div(value, bit), 2)
        total = total + bit * ((1 - mine) if number & bit else mine)
        bit *= 2
    return total


def spread_index(clip, part, cuts, rest, cut):
    bits = []
    bit = 1
    while bit < 4 * rest:
        mine = lax.rem(lax.div(clip, bit), 2)
        bits.append(1 - mine if part & bit else mine)
        bit *= 2
    inner = 0
    for value in bits[2:]:
        inner = 2 * inner + value
    outer = part // (4 * rest)
    return bits[0], bits[1], inner, pl.ds(outer * cut, cut)


class Wires:
    def __init__(self, send, recv, local):
        self.send, self.recv, self.local = send, recv, local
        self.sent, self.moved, self.done = [], [], []

    def to(self, peer, source, dest):
        slot = len(self.sent)
        copy = pltpu.make_async_remote_copy(
            src_ref=source,
            dst_ref=dest,
            send_sem=self.send.at[slot],
            recv_sem=self.recv.at[slot],
            device_id=peer,
            device_id_type=pl.DeviceIdType.MESH,
        )
        copy.start()
        self.sent.append(copy)
        return copy

    def drain(self, copy):
        copy.wait_send()
        self.done.append(copy)

    def finish(self):
        for copy in self.sent:
            if all(copy is not other for other in self.done):
                copy.wait_send()

    def move(self, source, dest):
        copy = pltpu.make_async_copy(source, dest, self.local.at[len(self.moved)])
        copy.start()
        self.moved.append(copy)
        return copy


def greet(peers):
    barrier = pltpu.get_barrier_semaphore()
    for peer in peers:
        pl.semaphore_signal(
            barrier, inc=1, device_id=peer, device_id_type=pl.DeviceIdType.MESH
        )
    pl.semaphore_wait(barrier, len(peers))


def by_rows(packed, frames):
    width = packed.shape[1] // frames
    return jnp.concatenate(
        [packed[:, frame * width : (frame + 1) * width] for frame in range(frames)], axis=0
    )


def own_lanes(row, head, blocks):
    part = row.shape[1] // blocks
    total = jnp.zeros((row.shape[0], part), FLOAT)
    for block in range(blocks):
        total = jnp.where(head == block, row[:, block * part : (block + 1) * part], total)
    return total


def pick(rows, first, count):
    lane = rows_iota((rows.shape[1], count))
    chosen = lane == lanes_iota((rows.shape[1], count)) + first
    return lax.dot_general(
        rows,
        chosen.astype(FLOAT),
        (((1,), (0,)), ((), ())),
        precision=lax.Precision.HIGHEST,
        preferred_element_type=FLOAT,
    )


def load_wide(wires, projections, dest, own_width):
    wide = dest.shape[0] // 3
    copies = []
    for kind in range(3):
        start = kind * wide
        copies.append(wires.move(projections.at[0, kind], dest.at[pl.ds(start, own_width)]))
        dest[start + own_width : start + wide] = jnp.zeros(
            (wide - own_width, dest.shape[1]), HALF
        )
    return copies


class Gather:
    def __init__(self, wires, peers, clip, head, sources, dest):
        self.wires, self.peers, self.dest = wires, peers, dest
        self.head = head
        self.rows = dest.shape[1]
        self.piece = self.rows // 4
        self.half = round_up(self.piece // 2, TILE)
        self.mine = lax.rem(clip, 4)
        self.far = flip(head, 2)
        self.own, start = [], 0
        for source in sources:
            count = source.shape[0]
            self.own.append(wires.move(source, dest.at[head, pl.ds(start, count)]))
            start += count
        self.source = sources[0] if len(sources) == 1 else dest.at[head]

    def settle(self):
        for copy in self.own:
            copy.wait()

    def spot(self, piece, first=0, count=None):
        start = pl.multiple_of(piece * self.piece + first, TILE)
        return pl.ds(start, self.piece if count is None else count)

    def start_far(self):
        here = self.spot(self.mine)
        self.cross = self.wires.to(
            self.peers["far"], self.source.at[here], self.dest.at[self.head, here]
        )

    def start_near(self):
        self.near = self.wires.to(self.peers["near"], self.source, self.dest.at[self.head])

    def share(self):
        self.cross.wait_recv()
        here = self.dest.at[self.far, self.spot(self.mine)]
        self.first = self.wires.to(self.peers["one"], here, here)
        self.second = self.wires.to(self.peers["two"], here, here)

    def share_again(self):
        self.second.wait_recv()
        here = self.dest.at[self.far, self.spot(flip(self.mine, 2), 0, self.half)]
        third = self.wires.to(self.peers["one"], here, here)
        self.first.wait_recv()
        here = self.dest.at[
            self.far, self.spot(flip(self.mine, 1), self.half, self.piece - self.half)
        ]
        self.rest = [third, self.wires.to(self.peers["two"], here, here)]

    def pass_on(self):
        for copy in self.rest:
            copy.wait_recv()
        here = self.dest.at[self.far]
        self.last = self.wires.to(self.peers["near"], here, here)


def time_groups(heads, groups, qkv, keep_t, weights_out, out, masks, same, equal):
    frames = qkv.shape[0]
    wide = qkv.shape[2] // 3
    total_rows = frames * TILE
    work = []
    for group in groups:
        spot = pl.ds(pl.multiple_of(group * TILE, TILE), TILE)
        piece = qkv[:, spot, :].reshape(total_rows, 3 * wide)
        kept = keep_t[spot, :]
        kept = jnp.concatenate(
            [jnp.broadcast_to(kept[:, f : f + 1], (TILE, total_rows)) for f in range(frames)],
            axis=0,
        )
        blocked = jnp.where(same & ((kept > 0.5) | equal), 0.0, MASKED)
        scores = []
        for head in range(heads):
            left = (head // 2) * PAIR
            query = piece[:, left : left + PAIR]
            key = piece[:, wide + left : wide + left + PAIR]
            scores.append(mm_t(key * masks[head % 2], query) + blocked)
        work.append((group, spot, piece, scores))
    softs = []
    for group, spot, piece, scores in work:
        found = [softmax_columns(s).astype(HALF) for s in scores]
        for head in range(heads):
            weights_out[group, head] = found[head]
        softs.append(found)
    for (group, spot, piece, _), found in zip(work, softs):
        results = []
        for pair in range(wide // PAIR):
            left = 2 * wide + pair * PAIR
            value = piece[:, left : left + PAIR]
            total = t_mm(found[2 * pair], value * masks[0])
            if 2 * pair + 1 < heads:
                total = total + t_mm(found[2 * pair + 1], value * masks[1])
            results.append(total.astype(HALF))
        joined = jnp.concatenate(results, axis=1)[:, : heads * HEAD_DIM]
        joined = joined.reshape(frames, TILE, heads * HEAD_DIM)
        local = frames // out.shape[0]
        for block in range(out.shape[0]):
            own = [joined[block * local + frame] for frame in range(local)]
            out[block, spot, :] = jnp.concatenate(own, axis=1)


def forward_kernel(
    heads,
    cuts,
    tokens,
    class_token,
    class_grad,
    keep,
    input_bias,
    hidden_bias,
    gains,
    shifts,
    biases,
    grads_in,
    projections,
    outputs_in,
    mixer_in,
    first_in,
    second_in,
    normed_o,
    qkv_o,
    time_soft_o,
    mixed_o,
    state_o,
    proj_o,
    space_normed_o,
    space_qkv_o,
    space_soft_o,
    spread_o,
    bundles_o,
    grad_o,
    whole_o,
    patch_out,
    class_out,
    sums_out,
    hidden_sums,
    normed,
    qkv,
    time_soft,
    mixed,
    mixed_here,
    state,
    proj,
    space_normed,
    space_qkv,
    space_soft,
    spread,
    joint,
    blocked,
    bundles,
    first,
    second,
    smalls,
    keep_t,
    time_weight,
    mixer,
    grads,
    class_parts,
    full,
    grad,
    mlp_normed,
    grads_half,
    normed_t,
    grads_t,
    total,
    normed_back,
    found,
    core_landing,
    whole,
    *rest_refs,
):
    send_sems, recv_sems, local_sems = rest_refs[-3:]
    landings = list(rest_refs[:-3])
    clip, head = lax.axis_index("clip"), lax.axis_index("head")
    frames, patches, width = tokens.shape
    all_frames, rows, _ = normed.shape
    blocks = all_frames // frames
    own_width = mixed.shape[2] // frames
    wide = qkv.shape[2] // 3
    flat = (frames * rows, width)
    shaped = (frames, rows, width)
    rest, block_rows = normed_t.shape[2:4]
    cut = width // cuts
    hidden = first.shape[2]
    peers = {
        "near": (clip, flip(head, 1)),
        "far": (clip, flip(head, 2)),
        "cross": (clip, flip(flip(head, 1), 2)),
        "one": (flip(clip, 1), head),
        "two": (flip(clip, 2), head),
    }
    others = [peers["near"], peers["far"], peers["cross"]]
    wires = Wires(send_sems, recv_sems, local_sems)
    bundle = Gather(
        wires,
        peers,
        clip,
        head,
        [outputs_in.at[0]] + [projections.at[1, kind] for kind in range(3)] + [outputs_in.at[1]],
        bundles,
    )
    weight_copies = load_wide(wires, projections, time_weight, own_width)
    mixer_copy = wires.move(mixer_in, mixer)
    grads_copy = wires.move(grads_in, grads)
    gather_first = Gather(wires, peers, clip, head, [first_in], first)
    gather_second = Gather(wires, peers, clip, head, [second_in], second)
    for number in range(4):
        smalls[head, :, number * own_width : (number + 1) * own_width] = input_bias[
            number // 2, number % 2 : number % 2 + 1
        ]
    smalls[head, :, 4 * own_width :] = hidden_bias[...]
    keep_t[:patches] = keep[...].astype(FLOAT).T
    keep_t[patches:] = jnp.zeros((rows - patches, all_frames), FLOAT)
    greet(list(peers.values()))

    bundle.settle()
    bundle.start_far()
    small_copies = [wires.to(peer, smalls.at[head], smalls.at[head]) for peer in others]

    mine = pl.multiple_of(head * frames, frames)
    for frame in range(frames):
        unit, _ = normalize(tokens[frame].astype(FLOAT))
        normed[mine + frame, :patches] = (unit * gains[0] + shifts[0]).astype(HALF)
        normed[mine + frame, patches:] = jnp.zeros((rows - patches, width), HALF)
    own_part = normed.at[pl.ds(mine, frames)]
    near_copy = wires.to(peers["near"], own_part, own_part)
    bundle.start_near()

    for copy in small_copies:
        copy.wait_recv()
    bias_row = smalls[head]
    bias_gap = jnp.zeros((1, wide - own_width), FLOAT)
    query_bias = jnp.concatenate([bias_row[:, :own_width], bias_gap], axis=1)
    value_bias = jnp.concatenate([bias_row[:, own_width : 2 * own_width], bias_gap], axis=1)
    for copy in weight_copies:
        copy.wait()

    def project(block):
        start = pl.multiple_of(block * frames, frames)
        raw = mm_t(normed[pl.ds(start, frames)].reshape(flat), time_weight[...])
        query = (raw[:, :wide] + query_bias).astype(HALF) * (HEAD_DIM**-0.5)
        value = (raw[:, 2 * wide :] + value_bias).astype(HALF)
        joined = jnp.concatenate(
            [query.astype(HALF), raw[:, wide : 2 * wide].astype(HALF), value], axis=1
        )
        qkv[pl.ds(start, frames)] = joined.reshape(frames, rows, 3 * wide)

    project(head)
    near_copy.wait_recv()
    project(flip(head, 1))
    far_start = pl.multiple_of(flip(head, 2) * frames, frames)
    wires.drain(bundle.cross)
    far_copies, passed = [], []
    for frame in range(frames):
        here = normed.at[mine + frame]
        far_copies.append(wires.to(peers["far"], here, here))
        if frame == 0:
            bundle.share()
        wires.drain(far_copies[-1])
    gather_first.start_far()
    for frame in range(frames):
        far_copies[frame].wait_recv()
        here = normed.at[far_start + frame]
        passed.append(wires.to(peers["near"], here, here))
    project(flip(head, 2))
    for copy in passed:
        copy.wait_recv()
    project(flip(flip(head, 1), 2))
    gather_first.start_near()
    bundle.share_again()
    saved = [wires.move(normed, normed_o), wires.move(qkv, qkv_o)]

    masks = half_masks()
    square = (all_frames * TILE,) * 2
    key_index, query_index = rows_iota(square), lanes_iota(square)
    same = lax.rem(key_index, TILE) == lax.rem(query_index, TILE)
    equal = key_index == query_index
    groups = rows // TILE
    batch = 3
    middle = (groups // batch) // 2

    def attend(start, stop):
        def body(step, carry):
            time_groups(
                heads,
                [step * batch + i for i in range(batch)],
                qkv,
                keep_t,
                time_soft,
                mixed,
                masks,
                same,
                equal,
            )
            return carry

        lax.fori_loop(start, stop, body, 0)

    def exchange(first_row, count):
        spot = pl.ds(first_row, count)
        copies = []
        for peer in others:
            copies.append(
                wires.to(peer, mixed.at[peer[1], spot], mixed_here.at[head, spot])
            )
        return copies

    cut_row = middle * batch * TILE
    attend(0, middle)
    exchanged = exchange(0, cut_row)
    attend(middle, groups // batch)
    for group in range(groups // batch * batch, groups):
        time_groups(heads, [group], qkv, keep_t, time_soft, mixed, masks, same, equal)
    exchanged = exchanged + exchange(cut_row, rows - cut_row)
    mixed_here[head] = mixed[head]
    saved = saved + [wires.move(time_soft, time_soft_o), wires.move(mixed, mixed_o)]
    bundle.pass_on()
    gather_first.share()
    gather_second.start_near()
    keep_all = keep_t[...]
    key_index, query_index = rows_iota((rows, rows)), lanes_iota((rows, rows))
    for frame in range(frames):
        chosen = lanes_iota(keep_all.shape) == mine + frame
        kept = jnp.sum(jnp.where(chosen, keep_all, 0.0), axis=1, keepdims=True)
        allowed = (kept > 0.5) | (key_index == patches) | (key_index == query_index)
        blocked[frame] = jnp.where(allowed, 0.0, MASKED)
    for copy in (bundle.near, bundle.last):
        copy.wait_recv()
    saved.append(wires.move(bundles, bundles_o))
    for place in range(blocks):
        joint[place * own_width : (place + 1) * own_width] = bundles[place, :own_width]
    mixer_copy.wait()
    for copy in exchanged:
        copy.wait_recv()
    gather_second.start_far()
    sum_here = jnp.zeros(flat, FLOAT)
    for place in range(blocks):
        sum_here = sum_here + mm(
            by_rows(mixed_here[place], frames), bundles[place, :own_width]
        )
    half = (sum_here + biases[0:1, :]).astype(HALF)
    proj[...] = half.reshape(shaped)
    added = (mm(half, mixer[...]) + biases[1:2, :]).reshape(shaped)
    for frame in range(frames):
        state[frame, :patches] = tokens[frame].astype(FLOAT) + added[frame, :patches]
        state[frame, patches : patches + 1] = class_token[...].astype(FLOAT)
        state[frame, patches + 1 :] = jnp.zeros((rows - patches - 1, width), FLOAT)
    saved = saved + [wires.move(proj, proj_o), wires.move(state, state_o)]

    unit, _ = normalize(state[...].reshape(flat))
    row = rows_iota((frames * rows, 1))
    real = lax.rem(row, rows) <= patches
    half = jnp.where(real, unit * gains[1] + shifts[1], 0.0).astype(HALF)
    space_normed[...] = half.reshape(shaped)
    start_bias = 2 * own_width
    for kind in range(3):
        for place in range(blocks):
            joint[place * own_width : (place + 1) * own_width] = bundles[
                place, (1 + kind) * own_width : (2 + kind) * own_width
            ]
        raw = mm_t(space_normed[...].reshape(flat), joint[...])
        if kind != 1:
            begin = start_bias + (kind // 2) * own_width
            bias = jnp.concatenate(
                [smalls[place][:, begin : begin + own_width] for place in range(blocks)], axis=1
            )
            raw = raw + bias
        raw = raw.astype(HALF)
        if kind == 0:
            raw = (raw * (HEAD_DIM**-0.5)).astype(HALF)
        space_qkv[kind] = raw.reshape(shaped)
    saved = saved + [wires.move(space_normed, space_normed_o), wires.move(space_qkv, space_qkv_o)]
    gather_first.share_again()
    gather_second.share()

    def one_frame(frame, carry):
        softs = []
        for pair in range(width // PAIR):
            spot = slice(pair * PAIR, (pair + 1) * PAIR)
            query, key = space_qkv[0, frame, :, spot], space_qkv[1, frame, :, spot]
            for side in range(2):
                scores = mm_t(key * masks[side], query) + blocked[frame]
                softs.append(softmax_columns(scores).astype(HALF))
                space_soft[frame, 2 * pair + side] = softs[-1]
        for pair in range(width // PAIR):
            spot = slice(pair * PAIR, (pair + 1) * PAIR)
            value = space_qkv[2, frame, :, spot]
            result = t_mm(softs[2 * pair], value * masks[0]) + t_mm(
                softs[2 * pair + 1], value * masks[1]
            )
            spread[frame, :, spot] = result.astype(HALF)
        return carry

    lax.fori_loop(0, frames, one_frame, 0)
    saved = saved + [wires.move(space_soft, space_soft_o), wires.move(spread, spread_o)]
    for place in range(blocks):
        joint[place * own_width : (place + 1) * own_width] = bundles[place, 4 * own_width :]
    added = mm(spread[...].reshape(flat), joint[...]).reshape(shaped)
    part = added[0, patches : patches + 1]
    for frame in range(1, frames):
        part = part + added[frame, patches : patches + 1]
    class_parts[head] = part * (1.0 / all_frames)
    class_copies = [
        wires.to(peer, class_parts.at[head], class_parts.at[head]) for peer in others
    ]
    full[...] = state[...] + added + biases[2:3, :]
    gather_first.pass_on()
    gather_second.share_again()

    lead = (head == 0).astype(FLOAT)
    is_class = row == patches
    is_real = (lax.rem(row, rows) < patches) | is_class
    grads_copy.wait()
    for frame in range(frames):
        chosen = lanes_iota(keep_all.shape) == mine + frame
        kept = jnp.sum(jnp.where(chosen, keep_all, 0.0), axis=1, keepdims=True)
        grad[frame, :patches] = grads[frame].astype(FLOAT) * kept[:patches]
        grad[frame, patches:] = jnp.zeros((rows - patches, width), FLOAT)
    grad[0, patches : patches + 1] = class_grad[...].astype(FLOAT)
    values = grad[...].reshape(flat)
    grads_half[...] = values.astype(HALF)
    turned = jnp.where(is_class, values * lead, values)
    sums_out[2:3] = jnp.sum(turned, axis=0, keepdims=True)
    turned = turned.astype(HALF).T
    for part in range(cuts):
        grads_t[spread_index(clip, part, cuts, rest, cut)] = turned[part * cut : (part + 1) * cut]
    for copy in class_copies:
        copy.wait_recv()
    class_state = class_token[...].astype(FLOAT) + biases[2:3, :]
    for place in range(blocks):
        class_state = class_state + class_parts[place]
    full[0, patches : patches + 1] = class_state
    unit, _ = normalize(full[...].reshape(flat))
    values = jnp.where(is_real, unit * gains[2] + shifts[2], 0.0)
    mlp_normed[...] = values.astype(HALF)
    turned = jnp.where(is_class, values * lead, values).astype(HALF).T
    for part in range(cuts):
        normed_t[spread_index(clip, part, cuts, rest, cut)] = turned[part * cut : (part + 1) * cut]
    class_row = jnp.where(is_class, lead, 1.0)
    gather_second.pass_on()
    gather_first.settle()
    gather_second.settle()
    sends, firsts = [], []
    half_lanes = [pl.ds(0, hidden), pl.ds(hidden, hidden)]
    for number, block in enumerate((1, 0, 3, 2)):
        place = flip_all(head, block, blocks)
        if number == 0:
            gather_first.near.wait_recv()
            gather_second.near.wait_recv()
        if number == 2:
            gather_first.last.wait_recv()
            gather_second.last.wait_recv()
        inner = mm(mlp_normed[...], first[place]) + smalls[place][:, 4 * own_width :]
        outer = mm_t(grads_half[...], second[place])
        chance, density = gelu_parts(inner)
        active = (inner * chance).astype(HALF)
        back = (outer * (chance + inner * density)).astype(HALF)
        hidden_sums[pl.ds(place, 1)] = jnp.sum(
            back.astype(FLOAT) * class_row, axis=0, keepdims=True
        )
        forward = mm(active, second[place])
        backward = mm_t(back, first[place])
        if number == 0:
            total[...] = forward
            normed_back[...] = backward
        else:
            total[...] += forward
            normed_back[...] += backward
        factors = [(normed_t, back), (grads_t, active)]
        across = number // 2
        if number % 2 == 0:
            if sends:
                wires.drain(sends[-1])
            for lanes, (turned, factor) in zip(half_lanes, factors):
                piece = mm(turned[...].reshape(width, frames * rows), factor)
                found[:, :, :, :, lanes] = piece.astype(HALF).reshape(
                    2, 2, rest, block_rows, hidden
                )
            sends.append(wires.to(peers["near"], found, core_landing.at[across]))
            continue
        sends[-1].wait_recv()
        for lanes, (turned, factor) in zip(half_lanes, factors):
            piece = mm(turned[...].reshape(width, frames * rows), factor)
            landed = core_landing[across, :, :, :, :, lanes].astype(FLOAT)
            whole[across, :, :, :, :, lanes] = (
                piece.reshape(2, 2, rest, block_rows, hidden) + landed
            ).astype(HALF)
        if across == 0:
            for name, (start, count) in column_groups(2 * hidden).items():
                lanes = pl.ds(start, count)
                landing = landings.pop(0) if HOPS[name][0] in "yz" else None
                if HOPS[name][0] == "y":
                    source, peer = whole.at[0, 1, :, :, :, lanes], peers["one"]
                elif HOPS[name][0] == "z":
                    source, peer = whole.at[0, :, 1, :, :, lanes], peers["two"]
                else:
                    continue
                firsts.append((wires.to(peer, source, landing), landing, name, lanes))
        else:
            saved.append(wires.move(whole.at[1], whole_o.at[1]))
    result = (full[...].reshape(flat) + total[...] + biases[3:4, :]).reshape(shaped)
    for frame in range(frames):
        chosen = lanes_iota(keep_all.shape) == mine + frame
        kept = jnp.sum(jnp.where(chosen, keep_all, 0.0), axis=1, keepdims=True)
        patch_out[frame] = result[frame, :patches] * kept[:patches]
    class_out[...] = own_lanes(result[0, patches : patches + 1], head, blocks)
    unit, inverse = normalize(full[...].reshape(flat))
    incoming = normed_back[...]
    weighted = jnp.where(is_class, incoming * lead, incoming)
    sums_out[0:1] = jnp.sum(weighted * unit, axis=0, keepdims=True)
    sums_out[1:2] = jnp.sum(weighted, axis=0, keepdims=True)
    sums_out[3:] = jnp.zeros((sums_out.shape[0] - 3, width), FLOAT)
    change = normalize_back(incoming * gains[2], unit, inverse)
    change = jnp.where(is_real, change, 0.0)
    grad[...] += change.reshape(shaped)
    saved.append(wires.move(grad, grad_o))
    for copy, *_ in firsts:
        copy.wait_recv()

    def add_first(index, carry):
        for _, landing, name, lanes in firsts:
            for outer in range(2):
                place = (0, 0, outer) if HOPS[name][0] == "y" else (0, outer, 0)
                spot = place + (index, slice(None), lanes)
                whole[spot] = (
                    whole[spot].astype(FLOAT) + landing[outer, index].astype(FLOAT)
                ).astype(HALF)
        return carry

    lax.fori_loop(0, rest, add_first, 0)
    wires.finish()
    saved.append(wires.move(whole.at[0], whole_o.at[0]))
    for copy in saved:
        copy.wait()


class Reduce:
    def __init__(self, wires, data, lanes, landings, hops, out, across=2, begun=None):
        self.wires, self.data, self.lanes = wires, data, lanes
        self.landings, self.hops, self.out, self.begun = landings, hops, out, begun
        self.extent = [across, 2, 2, data.shape[3]]
        self.at, self.copy = 0, None

    @property
    def idle(self):
        return self.copy is None and self.at < len(self.hops)

    def launch(self):
        axis, peer = self.hops[self.at]
        places = [pl.ds(0, size) for size in self.extent]
        if axis is not None:
            half = self.extent[axis] // 2
            places[axis] = pl.ds(half, half)
            self.extent[axis] = half
        self.first = [0, 0]
        source = self.data
        if self.begun is not None and self.at == 0:
            source = self.begun
            if axis != 0:
                places[0] = pl.ds(1, 1)
                self.first = [1, 0]
        self.copy = self.wires.to(
            peer,
            source.at[tuple(places) + (slice(None), self.lanes)],
            self.landings[self.at],
        )

    def wait(self):
        self.copy.wait_recv()
        if self.hops[self.at][0] is None:
            self.wires.drain(self.copy)
        self.copy = None

    def land(self):
        self.wait()
        landing = self.landings[self.at]
        self.at += 1
        tail = (slice(None), self.lanes)
        if self.at == len(self.hops):
            self.out(
                self.data[(0, 0, 0, 0) + tail].astype(FLOAT)
                + landing[0, 0, 0, 0].astype(FLOAT)
            )
            return
        start = self.first[0]
        _, second, third, rest = self.extent
        for place in [
            (a, b, c)
            for a in range(start, self.extent[0])
            for b in range(second)
            for c in range(third)
        ]:

            def add(index, carry):
                spot = place + (index,) + tail
                landed = landing[place[0] - start, place[1], place[2], index]
                self.data[spot] = (
                    self.data[spot].astype(FLOAT) + landed.astype(FLOAT)
                ).astype(HALF)
                return carry

            lax.fori_loop(0, rest, add, 0)


class Mixer(Reduce):
    def __init__(self, wires, data, head, near, far, landings, hops, out):
        half = data.shape[5] // 2
        bit = lax.rem(head, 2)
        super().__init__(
            wires,
            data,
            pl.ds(pl.multiple_of(bit * half, PAIR), half),
            landings,
            [None] + hops + [(None, far), None],
            out,
            1,
        )
        self.near = near
        self.other = pl.ds(pl.multiple_of((1 - bit) * half, PAIR), half)

    def launch(self):
        if self.at == 0:
            source = self.data.at[:, :, :, :, :, self.other]
        elif self.at == len(self.hops) - 1:
            source = self.data.at[0, 0, 0, 0, :, self.lanes]
        else:
            super().launch()
            return
        self.copy = self.wires.to(self.near, source, self.landings[self.at])

    def land(self):
        if 0 < self.at < len(self.hops) - 1:
            super().land()
            return
        self.copy.wait_recv()
        self.copy = None
        landing = self.landings[self.at]
        self.at += 1
        if self.at == len(self.hops):
            self.out[:, self.lanes] = self.data[0, 0, 0, 0, :, self.lanes].astype(FLOAT)
            self.out[:, self.other] = landing[...].astype(FLOAT)
            return
        for place in [(0, a, b) for a in range(2) for b in range(2)]:

            def add(index, carry):
                spot = place + (index, slice(None), self.lanes)
                self.data[spot] = (
                    self.data[spot].astype(FLOAT) + landing[place + (index,)].astype(FLOAT)
                ).astype(HALF)
                return carry

            lax.fori_loop(0, self.data.shape[3], add, 0)


class Vectors:
    def __init__(self, wires, sums, landing, peers, out):
        self.wires, self.sums, self.landing, self.peers, self.out = wires, sums, landing, peers, out
        self.at, self.copy = 0, None

    @property
    def idle(self):
        return self.copy is None and self.at < len(self.peers)

    def launch(self):
        self.copy = self.wires.to(
            self.peers[self.at], self.sums.at[self.at], self.landing.at[self.at]
        )

    def land(self):
        self.copy.wait_recv()
        self.copy = None
        total = self.sums[self.at] + self.landing[self.at]
        self.at += 1
        if self.at == len(self.peers):
            self.out(total)
        else:
            self.sums[self.at] = total


def backward_kernel(
    heads,
    cuts,
    tokens,
    class_token,
    gains,
    shifts,
    mlp_sums,
    hidden_sums,
    grad_in,
    bundles_in,
    projections,
    mixer_in,
    normed_in,
    qkv_in,
    time_soft_in,
    mixed_in,
    state_in,
    proj_in,
    space_normed_in,
    space_qkv_in,
    space_soft_in,
    spread_in,
    whole_in,
    patch_out,
    class_out,
    inputs_out,
    outputs_out,
    mixer_out,
    hidden_out,
    return_out,
    gains_out,
    shifts_out,
    biases_out,
    input_bias_out,
    hidden_bias_out,
    grad,
    bundles,
    time_output,
    weight,
    normed,
    qkv,
    time_soft,
    mixed,
    state,
    proj,
    space_normed,
    space_qkv,
    space_soft,
    spread,
    joint,
    outer_grad,
    mixed_back,
    proj_back,
    time_back,
    near_landing,
    far_landing,
    class_parts,
    mlp,
    space,
    space_landing,
    time_data,
    mixer_data,
    vectors,
    vector_landing,
    *rest,
):
    send_sems, recv_sems, local_sems = rest[-3:]
    landings = list(rest[:-3])
    clip, head = lax.axis_index("clip"), lax.axis_index("head")
    frames, patches, width = tokens.shape
    all_frames, rows, _ = normed.shape
    blocks = all_frames // frames
    own_width = mixed.shape[2] // frames
    wide = qkv.shape[2] // 3
    flat = (frames * rows, width)
    shaped = (frames, rows, width)
    cut = width // cuts
    rest_size = mlp.shape[3]
    hidden = mlp.shape[5] // 2
    near, far = flip(head, 1), flip(head, 2)
    cross = flip(near, 2)
    near_peer, far_peer, cross_peer = (clip, near), (clip, far), (clip, cross)
    others = [near_peer, far_peer, cross_peer]
    clip_peers = []
    bit = 1
    while bit < cuts:
        clip_peers.append((flip(clip, bit), head))
        bit *= 2
    wires = Wires(send_sems, recv_sems, local_sems)
    order = [
        (grad_in, grad),
        (bundles_in.at[:, pl.ds(own_width, 4 * own_width)], bundles),
        (space_soft_in, space_soft),
        (space_qkv_in, space_qkv),
        (whole_in, mlp),
        (state_in, state),
        (mixer_in, weight),
        (space_normed_in, space_normed),
        (spread_in, spread),
        (proj_in, proj),
        (qkv_in, qkv),
        (time_soft_in, time_soft),
        (bundles_in.at[head, pl.ds(0, own_width)], time_output),
        (normed_in, normed),
        (mixed_in, mixed),
    ]
    ready = {id(dest): wires.move(source, dest) for source, dest in order}

    def need(*refs):
        for ref in refs:
            ready[id(ref)].wait()

    greet(others + clip_peers)
    clip_hops = [
        (3 if 1 << number < rest_size else None, peer)
        for number, peer in enumerate(clip_peers[2:])
    ]
    steps = {
        "x": [(0, far_peer)],
        "y": [(1, clip_peers[0])],
        "z": [(2, clip_peers[1])],
        "w": clip_hops,
    }
    chains = {}

    def take(name):
        hops = [hop for code in HOPS[name] for hop in steps[code]]
        return hops, [landings.pop(0) for _ in hops]

    def chain(name, data, lanes, out, across=2, begun=None):
        hops, mine = take(name)
        chains[name] = Reduce(wires, data, lanes, mine, hops, out, across, begun)

    def run(place):
        for event in SCHEDULE.get(place, ()):
            if event[-1] == "+":
                chains[event[:-1]].launch()
            else:
                chains[event[:-1]].land()

    def put_inputs(layer, first, second):
        def write(value):
            for number, kind in enumerate((first, second)):
                piece = value[:, number * own_width : (number + 1) * own_width]
                if kind == 3:
                    outputs_out[layer] = piece.T
                else:
                    inputs_out[layer, kind] = piece

        return write

    def put_hidden(start, count):
        def write(value):
            inner = max(0, min(count, hidden - start))
            if inner:
                hidden_out[:, start : start + inner] = value[:, :inner]
            if count > inner:
                first = start + inner - hidden
                return_out[:, first : first + count - inner] = value[:, inner:]

        return write

    middle = 2 * own_width
    left, right = pl.ds(0, middle), pl.ds(middle, middle)
    for name, (start, count) in column_groups(2 * hidden).items():
        chain(
            name,
            mlp,
            pl.ds(start, count),
            put_hidden(start, count),
            2,
            whole_in,
        )
    chain("S", space.at[0], left, put_inputs(1, 0, 1))
    chain("R", space.at[0], right, put_inputs(1, 2, 3))
    chain("T", time_data, left, put_inputs(0, 3, 0), 1)
    chain("U", time_data, right, put_inputs(0, 1, 2), 1)
    hops, mine = take("X")
    mine = [landings.pop(0)] + mine + [landings.pop(0), landings.pop(0)]
    chains["X"] = Mixer(wires, mixer_data, head, near_peer, far_peer, mine, hops, mixer_out)

    def put_vectors(total):
        part = width // (blocks * cuts)
        shared = pick(total[:10], (clip * blocks + head) * part, part)
        for place in range(3):
            gains_out[place] = shared[place : place + 1]
            shifts_out[place] = shared[3 + place : 4 + place]
        biases_out[...] = shared[6:10]
        other = pick(total[10:14], (head * cuts + clip) * part, part)
        input_bias_out[0] = other[0:2]
        input_bias_out[1] = other[2:4]
        chosen = rows_iota((blocks, 1)) == head
        row = jnp.sum(jnp.where(chosen, total[14 : 14 + blocks], 0.0), axis=0, keepdims=True)
        hidden_bias_out[...] = pick(row, clip * (hidden // cuts), hidden // cuts)

    chains["V"] = Vectors(
        wires, vectors, vector_landing, [near_peer, far_peer] + clip_peers, put_vectors
    )
    run("begin")

    need(grad)
    lead = (head == 0).astype(FLOAT)
    row = lax.rem(rows_iota((frames * rows, 1)), rows)
    is_patch = row < patches
    class_grad = grad[0, patches : patches + 1]
    values = grad[...].reshape(flat)
    sums = {}
    sums["bias2"] = (
        jnp.sum(jnp.where(is_patch, values, 0.0), axis=0, keepdims=True) + lead * class_grad
    )
    values = jnp.where(
        is_patch, values, jnp.where(row == patches, class_grad * (1.0 / all_frames), 0.0)
    )
    half = values.astype(HALF)
    outer_grad[...] = half.reshape(shaped)
    need(bundles)
    for place in range(blocks):
        joint[place * own_width : (place + 1) * own_width] = bundles[place, 3 * own_width :]
    mixed_back[...] = mm_t(outer_grad[...].reshape(flat), joint[...]).astype(HALF).reshape(shaped)

    need(space_soft, space_qkv)
    masks = half_masks()

    def one_frame(frame, carry):
        pairs = width // PAIR
        for group in range(2):
            chosen = range(group * pairs // 2, (group + 1) * pairs // 2)
            backs, mines = [], []
            for pair in chosen:
                spot = slice(pair * PAIR, (pair + 1) * PAIR)
                value = space_qkv[2, frame, :, spot]
                for side in range(2):
                    mine = mixed_back[frame, :, spot] * masks[side]
                    mines.append(mine)
                    backs.append(mm_t(value, mine))
            scores = []
            for number, pair in enumerate(chosen):
                for side in range(2):
                    soft = space_soft[frame, 2 * pair + side].astype(FLOAT)
                    product = soft * backs[2 * number + side]
                    score = product - soft * jnp.sum(product, axis=0, keepdims=True)
                    scores.append(score.astype(HALF))
            for number, pair in enumerate(chosen):
                spot = slice(pair * PAIR, (pair + 1) * PAIR)
                query, key = space_qkv[0, frame, :, spot], space_qkv[1, frame, :, spot]
                left, right = scores[2 * number], scores[2 * number + 1]
                value_back = mm(space_soft[frame, 2 * pair], mines[2 * number]) + mm(
                    space_soft[frame, 2 * pair + 1], mines[2 * number + 1]
                )
                key_back = mm(left, query * masks[0]) + mm(right, query * masks[1])
                query_back = t_mm(left, key * masks[0]) + t_mm(right, key * masks[1])
                space_qkv[0, frame, :, spot] = (query_back * (HEAD_DIM**-0.5)).astype(HALF)
                space_qkv[1, frame, :, spot] = key_back.astype(HALF)
                space_qkv[2, frame, :, spot] = value_back.astype(HALF)
        return carry

    lax.fori_loop(0, frames, one_frame, 0)
    incoming = jnp.zeros(flat, FLOAT)
    for kind in range(3):
        for place in range(blocks):
            joint[place * own_width : (place + 1) * own_width] = bundles[
                place, kind * own_width : (1 + kind) * own_width
            ]
        piece = space_qkv[kind].reshape(flat)
        incoming = incoming + mm(piece, joint[...])
        if kind != 1:
            sums["space%d" % kind] = jnp.sum(piece.astype(FLOAT), axis=0, keepdims=True)
    need(state)
    unit, inverse = normalize(state[...].reshape(flat))
    sums["gain1"] = jnp.sum(incoming * unit, axis=0, keepdims=True)
    sums["shift1"] = jnp.sum(incoming, axis=0, keepdims=True)
    by_frame = incoming.reshape(shaped)
    part = by_frame[0, patches : patches + 1]
    for frame in range(1, frames):
        part = part + by_frame[frame, patches : patches + 1]
    class_parts[head] = part
    class_state_grad = class_grad
    change = normalize_back(incoming * gains[1], unit, inverse)
    result = jnp.where(is_patch, grad[...].reshape(flat) + change, 0.0)
    grad[...] = result.reshape(shaped)
    need(mlp)
    run("b")
    sums["bias1"] = jnp.sum(result, axis=0, keepdims=True)
    half = result.astype(HALF)
    time_grad = mixed_back
    time_grad[...] = half.reshape(shaped)
    need(weight)
    back = mm_t(time_grad[...].reshape(flat), weight[...]).astype(HALF)
    mine = pl.multiple_of(head * frames, frames)
    proj_back[pl.ds(mine, frames)] = back.reshape(shaped)
    far_copies = [
        wires.to(far_peer, proj_back.at[mine + frame], proj_back.at[mine + frame])
        for frame in range(frames)
    ]
    own_part = proj_back.at[pl.ds(mine, frames)]
    near_copy = wires.to(near_peer, own_part, own_part)
    class_copies = [
        wires.to(peer, class_parts.at[head], class_parts.at[head]) for peer in others
    ]
    sums["bias0"] = jnp.sum(back.astype(FLOAT), axis=0, keepdims=True)

    weight_copies = load_wide(wires, projections, weight, own_width)

    need(space_normed, spread, proj)

    def place_rows(part, result):
        return result[part * cut : (part + 1) * cut]

    def send_core(lanes):
        return wires.to(
            near_peer,
            space.at[1, :, :, :, :, :, lanes],
            space_landing.at[:, :, :, :, :, lanes],
        )

    core_copies = []
    turned = space_normed[...].reshape(flat).T
    for kind in range(4):
        if kind == 2:
            core_copies.append(send_core(left))
            run("sw")
        if kind == 3:
            turned = outer_grad[...].reshape(flat).T
            result = mm(turned, spread[...].reshape(flat)).astype(HALF)
        else:
            result = mm(turned, space_qkv[kind].reshape(flat)).astype(HALF)
        for block in range(blocks):
            relative = flip_all(head, block, blocks)
            core, across = lax.rem(relative, 2), lax.div(relative, 2)
            for part in range(cuts):
                space[
                    (core, across)
                    + spread_index(clip, part, cuts, rest_size, cut)
                    + (slice(kind * own_width, (kind + 1) * own_width),)
                ] = place_rows(part, result)[:, block * own_width : (block + 1) * own_width]
    core_copies.append(send_core(right))
    turned = proj[...].reshape(flat).T
    result = mm(turned, time_grad[...].reshape(flat)).astype(HALF)
    for part in range(cuts):
        mixer_data[(0,) + spread_index(clip, part, cuts, rest_size, cut)] = place_rows(part, result)
    run("X")
    run("x1")

    need(qkv, time_soft, time_output)
    for copy in weight_copies:
        copy.wait()

    def outer(block):
        start = pl.multiple_of(block * frames, frames)
        back = mm_t(proj_back[pl.ds(start, frames)].reshape(flat), time_output[...])
        back = back.astype(HALF)
        gap = jnp.zeros((frames * rows, wide - own_width), HALF)
        time_back[pl.ds(start, frames)] = jnp.concatenate([back, gap], axis=1).reshape(
            frames, rows, wide
        )

    outer(head)
    near_copy.wait_recv()
    outer(near)
    run("x2")

    def add_core(lanes):
        for place in [(a, b, c) for a in range(2) for b in range(2) for c in range(2)]:

            def add(index, carry):
                spot = place + (index, slice(None), lanes)
                space[(0,) + spot] = (
                    space[(0,) + spot].astype(FLOAT) + space_landing[spot].astype(FLOAT)
                ).astype(HALF)
                return carry

            lax.fori_loop(0, rest_size, add, 0)

    for number, lanes in enumerate((left, right)):
        run(("c1", "c2")[number])
        core_copies[number].wait_recv()
        add_core(lanes)
        run(("S", "R")[number])
    run("c3")
    passed = []
    for frame in range(frames):
        run(("ag0", "ag1")[min(frame, 1)])
        far_copies[frame].wait_recv()
        here = proj_back.at[far * frames + frame]
        passed.append(wires.to(near_peer, here, here))
    run("ag2")
    outer(far)
    for frame in range(frames):
        run(("p0", "p1")[min(frame, 1)])
        passed[frame].wait_recv()
    outer(cross)
    total_rows = all_frames * TILE
    groups = rows // TILE
    batch = 3

    def time_backward(chosen):
        work = []
        for group in chosen:
            spot = pl.ds(pl.multiple_of(group * TILE, TILE), TILE)
            piece = qkv[:, spot, :].reshape(total_rows, 3 * wide)
            outers = time_back[:, spot, :].reshape(total_rows, wide)
            backs, mines = [], []
            for number in range(heads):
                left = (number // 2) * PAIR
                own = outers[:, left : left + PAIR] * masks[number % 2]
                mines.append(own)
                backs.append(mm_t(piece[:, 2 * wide + left : 2 * wide + left + PAIR], own))
            work.append((group, spot, piece, mines, backs))
        for group, spot, piece, mines, backs in work:
            parts = [[], [], []]
            for pair in range(wide // PAIR):
                left = pair * PAIR
                query = piece[:, left : left + PAIR]
                key = piece[:, wide + left : wide + left + PAIR]
                found = None
                for side in range(2):
                    number = 2 * pair + side
                    if number >= heads:
                        continue
                    soft = time_soft[group, number]
                    large = soft.astype(FLOAT)
                    product = large * backs[number]
                    score = product - large * jnp.sum(product, axis=0, keepdims=True)
                    score = score.astype(HALF)
                    terms = [
                        t_mm(score, key * masks[side]),
                        mm(score, query * masks[side]),
                        mm(soft, mines[number]),
                    ]
                    found = terms if found is None else [x + y for x, y in zip(found, terms)]
                for kind, scale in enumerate((HEAD_DIM**-0.5, 1.0, 1.0)):
                    parts[kind].append((found[kind] * scale).astype(HALF))
            joined = jnp.concatenate(parts[0] + parts[1] + parts[2], axis=1)
            qkv[:, spot, :] = joined.reshape(all_frames, TILE, 3 * wide)

    def body(step, carry):
        time_backward([step * batch + i for i in range(batch)])
        return carry

    lax.fori_loop(0, groups // batch, body, 0)
    for group in range(groups // batch * batch, groups):
        time_backward([group])

    need(normed)
    run("at")
    norm_sums = [jnp.zeros((1, width), FLOAT), jnp.zeros((1, width), FLOAT)]
    bias_sums = jnp.zeros((1, 3 * wide), FLOAT)

    def inner(block):
        start = pl.multiple_of(block * frames, frames)
        piece = qkv[pl.ds(start, frames)].reshape(frames * rows, 3 * wide)
        result = mm(piece, weight[...])
        values = normed[pl.ds(start, frames)].reshape(flat).astype(FLOAT)
        norm_sums[0] = norm_sums[0] + jnp.sum(result * values, axis=0, keepdims=True)
        norm_sums[1] = norm_sums[1] + jnp.sum(result, axis=0, keepdims=True)
        return result, jnp.sum(piece.astype(FLOAT), axis=0, keepdims=True)

    result, more = inner(cross)
    bias_sums = bias_sums + more
    space_qkv[0] = result.astype(HALF).reshape(shaped)
    back_cross = wires.to(near_peer, space_qkv.at[0], near_landing.at[0])
    result, more = inner(far)
    bias_sums = bias_sums + more
    run("rc0")
    back_cross.wait_recv()
    result = result + near_landing[0].reshape(flat).astype(FLOAT)
    space_qkv[1] = result.astype(HALF).reshape(shaped)
    back_far = wires.to(far_peer, space_qkv.at[1], far_landing)
    result, more = inner(near)
    bias_sums = bias_sums + more
    space_qkv[2] = result.astype(HALF).reshape(shaped)
    back_near = wires.to(near_peer, space_qkv.at[2], near_landing.at[1])
    run("rn")
    result, more = inner(head)
    bias_sums = bias_sums + more
    outer_grad[...] = result.astype(HALF).reshape(shaped)

    sums["gain0"] = (norm_sums[0] - norm_sums[1] * shifts[0]) / gains[0]
    sums["shift0"] = norm_sums[1]
    lane = lanes_iota((1, width))
    here = (lane >= head * own_width) & (lane < (head + 1) * own_width)
    for kind in (0, 2):
        own = bias_sums[:, kind * wide : kind * wide + own_width]
        repeated = jnp.concatenate([own] * blocks, axis=1)
        sums["time%d" % kind] = jnp.where(here, repeated, 0.0)
    names = [
        sums["gain0"],
        sums["gain1"],
        mlp_sums[0:1],
        sums["shift0"],
        sums["shift1"],
        mlp_sums[1:2],
        sums["bias0"],
        sums["bias1"],
        sums["bias2"],
        mlp_sums[2:3],
        sums["time0"],
        sums["time2"],
        sums["space0"],
        sums["space2"],
    ]
    for number, value in enumerate(names):
        vectors[0, number : number + 1] = value
    vectors[0, len(names) : len(names) + blocks] = hidden_sums[...]
    vectors[0, len(names) + blocks :] = jnp.zeros(
        (vectors.shape[1] - len(names) - blocks, width), FLOAT
    )
    run("V")
    run("v")

    need(mixed)

    def over_blocks(left, right):
        total = None
        for block in range(blocks):
            spot = slice(block * frames, (block + 1) * frames)
            term = t_mm(left[spot].reshape(flat), right(block, spot))
            total = term if total is None else total + term
        return total

    def put_time(kind, result):
        result = result.astype(HALF)
        lanes = slice(kind * own_width, (kind + 1) * own_width)
        for part in range(cuts):
            time_data[(0,) + spread_index(clip, part, cuts, rest_size, cut) + (lanes,)] = (
                place_rows(part, result)
            )

    def columns(kind):
        first = kind * wide
        return lambda block, spot: qkv[spot, :, first : first + wide].reshape(
            frames * rows, wide
        )

    put_time(0, over_blocks(proj_back, lambda block, spot: by_rows(mixed[block], frames)))
    put_time(1, over_blocks(normed, columns(0))[:, :own_width])
    run("T")
    run("t1")
    put_time(2, over_blocks(normed, columns(1))[:, :own_width])
    run("t2")
    put_time(3, over_blocks(normed, columns(2))[:, :own_width])
    run("U")
    run("t3")

    back_near.wait_recv()
    run("rx")
    back_far.wait_recv()
    for frame in range(frames):
        unit, inverse = normalize(tokens[frame].astype(FLOAT))
        incoming = (
            outer_grad[frame, :patches].astype(FLOAT)
            + near_landing[1, frame, :patches].astype(FLOAT)
            + far_landing[frame, :patches].astype(FLOAT)
        )
        patch_out[frame] = grad[frame, :patches] + normalize_back(
            incoming * gains[0], unit, inverse
        )
    for copy in class_copies:
        copy.wait_recv()
    unit, inverse = normalize(class_token[...].astype(FLOAT))
    incoming = class_parts[0]
    for place in range(1, blocks):
        incoming = incoming + class_parts[place]
    result = class_state_grad + normalize_back(incoming * gains[1], unit, inverse)
    class_out[...] = own_lanes(result, head, blocks)

    run("fin")
    run("tail")
    while True:
        for item in chains.values():
            if item.idle:
                item.launch()
        live = [item for item in chains.values() if item.copy is not None]
        if not live:
            break
        for item in live:
            item.land()
    wires.finish()


VMEM = pl.BlockSpec(memory_space=pltpu.VMEM)
ANY = pl.BlockSpec(memory_space=pl.ANY)
WIRES = 96
LIMIT = 125 * 2**19


def shape(dims, kind=HALF):
    return jax.ShapeDtypeStruct(tuple(dims), kind)


def room(dims, kind=HALF):
    return pltpu.VMEM(tuple(dims), kind)


def landing_rooms(axes, start, rest, cut, columns, begun):
    extent = list(start) + [rest]
    found = []
    for axis in axes:
        if axis is not None:
            extent[axis] //= 2
        first = [1] if begun and not found else extent[:1]
        found.append(room(first + extent[1:] + [cut, columns]))
    return found


def on_device(
    patch_tokens,
    class_token,
    keep_mask,
    patch_grad,
    class_grad,
    norm_gain,
    norm_bias,
    input_weight,
    input_bias,
    output_weight,
    time_mixer,
    output_bias,
    hidden_weight,
    hidden_bias,
    return_weight,
):
    blocks = lax.axis_size("head")
    clips = lax.axis_size("clip")
    head_index = lax.axis_index("head")
    clip_index = lax.axis_index("clip")
    _, frames, patches, width = patch_tokens.shape
    all_frames = keep_mask.shape[1]
    own_width = input_weight.shape[-1]
    heads = own_width // HEAD_DIM
    all_heads = heads * blocks
    hidden = hidden_weight.shape[-1]
    rows = round_up(patches + 1, TILE)
    groups = rows // TILE
    group_rows = all_frames * TILE
    wide = round_up(own_width, PAIR)
    cut = width // clips
    dense = 1
    while cut * dense % TILE:
        dense *= 2
    block_rows = cut * dense
    rest = clips // (4 * dense)
    tokens = frames * rows
    biases = output_bias[0]
    patch_state = patch_tokens[0]

    projections = jnp.transpose(input_weight[0], (0, 2, 3, 1))
    gains = jnp.transpose(norm_gain, (1, 0, 2))
    shifts = jnp.transpose(norm_bias, (1, 0, 2))

    full = (frames, rows, width)
    everything = (all_frames, rows, width)
    qkv_dims = (all_frames, rows, 3 * wide)
    time_soft_dims = (groups, heads, group_rows, group_rows)
    mixed_dims = (blocks, rows, frames * own_width)
    space_soft_dims = (frames, all_heads, rows, rows)
    bundle_dims = (blocks, 5 * own_width, width)
    halves = (2, 2, 2, rest, block_rows, 2 * hidden)
    kept_outs = [
        shape(everything),
        shape(qkv_dims),
        shape(time_soft_dims),
        shape(mixed_dims),
        shape(full, FLOAT),
        shape(full),
        shape(full),
        shape((3,) + full),
        shape(space_soft_dims),
        shape(full),
        shape(bundle_dims),
        shape(full, FLOAT),
        shape(halves),
    ]
    direct_outs = [
        shape((frames, patches, width), FLOAT),
        shape((1, width // blocks), FLOAT),
        shape((8, width), FLOAT),
        shape((blocks, hidden), FLOAT),
    ]
    sems = [pltpu.SemaphoreType.DMA((WIRES,))] * 3
    (
        normed, qkv, time_soft, mixed, state, proj, space_normed, space_qkv, space_soft, spread,
        bundles, grads, whole, patch_out, class_out, mlp_sums, hidden_sums,
    ) = pl.pallas_call(
        functools.partial(forward_kernel, heads, clips),
        out_shape=kept_outs + direct_outs,
        in_specs=[VMEM] * 9 + [ANY] * 6,
        out_specs=[ANY] * len(kept_outs) + [VMEM] * len(direct_outs),
        scratch_shapes=[
            room(everything),
            room(qkv_dims),
            room(time_soft_dims),
            room(mixed_dims),
            room(mixed_dims),
            room(full, FLOAT),
            room(full),
            room(full),
            room((3,) + full),
            room(space_soft_dims),
            room(full),
            room((width, width)),
            room((frames, rows, rows), FLOAT),
            room(bundle_dims),
            room((blocks, width, hidden)),
            room((blocks, hidden, width)),
            room((blocks, 1, 4 * own_width + hidden), FLOAT),
            room((rows, all_frames), FLOAT),
            room((3 * wide, width)),
            room((width, width)),
            room((frames, patches, width)),
            room((blocks, 1, width), FLOAT),
            room(full, FLOAT),
            room(full, FLOAT),
            room((tokens, width)),
            room((tokens, width)),
            room((2, 2, rest, block_rows, tokens)),
            room((2, 2, rest, block_rows, tokens)),
            room((tokens, width), FLOAT),
            room((tokens, width), FLOAT),
            room(halves[1:]),
            room(halves),
            room(halves),
        ]
        + [
            room((2, rest, block_rows, count))
            for name, (_, count) in column_groups(2 * hidden).items()
            if HOPS[name][0] in "yz"
        ]
        + sems,
        cost_estimate=pl.CostEstimate(
            flops=int(30e9), bytes_accessed=int(40e6), transcendentals=0
        ),
        compiler_params=pltpu.CompilerParams(
            vmem_limit_bytes=LIMIT, collective_id=0, has_side_effects=True
        ),
        name="forward",
    )(
        patch_state,
        class_token,
        class_grad,
        keep_mask[0],
        input_bias[0],
        hidden_bias,
        gains,
        shifts,
        biases,
        patch_grad[0],
        projections,
        output_weight[0],
        time_mixer[0],
        hidden_weight[0],
        return_weight[0],
    )

    clip_bits = clips.bit_length() - 1
    later = [3 if 1 << number < rest else None for number in range(clip_bits - 2)]
    steps = {"x": [0], "y": [1], "z": [2], "w": later}
    vector_rows = round_up(14 + blocks, 8)
    vector_hops = 2 + clip_bits
    pieces = [
        (name, 2, count, HOPS[name][0] != "x")
        for name, (_, count) in column_groups(2 * hidden).items()
    ]
    middle = 2 * own_width
    pieces += [("S", 2, middle, False), ("R", 2, middle, False)]
    pieces += [("T", 1, middle, False), ("U", 1, middle, False)]
    landings = []
    for name, across, columns, begun in pieces:
        axes = [axis for code in HOPS[name] for axis in steps[code]]
        landings += landing_rooms(axes, (across, 2, 2), rest, block_rows, columns, begun)
    axes = [axis for code in HOPS["X"] for axis in steps[code]]
    half_width = width // 2
    landings += landing_rooms(axes, (1, 2, 2), rest, block_rows, half_width, False)
    landings.append(room((1, 2, 2, rest, block_rows, half_width)))
    landings.append(room((1, 1, 1, 1, block_rows, half_width)))
    landings.append(room((block_rows, half_width)))
    part = width // (clips * blocks)
    hidden_part = hidden // clips
    (
        patch_input_grad, class_input_grad, inputs_total, outputs_total, mixer_total,
        hidden_total, return_total, gain_grad, shift_grad, bias_grad, input_bias_grad,
        hidden_bias_grad,
    ) = pl.pallas_call(
        functools.partial(backward_kernel, heads, clips),
        out_shape=[
            shape((frames, patches, width), FLOAT),
            shape((1, width // blocks), FLOAT),
            shape((2, 3, block_rows, own_width), FLOAT),
            shape((2, own_width, block_rows), FLOAT),
            shape((block_rows, width), FLOAT),
            shape((block_rows, hidden), FLOAT),
            shape((block_rows, hidden), FLOAT),
            shape((3, 1, part), FLOAT),
            shape((3, 1, part), FLOAT),
            shape((4, part), FLOAT),
            shape((2, 2, part), FLOAT),
            shape((1, hidden_part), FLOAT),
        ],
        in_specs=[VMEM] * 6 + [ANY] * 15,
        out_specs=[VMEM] * 12,
        scratch_shapes=[
            room(full, FLOAT),
            room((blocks, 4 * own_width, width)),
            room((own_width, width)),
            room((width, width)),
            room(everything),
            room(qkv_dims),
            room(time_soft_dims),
            room(mixed_dims),
            room(full, FLOAT),
            room(full),
            room(full),
            room((3,) + full),
            room(space_soft_dims),
            room(full),
            room((width, width)),
            room(full),
            room(full),
            room(everything),
            room((all_frames, rows, wide)),
            room((2,) + full),
            room(full),
            room((blocks, 1, width), FLOAT),
            room(halves),
            room((2, 2, 2, 2, rest, block_rows, 4 * own_width)),
            room((2, 2, 2, rest, block_rows, 4 * own_width)),
            room((1, 2, 2, rest, block_rows, 4 * own_width)),
            room((1, 2, 2, rest, block_rows, width)),
            room((vector_hops, vector_rows, width), FLOAT),
            room((vector_hops, vector_rows, width), FLOAT),
        ]
        + landings
        + sems,
        cost_estimate=pl.CostEstimate(
            flops=int(20e9), bytes_accessed=int(40e6), transcendentals=0
        ),
        compiler_params=pltpu.CompilerParams(
            vmem_limit_bytes=LIMIT, collective_id=1, has_side_effects=True
        ),
        name="backward",
    )(
        patch_state,
        class_token,
        gains,
        shifts,
        mlp_sums,
        hidden_sums,
        grads,
        bundles,
        projections,
        time_mixer[0],
        normed,
        qkv,
        time_soft,
        mixed,
        state,
        proj,
        space_normed,
        space_qkv,
        space_soft,
        spread,
        whole,
    )

    if dense > 1:
        start = lax.div(clip_index, clips // dense) * cut
        inputs_total = lax.dynamic_slice_in_dim(inputs_total, start, cut, 2)
        outputs_total = lax.dynamic_slice_in_dim(outputs_total, start, cut, 2)
        mixer_total, hidden_total, return_total = [
            lax.dynamic_slice_in_dim(total, start, cut, 0)
            for total in (mixer_total, hidden_total, return_total)
        ]
    share = cut // blocks
    mixer_grad = lax.dynamic_slice_in_dim(mixer_total, head_index * share, share, 0)
    return (
        patch_out[None],
        class_out,
        patch_input_grad[None],
        class_input_grad,
        jnp.transpose(gain_grad, (1, 0, 2)),
        jnp.transpose(shift_grad, (1, 0, 2)),
        jnp.transpose(inputs_total, (0, 2, 1, 3))[None],
        input_bias_grad[None],
        outputs_total[None],
        mixer_grad[None],
        bias_grad[None],
        hidden_total[None],
        hidden_bias_grad,
        return_total.T[None],
    )


def solution(mesh):
    in_specs = (
        P("clip", "head", None, None),
        P("clip", None),
        P("clip", None, None),
        P("clip", "head", None, None),
        P("clip", None),
        P(),
        P(),
        P(None, None, None, None, "head"),
        P(None, None, None, "head"),
        P(None, None, "head", None),
        P(),
        P(),
        P(None, None, "head"),
        P(None, "head"),
        P(None, "head", None),
    )
    out_specs = (
        P("clip", "head", None, None),
        P("clip", "head"),
        P("clip", "head", None, None),
        P("clip", "head"),
        P(None, None, ("clip", "head")),
        P(None, None, ("clip", "head")),
        P(None, None, "clip", None, "head"),
        P(None, None, None, ("head", "clip")),
        P(None, None, "head", "clip"),
        P(None, ("clip", "head"), None),
        P(None, None, ("clip", "head")),
        P(None, "clip", "head"),
        P(None, ("head", "clip")),
        P(None, "head", "clip"),
    )
    return jax.shard_map(
        on_device, mesh=mesh, in_specs=in_specs, out_specs=out_specs, check_vma=False
    )
```

```python
import functools

import jax
import jax.numpy as jnp
from jax import lax
from jax.experimental import pallas as pl
from jax.experimental.pallas import tpu as pltpu
from jax.sharding import PartitionSpec as P

HEAD_DIM = 64
PAIR = 2 * HEAD_DIM
TILE = 16
EPSILON = 1e-06
MASKED = -1e30
FLOAT = jnp.float32
HALF = jnp.bfloat16
ROW_ROW = (((1,), (1,)), ((), ()))
COL_COL = (((0,), (0,)), ((), ()))
ROOT_HALF = 0.7071067811865476
ROOT_TWO_PI = 0.3989422804014327


HOPS = {
    "A": "yzxw",
    "B": "zxyw",
    "C": "xyzw",
    "S": "yzxw",
    "R": "zxyw",
    "T": "yzw",
    "U": "yzw",
    "X": "yzw",
}
SHARES = (4, 6, 2)
SCHEDULE = {
    "begin": (
        "A+", "B+", "C+",
    ),
    "sw": (
        "A-", "A+", "C-", "C+",
    ),
    "X": (
        "X+",
    ),
    "x1": (
        "B-",
    ),
    "S": (
        "S+",
    ),
    "c2": (
        "C-", "C+",
    ),
    "R": (
        "R+",
    ),
    "c3": (
        "X-", "X+",
    ),
    "ag0": (
        "A-",
    ),
    "ag2": (
        "B+", "A+",
    ),
    "p0": (
        "C-", "C+",
    ),
    "rc0": (
        "C-",
    ),
    "rn": (
        "A-", "A+", "X-", "X+",
    ),
    "V": (
        "V+",
    ),
    "T": (
        "T+",
    ),
    "t1": (
        "V-", "V+", "S-", "S+", "R-", "R+",
    ),
    "U": (
        "U+",
    ),
    "rx": (
        "X-", "X+", "A-", "V-", "V+", "T-", "T+", "B-", "B+", "V-", "V+", "X-", "X+", "S-",
        "S+", "U-", "U+", "V-", "V+", "T-", "T+", "R-", "R+", "B-", "B+", "X-", "X+", "U-",
        "U+", "X-", "S-", "S+", "R-", "R+",
    ),
    "tail": (
        "V-", "T-", "U-", "S-", "R-", "B-",
    ),
}
FORWARD = {
    "pre": ("O+", "P+", "Q+",),
    "after0": ("J+",),
    "afterto2": ("K+",),
    "f0": ("Os", "Ot", "Ps", "Qs", "On",),
    "f1": ("Pt", "Qt",),
    "c": ("Pn", "Qn",),
    "to": ("Js",),
    "e": ("Jt",),
    "i": ("Jn", "Ks",),
    "m2": ("Kt",),
    "cs0": ("Kn",),
}


def column_groups(total):
    found, start = {}, 0
    for name, share in zip("ABC", SHARES):
        count = total * share // sum(SHARES)
        if count:
            found[name] = (start, count)
        start += count
    return found


def round_up(value, unit):
    return -(-value // unit) * unit


def mm(left, right):
    return jnp.dot(left, right, preferred_element_type=FLOAT)


def mm_t(left, right):
    return lax.dot_general(left, right, ROW_ROW, preferred_element_type=FLOAT)


def t_mm(left, right):
    return lax.dot_general(left, right, COL_COL, preferred_element_type=FLOAT)


def normalize(values):
    average = jnp.mean(values, axis=-1, keepdims=True)
    centred = values - average
    spread = jnp.mean(centred * centred, axis=-1, keepdims=True)
    inverse = lax.rsqrt(spread + EPSILON)
    return centred * inverse, inverse


def normalize_back(scaled, unit, inverse):
    first = jnp.mean(scaled, axis=-1, keepdims=True)
    second = jnp.mean(scaled * unit, axis=-1, keepdims=True)
    return (scaled - first - unit * second) * inverse


def rows_iota(shape):
    return lax.broadcasted_iota(jnp.int32, shape, 0)


def lanes_iota(shape):
    return lax.broadcasted_iota(jnp.int32, shape, 1)


def half_masks():
    lanes = lanes_iota((1, PAIR))
    first = (lanes < HEAD_DIM).astype(HALF)
    return first, (1 - first).astype(HALF)


def softmax_columns(scores):
    top = jnp.max(scores, axis=0, keepdims=True)
    exponent = jnp.exp(scores - top)
    total = jnp.sum(exponent, axis=0, keepdims=True)
    return exponent * (1.0 / total)


def gelu_parts(values):
    size = jnp.abs(values)
    density = jnp.exp(-0.5 * values * values)
    step = 1.0 / (1.0 + (0.3275911 * ROOT_HALF) * size)
    tail = step * (
        0.5 * 0.254829592
        + step
        * (
            0.5 * -0.284496736
            + step * (0.5 * 1.421413741 + step * (0.5 * -1.453152027 + step * (0.5 * 1.061405429)))
        )
    )
    tail = tail * density
    return jnp.where(values < 0.0, tail, 1.0 - tail), density * ROOT_TWO_PI


def flip(value, mask):
    return value + mask - 2 * mask * lax.rem(lax.div(value, mask), 2)


def flip_all(value, number, size):
    total, bit = 0, 1
    while bit < size:
        mine = lax.rem(lax.div(value, bit), 2)
        total = total + bit * ((1 - mine) if number & bit else mine)
        bit *= 2
    return total


def spread_index(clip, part, cuts, rest, cut):
    bits = []
    bit = 1
    while bit < 4 * rest:
        mine = lax.rem(lax.div(clip, bit), 2)
        bits.append(1 - mine if part & bit else mine)
        bit *= 2
    inner = 0
    for value in bits[2:]:
        inner = 2 * inner + value
    outer = part // (4 * rest)
    return bits[0], bits[1], inner, pl.ds(outer * cut, cut)


class Wires:
    def __init__(self, send, recv, local):
        self.send, self.recv, self.local = send, recv, local
        self.sent, self.moved, self.done = [], [], []

    def to(self, peer, source, dest):
        slot = len(self.sent)
        copy = pltpu.make_async_remote_copy(
            src_ref=source,
            dst_ref=dest,
            send_sem=self.send.at[slot],
            recv_sem=self.recv.at[slot],
            device_id=peer,
            device_id_type=pl.DeviceIdType.MESH,
        )
        copy.start()
        self.sent.append(copy)
        return copy

    def drain(self, copy):
        copy.wait_send()
        self.done.append(copy)

    def finish(self):
        for copy in self.sent:
            if all(copy is not other for other in self.done):
                copy.wait_send()

    def move(self, source, dest):
        copy = pltpu.make_async_copy(source, dest, self.local.at[len(self.moved)])
        copy.start()
        self.moved.append(copy)
        return copy


def greet(peers):
    barrier = pltpu.get_barrier_semaphore()
    for peer in peers:
        pl.semaphore_signal(
            barrier, inc=1, device_id=peer, device_id_type=pl.DeviceIdType.MESH
        )
    pl.semaphore_wait(barrier, len(peers))


def by_rows(packed, frames):
    width = packed.shape[1] // frames
    return jnp.concatenate(
        [packed[:, frame * width : (frame + 1) * width] for frame in range(frames)], axis=0
    )


def own_lanes(row, head, blocks):
    part = row.shape[1] // blocks
    total = jnp.zeros((row.shape[0], part), FLOAT)
    for block in range(blocks):
        total = jnp.where(head == block, row[:, block * part : (block + 1) * part], total)
    return total


def pick(rows, first, count):
    lane = rows_iota((rows.shape[1], count))
    chosen = lane == lanes_iota((rows.shape[1], count)) + first
    return lax.dot_general(
        rows,
        chosen.astype(FLOAT),
        (((1,), (0,)), ((), ())),
        precision=lax.Precision.HIGHEST,
        preferred_element_type=FLOAT,
    )


def load_wide(wires, projections, dest, own_width):
    wide = dest.shape[0] // 3
    copies = []
    for kind in range(3):
        start = kind * wide
        copies.append(wires.move(projections.at[0, kind], dest.at[pl.ds(start, own_width)]))
        dest[start + own_width : start + wide] = jnp.zeros(
            (wide - own_width, dest.shape[1]), HALF
        )
    return copies


class Gather:
    def __init__(self, wires, peers, clip, head, sources, dest, first=0):
        self.wires, self.peers, self.dest, self.head, self.first = wires, peers, dest, head, first
        self.own, start = [], first
        for source in sources:
            count = source.shape[0]
            self.own.append(wires.move(source, dest.at[head, pl.ds(start, count)]))
            start += count
        self.rows = start - first
        self.piece = self.rows // 4
        self.half = round_up(self.piece // 2, TILE)
        self.mine = lax.rem(clip, 4)
        self.far = flip(head, 2)

    def settle(self):
        for copy in self.own:
            copy.wait()

    def spot(self, piece, first=0, count=None):
        start = pl.multiple_of(self.first + piece * self.piece + first, TILE)
        return pl.ds(start, self.piece if count is None else count)

    def begin(self):
        here = self.dest.at[self.head, self.spot(self.mine)]
        self.cross = self.wires.to(self.peers["far"], here, here)

    def begin_near(self):
        here = self.dest.at[self.head, pl.ds(self.first, self.rows)]
        self.near = self.wires.to(self.peers["near"], here, here)

    def share(self):
        self.cross.wait_recv()
        here = self.dest.at[self.far, self.spot(self.mine)]
        self.one = self.wires.to(self.peers["one"], here, here)
        self.two = self.wires.to(self.peers["two"], here, here)

    def share_again(self):
        self.two.wait_recv()
        here = self.dest.at[self.far, self.spot(flip(self.mine, 2), 0, self.half)]
        third = self.wires.to(self.peers["one"], here, here)
        self.one.wait_recv()
        here = self.dest.at[
            self.far, self.spot(flip(self.mine, 1), self.half, self.piece - self.half)
        ]
        self.rest = [third, self.wires.to(self.peers["two"], here, here)]

    def pass_on(self):
        for copy in self.rest:
            copy.wait_recv()
        here = self.dest.at[self.far, pl.ds(self.first, self.rows)]
        self.last = self.wires.to(self.peers["near"], here, here)

    def finish(self):
        self.near.wait_recv()
        self.last.wait_recv()


def time_groups(heads, groups, qkv, keep_t, weights_out, out, masks, same, equal):
    frames = qkv.shape[0]
    wide = qkv.shape[2] // 3
    total_rows = frames * TILE
    work = []
    for group in groups:
        spot = pl.ds(pl.multiple_of(group * TILE, TILE), TILE)
        piece = qkv[:, spot, :].reshape(total_rows, 3 * wide)
        kept = keep_t[spot, :]
        kept = jnp.concatenate(
            [jnp.broadcast_to(kept[:, f : f + 1], (TILE, total_rows)) for f in range(frames)],
            axis=0,
        )
        blocked = jnp.where(same & ((kept > 0.5) | equal), 0.0, MASKED)
        scores = []
        for head in range(heads):
            left = (head // 2) * PAIR
            query = piece[:, left : left + PAIR]
            key = piece[:, wide + left : wide + left + PAIR]
            scores.append(mm_t(key * masks[head % 2], query) + blocked)
        work.append((group, spot, piece, scores))
    softs = []
    for group, spot, piece, scores in work:
        found = [softmax_columns(s).astype(HALF) for s in scores]
        for head in range(heads):
            weights_out[group, head] = found[head]
        softs.append(found)
    for (group, spot, piece, _), found in zip(work, softs):
        results = []
        for pair in range(wide // PAIR):
            left = 2 * wide + pair * PAIR
            value = piece[:, left : left + PAIR]
            total = t_mm(found[2 * pair], value * masks[0])
            if 2 * pair + 1 < heads:
                total = total + t_mm(found[2 * pair + 1], value * masks[1])
            results.append(total.astype(HALF))
        joined = jnp.concatenate(results, axis=1)[:, : heads * HEAD_DIM]
        joined = joined.reshape(frames, TILE, heads * HEAD_DIM)
        local = frames // out.shape[0]
        for block in range(out.shape[0]):
            own = [joined[block * local + frame] for frame in range(local)]
            out[block, spot, :] = jnp.concatenate(own, axis=1)


def forward_kernel(
    heads,
    cuts,
    tokens_in,
    class_token,
    class_grad,
    keep,
    input_bias,
    hidden_bias,
    gains,
    shifts,
    biases,
    grads_in,
    projections,
    outputs_in,
    mixer_in,
    first_in,
    second_in,
    normed_o,
    qkv_o,
    time_soft_o,
    mixed_o,
    state_o,
    proj_o,
    space_normed_o,
    space_qkv_o,
    space_soft_o,
    spread_o,
    bundles_o,
    grad_o,
    whole_o,
    patch_out,
    class_out,
    sums_out,
    hidden_sums,
    normed,
    qkv,
    time_soft,
    mixed,
    mixed_here,
    state,
    proj,
    space_normed,
    space_qkv,
    space_soft,
    spread,
    joint,
    blocked,
    bundles,
    first,
    second,
    smalls,
    keep_t,
    time_weight,
    mixer,
    grads,
    class_parts,
    grad,
    mlp_normed,
    grads_half,
    normed_t,
    grads_t,
    total,
    normed_back,
    found,
    core_landing,
    whole,
    *rest_refs,
):
    send_sems, recv_sems, local_sems = rest_refs[-3:]
    landings = list(rest_refs[:-3])
    clip, head = lax.axis_index("clip"), lax.axis_index("head")
    patches, frames, width = tokens_in.shape
    all_frames, rows, _ = normed.shape
    blocks = all_frames // frames
    own_width = mixed.shape[2] // frames
    wide = qkv.shape[2] // 3
    flat = (frames * rows, width)
    shaped = (frames, rows, width)
    rest, block_rows = normed_t.shape[2:4]
    cut = width // cuts
    hidden = first.shape[2]
    peers = {
        "near": (clip, flip(head, 1)),
        "far": (clip, flip(head, 2)),
        "cross": (clip, flip(flip(head, 1), 2)),
        "one": (flip(clip, 1), head),
        "two": (flip(clip, 2), head),
    }
    others = [peers["near"], peers["far"], peers["cross"]]
    wires = Wires(send_sems, recv_sems, local_sems)
    gathers = {
        "O": Gather(wires, peers, clip, head, [outputs_in.at[0]], bundles),
        "P": Gather(
            wires,
            peers,
            clip,
            head,
            [projections.at[1, 0], projections.at[1, 1]],
            bundles,
            own_width,
        ),
        "Q": Gather(
            wires,
            peers,
            clip,
            head,
            [projections.at[1, 2], outputs_in.at[1]],
            bundles,
            3 * own_width,
        ),
    }
    weight_copies = load_wide(wires, projections, time_weight, own_width)
    mixer_copy = wires.move(mixer_in, mixer)
    grads_copy = wires.move(grads_in, grads)
    gathers["J"] = Gather(wires, peers, clip, head, [first_in], first)
    gathers["K"] = Gather(wires, peers, clip, head, [second_in], second)

    def run(place):
        for event in FORWARD.get(place, ()):
            item = gathers[event[0]]
            steps = {"+": item.begin, "s": item.share, "t": item.share_again, "n": item.pass_on}
            steps[event[1]]()

    for number in range(4):
        smalls[head, :, number * own_width : (number + 1) * own_width] = input_bias[
            number // 2, number % 2 : number % 2 + 1
        ]
    smalls[head, :, 4 * own_width :] = hidden_bias[...]
    keep_t[:patches] = keep[...].astype(FLOAT).T
    keep_t[patches:] = jnp.zeros((rows - patches, all_frames), FLOAT)
    greet(list(peers.values()))

    for item in gathers.values():
        item.settle()
    run("pre")
    small_copies = [wires.to(peer, smalls.at[head], smalls.at[head]) for peer in others]

    tokens = jnp.swapaxes(tokens_in[...], 0, 1)
    mine = pl.multiple_of(head * frames, frames)
    for frame in range(frames):
        unit, _ = normalize(tokens[frame].astype(FLOAT))
        normed[mine + frame, :patches] = (unit * gains[0] + shifts[0]).astype(HALF)
        normed[mine + frame, patches:] = jnp.zeros((rows - patches, width), HALF)
    own_part = normed.at[pl.ds(mine, frames)]
    near_copy = wires.to(peers["near"], own_part, own_part)
    far_copies = [wires.to(peers["far"], normed.at[mine], normed.at[mine])]

    for copy in small_copies:
        copy.wait_recv()
    bias_row = smalls[head]
    bias_gap = jnp.zeros((1, wide - own_width), FLOAT)
    query_bias = jnp.concatenate([bias_row[:, :own_width], bias_gap], axis=1)
    value_bias = jnp.concatenate([bias_row[:, own_width : 2 * own_width], bias_gap], axis=1)
    for copy in weight_copies:
        copy.wait()

    def project(block):
        start = pl.multiple_of(block * frames, frames)
        raw = mm_t(normed[pl.ds(start, frames)].reshape(flat), time_weight[...])
        query = (raw[:, :wide] + query_bias).astype(HALF) * (HEAD_DIM**-0.5)
        value = (raw[:, 2 * wide :] + value_bias).astype(HALF)
        joined = jnp.concatenate(
            [query.astype(HALF), raw[:, wide : 2 * wide].astype(HALF), value], axis=1
        )
        qkv[pl.ds(start, frames)] = joined.reshape(frames, rows, 3 * wide)

    row = rows_iota((frames * rows, 1))
    lead = (head == 0).astype(FLOAT)
    is_class = row == patches
    is_real = (lax.rem(row, rows) < patches) | is_class
    keep_all = keep_t[...]

    def prepare_grads():
        grads_copy.wait()
        back_rows = jnp.swapaxes(grads[...], 0, 1)
        for frame in range(frames):
            chosen = lanes_iota(keep_all.shape) == mine + frame
            kept = jnp.sum(jnp.where(chosen, keep_all, 0.0), axis=1, keepdims=True)
            grad[frame, :patches] = back_rows[frame].astype(FLOAT) * kept[:patches]
            grad[frame, patches:] = jnp.zeros((rows - patches, width), FLOAT)
        grad[0, patches : patches + 1] = class_grad[...].astype(FLOAT)
        values = grad[...].reshape(flat)
        grads_half[...] = values.astype(HALF)
        turned = jnp.where(is_class, values * lead, values)
        sums_out[2:3] = jnp.sum(turned, axis=0, keepdims=True)
        turned = turned.astype(HALF).T
        for part in range(cuts):
            grads_t[spread_index(clip, part, cuts, rest, cut)] = turned[part * cut : (part + 1) * cut]

    project(head)
    near_copy.wait_recv()
    project(flip(head, 1))
    run("a")
    for frame in range(1, frames):
        here = normed.at[mine + frame]
        far_copies.append(wires.to(peers["far"], here, here))
    for name in "OPQ":
        gathers[name].begin_near()
    prepare_grads()
    far_start = pl.multiple_of(flip(head, 2) * frames, frames)
    passed = []
    for frame in range(frames):
        run("f%d" % min(frame, 1))
        far_copies[frame].wait_recv()
        here = normed.at[far_start + frame]
        passed.append(wires.to(peers["near"], here, here))
        run("after%d" % min(frame, 1))
    project(flip(head, 2))
    run("p")
    for copy in passed:
        copy.wait_recv()
    project(flip(flip(head, 1), 2))
    run("b")
    saved = [wires.move(normed, normed_o), wires.move(qkv, qkv_o)]

    masks = half_masks()
    square = (all_frames * TILE,) * 2
    key_index, query_index = rows_iota(square), lanes_iota(square)
    same = lax.rem(key_index, TILE) == lax.rem(query_index, TILE)
    equal = key_index == query_index
    groups = rows // TILE
    batch = 3
    middle = (groups // batch) // 2

    def attend(start, stop):
        def body(step, carry):
            time_groups(
                heads,
                [step * batch + i for i in range(batch)],
                qkv,
                keep_t,
                time_soft,
                mixed,
                masks,
                same,
                equal,
            )
            return carry

        lax.fori_loop(start, stop, body, 0)

    def exchange(first_row, count):
        spot = pl.ds(first_row, count)
        copies = []
        for peer in others:
            copies.append(
                wires.to(peer, mixed.at[peer[1], spot], mixed_here.at[head, spot])
            )
        return copies

    cut_row = middle * batch * TILE
    attend(0, middle)
    exchanged = exchange(0, cut_row)
    run("c")
    attend(middle, groups // batch)
    for group in range(groups // batch * batch, groups):
        time_groups(heads, [group], qkv, keep_t, time_soft, mixed, masks, same, equal)
    exchanged = exchanged + exchange(cut_row, rows - cut_row)
    run("d")
    for name in "JK":
        gathers[name].begin_near()
    run("afterto")
    mixed_here[head] = mixed[head]
    saved = saved + [wires.move(time_soft, time_soft_o), wires.move(mixed, mixed_o)]
    key_index, query_index = rows_iota((rows, rows)), lanes_iota((rows, rows))
    for frame in range(frames):
        chosen = lanes_iota(keep_all.shape) == mine + frame
        kept = jnp.sum(jnp.where(chosen, keep_all, 0.0), axis=1, keepdims=True)
        allowed = (kept > 0.5) | (key_index == patches) | (key_index == query_index)
        blocked[frame] = jnp.where(allowed, 0.0, MASKED)
    mixer_copy.wait()
    run("to")
    for copy in exchanged:
        copy.wait_recv()
    run("afterto2")
    run("F1b!")
    gathers["O"].finish()
    sum_here = jnp.zeros(flat, FLOAT)
    for place in range(blocks):
        sum_here = sum_here + mm(
            by_rows(mixed_here[place], frames), bundles[place, :own_width]
        )
    half = (sum_here + biases[0:1, :]).astype(HALF)
    proj[...] = half.reshape(shaped)
    added = (mm(half, mixer[...]) + biases[1:2, :]).reshape(shaped)
    tokens = jnp.swapaxes(tokens_in[...], 0, 1)
    for frame in range(frames):
        state[frame, :patches] = tokens[frame].astype(FLOAT) + added[frame, :patches]
        state[frame, patches : patches + 1] = class_token[...].astype(FLOAT)
        state[frame, patches + 1 :] = jnp.zeros((rows - patches - 1, width), FLOAT)
    saved.append(wires.move(proj, proj_o))
    state_copy = wires.move(state, state_o)
    run("f1b")

    unit, _ = normalize(state[...].reshape(flat))
    real = lax.rem(row, rows) <= patches
    half = jnp.where(real, unit * gains[1] + shifts[1], 0.0).astype(HALF)
    space_normed[...] = half.reshape(shaped)
    run("e")
    run("q!")
    gathers["P"].finish()
    start_bias = 2 * own_width
    for kind in range(3):
        if kind == 2:
            run("f")
            run("v!")
            gathers["Q"].finish()
            saved.append(wires.move(bundles, bundles_o))
        for place in range(blocks):
            joint[place * own_width : (place + 1) * own_width] = bundles[
                place, (1 + kind) * own_width : (2 + kind) * own_width
            ]
        raw = mm_t(space_normed[...].reshape(flat), joint[...])
        if kind != 1:
            begin = start_bias + (kind // 2) * own_width
            bias = jnp.concatenate(
                [smalls[place][:, begin : begin + own_width] for place in range(blocks)], axis=1
            )
            raw = raw + bias
        raw = raw.astype(HALF)
        if kind == 0:
            raw = (raw * (HEAD_DIM**-0.5)).astype(HALF)
        space_qkv[kind] = raw.reshape(shaped)
    saved = saved + [wires.move(space_normed, space_normed_o), wires.move(space_qkv, space_qkv_o)]
    run("g")

    def one_frame(frame, carry):
        softs = []
        for pair in range(width // PAIR):
            spot = slice(pair * PAIR, (pair + 1) * PAIR)
            query, key = space_qkv[0, frame, :, spot], space_qkv[1, frame, :, spot]
            for side in range(2):
                scores = mm_t(key * masks[side], query) + blocked[frame]
                softs.append(softmax_columns(scores).astype(HALF))
                space_soft[frame, 2 * pair + side] = softs[-1]
        for pair in range(width // PAIR):
            spot = slice(pair * PAIR, (pair + 1) * PAIR)
            value = space_qkv[2, frame, :, spot]
            result = t_mm(softs[2 * pair], value * masks[0]) + t_mm(
                softs[2 * pair + 1], value * masks[1]
            )
            spread[frame, :, spot] = result.astype(HALF)
        return carry

    lax.fori_loop(0, frames, one_frame, 0)
    run("h")
    run("i")
    saved = saved + [wires.move(space_soft, space_soft_o), wires.move(spread, spread_o)]
    for place in range(blocks):
        joint[place * own_width : (place + 1) * own_width] = bundles[place, 4 * own_width :]
    added = mm(spread[...].reshape(flat), joint[...]).reshape(shaped)
    part = added[0, patches : patches + 1]
    for frame in range(1, frames):
        part = part + added[frame, patches : patches + 1]
    class_parts[head] = part * (1.0 / all_frames)
    class_copies = [
        wires.to(peer, class_parts.at[head], class_parts.at[head]) for peer in others
    ]
    state_copy.wait()
    full = state
    full[...] = state[...] + added + biases[2:3, :]
    run("cl")

    for copy in class_copies:
        copy.wait_recv()
    class_state = class_token[...].astype(FLOAT) + biases[2:3, :]
    for place in range(blocks):
        class_state = class_state + class_parts[place]
    full[0, patches : patches + 1] = class_state
    unit, _ = normalize(full[...].reshape(flat))
    values = jnp.where(is_real, unit * gains[2] + shifts[2], 0.0)
    mlp_normed[...] = values.astype(HALF)
    turned = jnp.where(is_class, values * lead, values).astype(HALF).T
    for part in range(cuts):
        normed_t[spread_index(clip, part, cuts, rest, cut)] = turned[part * cut : (part + 1) * cut]
    class_row = jnp.where(is_class, lead, 1.0)
    run("m0")
    sends, firsts = [], []
    half_lanes = [pl.ds(0, hidden), pl.ds(hidden, hidden)]
    for number, block in enumerate((1, 0, 3, 2)):
        place = flip_all(head, block, blocks)
        if number == 0:
            gathers["J"].near.wait_recv()
            gathers["K"].near.wait_recv()
        if number == 2:
            run("m4")
            run("W1!")
            gathers["J"].last.wait_recv()
            run("W2!")
            gathers["K"].last.wait_recv()
        inner = mm(mlp_normed[...], first[place]) + smalls[place][:, 4 * own_width :]
        outer = mm_t(grads_half[...], second[place])
        chance, density = gelu_parts(inner)
        active = (inner * chance).astype(HALF)
        back = (outer * (chance + inner * density)).astype(HALF)
        hidden_sums[pl.ds(place, 1)] = jnp.sum(
            back.astype(FLOAT) * class_row, axis=0, keepdims=True
        )
        if number < 2:
            run(("m1", "m3")[number])
        forward = mm(active, second[place])
        backward = mm_t(back, first[place])
        if number == 0:
            total[...] = forward
            normed_back[...] = backward
        else:
            total[...] += forward
            normed_back[...] += backward
        factors = [(normed_t, back), (grads_t, active)]
        across = number // 2
        if number % 2 == 0:
            for copy in sends:
                wires.drain(copy)
            sends = []
            for lanes, (turned, factor) in zip(half_lanes, factors):
                piece = mm(turned[...].reshape(width, frames * rows), factor)
                found[:, :, :, :, lanes] = piece.astype(HALF).reshape(
                    2, 2, rest, block_rows, hidden
                )
                sends.append(
                    wires.to(
                        peers["near"],
                        found.at[:, :, :, :, lanes],
                        core_landing.at[across, :, :, :, :, lanes],
                    )
                )
            if number == 0:
                run("m2")
            continue
        if number == 1:
            run("cs0")
        for copy, lanes, (turned, factor) in zip(sends, half_lanes, factors):
            piece = mm(turned[...].reshape(width, frames * rows), factor)
            copy.wait_recv()
            landed = core_landing[across, :, :, :, :, lanes].astype(FLOAT)
            whole[across, :, :, :, :, lanes] = (
                piece.reshape(2, 2, rest, block_rows, hidden) + landed
            ).astype(HALF)
        if across == 0:
            for name, (start, count) in column_groups(2 * hidden).items():
                lanes = pl.ds(start, count)
                landing = landings.pop(0) if HOPS[name][0] in "yz" else None
                if HOPS[name][0] == "y":
                    source, peer = whole.at[0, 1, :, :, :, lanes], peers["one"]
                elif HOPS[name][0] == "z":
                    source, peer = whole.at[0, :, 1, :, :, lanes], peers["two"]
                else:
                    continue
                firsts.append((wires.to(peer, source, landing), landing, name, lanes))
        else:
            saved.append(wires.move(whole.at[1], whole_o.at[1]))
    result = (full[...].reshape(flat) + total[...] + biases[3:4, :]).reshape(shaped)
    for frame in range(frames):
        chosen = lanes_iota(keep_all.shape) == mine + frame
        kept = jnp.sum(jnp.where(chosen, keep_all, 0.0), axis=1, keepdims=True)
        patch_out[frame] = result[frame, :patches] * kept[:patches]
    class_out[...] = own_lanes(result[0, patches : patches + 1], head, blocks)
    unit, inverse = normalize(full[...].reshape(flat))
    incoming = normed_back[...]
    weighted = jnp.where(is_class, incoming * lead, incoming)
    sums_out[0:1] = jnp.sum(weighted * unit, axis=0, keepdims=True)
    sums_out[1:2] = jnp.sum(weighted, axis=0, keepdims=True)
    sums_out[3:] = jnp.zeros((sums_out.shape[0] - 3, width), FLOAT)
    change = normalize_back(incoming * gains[2], unit, inverse)
    change = jnp.where(is_real, change, 0.0)
    grad[...] += change.reshape(shaped)
    saved.append(wires.move(grad, grad_o))
    for copy, *_ in firsts:
        copy.wait_recv()

    def add_first(index, carry):
        for _, landing, name, lanes in firsts:
            for outer in range(2):
                place = (0, 0, outer) if HOPS[name][0] == "y" else (0, outer, 0)
                spot = place + (index, slice(None), lanes)
                whole[spot] = (
                    whole[spot].astype(FLOAT) + landing[outer, index].astype(FLOAT)
                ).astype(HALF)
        return carry

    lax.fori_loop(0, rest, add_first, 0)
    wires.finish()
    saved.append(wires.move(whole.at[0], whole_o.at[0]))
    for copy in saved:
        copy.wait()


class Reduce:
    def __init__(self, wires, data, lanes, landings, hops, out, across=2, begun=None):
        self.wires, self.data, self.lanes = wires, data, lanes
        self.landings, self.hops, self.out, self.begun = landings, hops, out, begun
        self.extent = [across, 2, 2, data.shape[3]]
        self.at, self.copy = 0, None

    @property
    def idle(self):
        return self.copy is None and self.at < len(self.hops)

    def launch(self):
        axis, peer = self.hops[self.at]
        places = [pl.ds(0, size) for size in self.extent]
        if axis is not None:
            half = self.extent[axis] // 2
            places[axis] = pl.ds(half, half)
            self.extent[axis] = half
        self.first = [0, 0]
        source = self.data
        if self.begun is not None and self.at == 0:
            source = self.begun
            if axis != 0:
                places[0] = pl.ds(1, 1)
                self.first = [1, 0]
        self.copy = self.wires.to(
            peer,
            source.at[tuple(places) + (slice(None), self.lanes)],
            self.landings[self.at],
        )

    def wait(self):
        self.copy.wait_recv()
        if self.hops[self.at][0] is None:
            self.wires.drain(self.copy)
        self.copy = None

    def land(self):
        self.wait()
        landing = self.landings[self.at]
        self.at += 1
        tail = (slice(None), self.lanes)
        if self.at == len(self.hops):
            self.out(
                self.data[(0, 0, 0, 0) + tail].astype(FLOAT)
                + landing[0, 0, 0, 0].astype(FLOAT)
            )
            return
        start = self.first[0]
        _, second, third, rest = self.extent
        for place in [
            (a, b, c)
            for a in range(start, self.extent[0])
            for b in range(second)
            for c in range(third)
        ]:

            def add(index, carry):
                spot = place + (index,) + tail
                landed = landing[place[0] - start, place[1], place[2], index]
                self.data[spot] = (
                    self.data[spot].astype(FLOAT) + landed.astype(FLOAT)
                ).astype(HALF)
                return carry

            lax.fori_loop(0, rest, add, 0)


class Mixer(Reduce):
    def __init__(self, wires, data, head, near, far, landings, hops, out):
        half = data.shape[5] // 2
        bit = lax.rem(head, 2)
        super().__init__(
            wires,
            data,
            pl.ds(pl.multiple_of(bit * half, PAIR), half),
            landings,
            [None] + hops + [(None, far), None],
            out,
            1,
        )
        self.near = near
        self.other = pl.ds(pl.multiple_of((1 - bit) * half, PAIR), half)

    def launch(self):
        if self.at == 0:
            source = self.data.at[:, :, :, :, :, self.other]
        elif self.at == len(self.hops) - 1:
            source = self.data.at[0, 0, 0, 0, :, self.lanes]
        else:
            super().launch()
            return
        self.copy = self.wires.to(self.near, source, self.landings[self.at])

    def land(self):
        if 0 < self.at < len(self.hops) - 1:
            super().land()
            return
        self.copy.wait_recv()
        self.copy = None
        landing = self.landings[self.at]
        self.at += 1
        if self.at == len(self.hops):
            self.out[:, self.lanes] = self.data[0, 0, 0, 0, :, self.lanes].astype(FLOAT)
            self.out[:, self.other] = landing[...].astype(FLOAT)
            return
        for place in [(0, a, b) for a in range(2) for b in range(2)]:

            def add(index, carry):
                spot = place + (index, slice(None), self.lanes)
                self.data[spot] = (
                    self.data[spot].astype(FLOAT) + landing[place + (index,)].astype(FLOAT)
                ).astype(HALF)
                return carry

            lax.fori_loop(0, self.data.shape[3], add, 0)


class Vectors:
    def __init__(self, wires, sums, landing, peers, out):
        self.wires, self.sums, self.landing, self.peers, self.out = wires, sums, landing, peers, out
        self.at, self.copy = 0, None

    @property
    def idle(self):
        return self.copy is None and self.at < len(self.peers)

    def launch(self):
        self.copy = self.wires.to(
            self.peers[self.at], self.sums.at[self.at], self.landing.at[self.at]
        )

    def land(self):
        self.copy.wait_recv()
        self.copy = None
        total = self.sums[self.at] + self.landing[self.at]
        self.at += 1
        if self.at == len(self.peers):
            self.out(total)
        else:
            self.sums[self.at] = total


def backward_kernel(
    heads,
    cuts,
    tokens_in,
    class_token,
    gains,
    shifts,
    mlp_sums,
    hidden_sums,
    grad_in,
    bundles_in,
    projections,
    mixer_in,
    normed_in,
    qkv_in,
    time_soft_in,
    mixed_in,
    state_in,
    proj_in,
    space_normed_in,
    space_qkv_in,
    space_soft_in,
    spread_in,
    whole_in,
    patch_out,
    class_out,
    inputs_out,
    outputs_out,
    mixer_out,
    hidden_out,
    return_out,
    gains_out,
    shifts_out,
    biases_out,
    input_bias_out,
    hidden_bias_out,
    grad,
    bundles,
    time_output,
    weight,
    normed,
    qkv,
    time_soft,
    mixed,
    state,
    proj,
    space_normed,
    space_qkv,
    space_soft,
    spread,
    joint,
    outer_grad,
    mixed_back,
    proj_back,
    time_back,
    near_landing,
    far_landing,
    class_parts,
    mlp,
    space,
    space_landing,
    time_data,
    mixer_data,
    vectors,
    vector_landing,
    *rest,
):
    send_sems, recv_sems, local_sems = rest[-3:]
    landings = list(rest[:-3])
    clip, head = lax.axis_index("clip"), lax.axis_index("head")
    patches, frames, width = tokens_in.shape
    all_frames, rows, _ = normed.shape
    blocks = all_frames // frames
    own_width = mixed.shape[2] // frames
    wide = qkv.shape[2] // 3
    flat = (frames * rows, width)
    shaped = (frames, rows, width)
    cut = width // cuts
    rest_size = mlp.shape[3]
    hidden = mlp.shape[5] // 2
    near, far = flip(head, 1), flip(head, 2)
    cross = flip(near, 2)
    near_peer, far_peer, cross_peer = (clip, near), (clip, far), (clip, cross)
    others = [near_peer, far_peer, cross_peer]
    clip_peers = []
    bit = 1
    while bit < cuts:
        clip_peers.append((flip(clip, bit), head))
        bit *= 2
    wires = Wires(send_sems, recv_sems, local_sems)
    order = [
        (grad_in, grad),
        (bundles_in.at[:, pl.ds(own_width, 4 * own_width)], bundles),
        (space_soft_in, space_soft),
        (space_qkv_in, space_qkv),
        (state_in, state),
        (mixer_in, weight),
    ]
    order_later = [
        (whole_in, mlp),
        (space_normed_in, space_normed),
        (spread_in, spread),
        (proj_in, proj),
        (qkv_in, qkv),
        (time_soft_in, time_soft),
        (bundles_in.at[head, pl.ds(0, own_width)], time_output),
        (normed_in, normed),
        (mixed_in, mixed),
    ]
    ready = {id(dest): wires.move(source, dest) for source, dest in order}

    def need(*refs):
        for ref in refs:
            ready[id(ref)].wait()

    greet(others + clip_peers)
    clip_hops = [
        (3 if 1 << number < rest_size else None, peer)
        for number, peer in enumerate(clip_peers[2:])
    ]
    steps = {
        "x": [(0, far_peer)],
        "y": [(1, clip_peers[0])],
        "z": [(2, clip_peers[1])],
        "w": clip_hops,
    }
    chains = {}

    def take(name):
        hops = [hop for code in HOPS[name] for hop in steps[code]]
        return hops, [landings.pop(0) for _ in hops]

    def chain(name, data, lanes, out, across=2, begun=None):
        hops, mine = take(name)
        chains[name] = Reduce(wires, data, lanes, mine, hops, out, across, begun)

    def run(place):
        for event in SCHEDULE.get(place, ()):
            if event[-1] == "+":
                chains[event[:-1]].launch()
            else:
                chains[event[:-1]].land()

    def put_inputs(layer, first, second):
        def write(value):
            for number, kind in enumerate((first, second)):
                piece = value[:, number * own_width : (number + 1) * own_width]
                if kind == 3:
                    outputs_out[layer] = piece.T
                else:
                    inputs_out[layer, kind] = piece

        return write

    def put_hidden(start, count):
        def write(value):
            inner = max(0, min(count, hidden - start))
            if inner:
                hidden_out[:, start : start + inner] = value[:, :inner]
            if count > inner:
                first = start + inner - hidden
                return_out[:, first : first + count - inner] = value[:, inner:]

        return write

    middle = 2 * own_width
    left, right = pl.ds(0, middle), pl.ds(middle, middle)
    for name, (start, count) in column_groups(2 * hidden).items():
        chain(
            name,
            mlp,
            pl.ds(start, count),
            put_hidden(start, count),
            2,
            whole_in,
        )
    chain("S", space.at[0], left, put_inputs(1, 0, 1))
    chain("R", space.at[0], right, put_inputs(1, 2, 3))
    chain("T", time_data, left, put_inputs(0, 3, 0), 1)
    chain("U", time_data, right, put_inputs(0, 1, 2), 1)
    hops, mine = take("X")
    mine = [landings.pop(0)] + mine + [landings.pop(0), landings.pop(0)]
    chains["X"] = Mixer(wires, mixer_data, head, near_peer, far_peer, mine, hops, mixer_out)

    def put_vectors(total):
        part = width // (blocks * cuts)
        shared = pick(total[:10], (clip * blocks + head) * part, part)
        for place in range(3):
            gains_out[place] = shared[place : place + 1]
            shifts_out[place] = shared[3 + place : 4 + place]
        biases_out[...] = shared[6:10]
        other = pick(total[10:14], (head * cuts + clip) * part, part)
        input_bias_out[0] = other[0:2]
        input_bias_out[1] = other[2:4]
        chosen = rows_iota((blocks, 1)) == head
        row = jnp.sum(jnp.where(chosen, total[14 : 14 + blocks], 0.0), axis=0, keepdims=True)
        hidden_bias_out[...] = pick(row, clip * (hidden // cuts), hidden // cuts)

    chains["V"] = Vectors(
        wires, vectors, vector_landing, [near_peer, far_peer] + clip_peers, put_vectors
    )
    run("begin")

    need(grad)
    lead = (head == 0).astype(FLOAT)
    row = lax.rem(rows_iota((frames * rows, 1)), rows)
    is_patch = row < patches
    class_grad = grad[0, patches : patches + 1]
    values = grad[...].reshape(flat)
    sums = {}
    sums["bias2"] = (
        jnp.sum(jnp.where(is_patch, values, 0.0), axis=0, keepdims=True) + lead * class_grad
    )
    values = jnp.where(
        is_patch, values, jnp.where(row == patches, class_grad * (1.0 / all_frames), 0.0)
    )
    half = values.astype(HALF)
    outer_grad[...] = half.reshape(shaped)
    ready.update({id(dest): wires.move(source, dest) for source, dest in order_later})
    need(bundles)
    for place in range(blocks):
        joint[place * own_width : (place + 1) * own_width] = bundles[place, 3 * own_width :]
    mixed_back[...] = mm_t(outer_grad[...].reshape(flat), joint[...]).astype(HALF).reshape(shaped)

    need(space_soft, space_qkv)
    masks = half_masks()

    def one_frame(frame, carry):
        pairs = width // PAIR
        for group in range(2):
            chosen = range(group * pairs // 2, (group + 1) * pairs // 2)
            backs, mines = [], []
            for pair in chosen:
                spot = slice(pair * PAIR, (pair + 1) * PAIR)
                value = space_qkv[2, frame, :, spot]
                for side in range(2):
                    mine = mixed_back[frame, :, spot] * masks[side]
                    mines.append(mine)
                    backs.append(mm_t(value, mine))
            scores = []
            for number, pair in enumerate(chosen):
                for side in range(2):
                    soft = space_soft[frame, 2 * pair + side].astype(FLOAT)
                    product = soft * backs[2 * number + side]
                    score = product - soft * jnp.sum(product, axis=0, keepdims=True)
                    scores.append(score.astype(HALF))
            for number, pair in enumerate(chosen):
                spot = slice(pair * PAIR, (pair + 1) * PAIR)
                query, key = space_qkv[0, frame, :, spot], space_qkv[1, frame, :, spot]
                left, right = scores[2 * number], scores[2 * number + 1]
                value_back = mm(space_soft[frame, 2 * pair], mines[2 * number]) + mm(
                    space_soft[frame, 2 * pair + 1], mines[2 * number + 1]
                )
                key_back = mm(left, query * masks[0]) + mm(right, query * masks[1])
                query_back = t_mm(left, key * masks[0]) + t_mm(right, key * masks[1])
                space_qkv[0, frame, :, spot] = (query_back * (HEAD_DIM**-0.5)).astype(HALF)
                space_qkv[1, frame, :, spot] = key_back.astype(HALF)
                space_qkv[2, frame, :, spot] = value_back.astype(HALF)
        return carry

    lax.fori_loop(0, frames, one_frame, 0)
    incoming = jnp.zeros(flat, FLOAT)
    for kind in range(3):
        for place in range(blocks):
            joint[place * own_width : (place + 1) * own_width] = bundles[
                place, kind * own_width : (1 + kind) * own_width
            ]
        piece = space_qkv[kind].reshape(flat)
        incoming = incoming + mm(piece, joint[...])
        if kind != 1:
            sums["space%d" % kind] = jnp.sum(piece.astype(FLOAT), axis=0, keepdims=True)
    need(state)
    unit, inverse = normalize(state[...].reshape(flat))
    sums["gain1"] = jnp.sum(incoming * unit, axis=0, keepdims=True)
    sums["shift1"] = jnp.sum(incoming, axis=0, keepdims=True)
    by_frame = incoming.reshape(shaped)
    part = by_frame[0, patches : patches + 1]
    for frame in range(1, frames):
        part = part + by_frame[frame, patches : patches + 1]
    class_parts[head] = part
    class_state_grad = class_grad
    change = normalize_back(incoming * gains[1], unit, inverse)
    result = jnp.where(is_patch, grad[...].reshape(flat) + change, 0.0)
    grad[...] = result.reshape(shaped)
    need(mlp)
    run("b")
    sums["bias1"] = jnp.sum(result, axis=0, keepdims=True)
    half = result.astype(HALF)
    time_grad = mixed_back
    time_grad[...] = half.reshape(shaped)
    need(weight)
    back = mm_t(time_grad[...].reshape(flat), weight[...]).astype(HALF)
    mine = pl.multiple_of(head * frames, frames)
    proj_back[pl.ds(mine, frames)] = back.reshape(shaped)
    far_copies = [
        wires.to(far_peer, proj_back.at[mine + frame], proj_back.at[mine + frame])
        for frame in range(frames)
    ]
    own_part = proj_back.at[pl.ds(mine, frames)]
    near_copy = wires.to(near_peer, own_part, own_part)
    class_copies = [
        wires.to(peer, class_parts.at[head], class_parts.at[head]) for peer in others
    ]
    sums["bias0"] = jnp.sum(back.astype(FLOAT), axis=0, keepdims=True)

    weight_copies = load_wide(wires, projections, weight, own_width)

    need(space_normed, spread, proj)

    def place_rows(part, result):
        return result[part * cut : (part + 1) * cut]

    def send_core(lanes):
        return wires.to(
            near_peer,
            space.at[1, :, :, :, :, :, lanes],
            space_landing.at[:, :, :, :, :, lanes],
        )

    core_copies = []
    turned = space_normed[...].reshape(flat).T
    for kind in range(4):
        if kind == 2:
            core_copies.append(send_core(left))
            run("sw")
        if kind == 3:
            turned = outer_grad[...].reshape(flat).T
            result = mm(turned, spread[...].reshape(flat)).astype(HALF)
        else:
            result = mm(turned, space_qkv[kind].reshape(flat)).astype(HALF)
        for block in range(blocks):
            relative = flip_all(head, block, blocks)
            core, across = lax.rem(relative, 2), lax.div(relative, 2)
            for part in range(cuts):
                space[
                    (core, across)
                    + spread_index(clip, part, cuts, rest_size, cut)
                    + (slice(kind * own_width, (kind + 1) * own_width),)
                ] = place_rows(part, result)[:, block * own_width : (block + 1) * own_width]
    core_copies.append(send_core(right))
    turned = proj[...].reshape(flat).T
    result = mm(turned, time_grad[...].reshape(flat)).astype(HALF)
    for part in range(cuts):
        mixer_data[(0,) + spread_index(clip, part, cuts, rest_size, cut)] = place_rows(part, result)
    run("X")
    run("x1")

    need(qkv, time_soft, time_output)
    for copy in weight_copies:
        copy.wait()

    def outer(block):
        start = pl.multiple_of(block * frames, frames)
        back = mm_t(proj_back[pl.ds(start, frames)].reshape(flat), time_output[...])
        back = back.astype(HALF)
        gap = jnp.zeros((frames * rows, wide - own_width), HALF)
        time_back[pl.ds(start, frames)] = jnp.concatenate([back, gap], axis=1).reshape(
            frames, rows, wide
        )

    outer(head)
    near_copy.wait_recv()
    outer(near)
    run("x2")

    def add_core(lanes):
        for place in [(a, b, c) for a in range(2) for b in range(2) for c in range(2)]:

            def add(index, carry):
                spot = place + (index, slice(None), lanes)
                space[(0,) + spot] = (
                    space[(0,) + spot].astype(FLOAT) + space_landing[spot].astype(FLOAT)
                ).astype(HALF)
                return carry

            lax.fori_loop(0, rest_size, add, 0)

    for number, lanes in enumerate((left, right)):
        run(("c1", "c2")[number])
        core_copies[number].wait_recv()
        add_core(lanes)
        run(("S", "R")[number])
    run("c3")
    passed = []
    for frame in range(frames):
        run(("ag0", "ag1")[min(frame, 1)])
        far_copies[frame].wait_recv()
        here = proj_back.at[far * frames + frame]
        passed.append(wires.to(near_peer, here, here))
    run("ag2")
    outer(far)
    for frame in range(frames):
        run(("p0", "p1")[min(frame, 1)])
        passed[frame].wait_recv()
    outer(cross)
    total_rows = all_frames * TILE
    groups = rows // TILE
    batch = 3

    def time_backward(chosen):
        work = []
        for group in chosen:
            spot = pl.ds(pl.multiple_of(group * TILE, TILE), TILE)
            piece = qkv[:, spot, :].reshape(total_rows, 3 * wide)
            outers = time_back[:, spot, :].reshape(total_rows, wide)
            backs, mines = [], []
            for number in range(heads):
                left = (number // 2) * PAIR
                own = outers[:, left : left + PAIR] * masks[number % 2]
                mines.append(own)
                backs.append(mm_t(piece[:, 2 * wide + left : 2 * wide + left + PAIR], own))
            work.append((group, spot, piece, mines, backs))
        for group, spot, piece, mines, backs in work:
            parts = [[], [], []]
            for pair in range(wide // PAIR):
                left = pair * PAIR
                query = piece[:, left : left + PAIR]
                key = piece[:, wide + left : wide + left + PAIR]
                found = None
                for side in range(2):
                    number = 2 * pair + side
                    if number >= heads:
                        continue
                    soft = time_soft[group, number]
                    large = soft.astype(FLOAT)
                    product = large * backs[number]
                    score = product - large * jnp.sum(product, axis=0, keepdims=True)
                    score = score.astype(HALF)
                    terms = [
                        t_mm(score, key * masks[side]),
                        mm(score, query * masks[side]),
                        mm(soft, mines[number]),
                    ]
                    found = terms if found is None else [x + y for x, y in zip(found, terms)]
                for kind, scale in enumerate((HEAD_DIM**-0.5, 1.0, 1.0)):
                    parts[kind].append((found[kind] * scale).astype(HALF))
            joined = jnp.concatenate(parts[0] + parts[1] + parts[2], axis=1)
            qkv[:, spot, :] = joined.reshape(all_frames, TILE, 3 * wide)

    def body(step, carry):
        time_backward([step * batch + i for i in range(batch)])
        return carry

    lax.fori_loop(0, groups // batch, body, 0)
    for group in range(groups // batch * batch, groups):
        time_backward([group])

    need(normed)
    run("at")
    norm_sums = [jnp.zeros((1, width), FLOAT), jnp.zeros((1, width), FLOAT)]
    bias_sums = jnp.zeros((1, 3 * wide), FLOAT)

    def inner(block):
        start = pl.multiple_of(block * frames, frames)
        piece = qkv[pl.ds(start, frames)].reshape(frames * rows, 3 * wide)
        result = mm(piece, weight[...])
        values = normed[pl.ds(start, frames)].reshape(flat).astype(FLOAT)
        norm_sums[0] = norm_sums[0] + jnp.sum(result * values, axis=0, keepdims=True)
        norm_sums[1] = norm_sums[1] + jnp.sum(result, axis=0, keepdims=True)
        return result, jnp.sum(piece.astype(FLOAT), axis=0, keepdims=True)

    result, more = inner(cross)
    bias_sums = bias_sums + more
    space_qkv[0] = result.astype(HALF).reshape(shaped)
    back_cross = wires.to(near_peer, space_qkv.at[0], near_landing.at[0])
    result, more = inner(far)
    bias_sums = bias_sums + more
    run("rc0")
    back_cross.wait_recv()
    result = result + near_landing[0].reshape(flat).astype(FLOAT)
    space_qkv[1] = result.astype(HALF).reshape(shaped)
    back_far = wires.to(far_peer, space_qkv.at[1], far_landing)
    result, more = inner(near)
    bias_sums = bias_sums + more
    space_qkv[2] = result.astype(HALF).reshape(shaped)
    back_near = wires.to(near_peer, space_qkv.at[2], near_landing.at[1])
    run("rn")
    result, more = inner(head)
    bias_sums = bias_sums + more
    outer_grad[...] = result.astype(HALF).reshape(shaped)

    sums["gain0"] = (norm_sums[0] - norm_sums[1] * shifts[0]) / gains[0]
    sums["shift0"] = norm_sums[1]
    lane = lanes_iota((1, width))
    here = (lane >= head * own_width) & (lane < (head + 1) * own_width)
    for kind in (0, 2):
        own = bias_sums[:, kind * wide : kind * wide + own_width]
        repeated = jnp.concatenate([own] * blocks, axis=1)
        sums["time%d" % kind] = jnp.where(here, repeated, 0.0)
    names = [
        sums["gain0"],
        sums["gain1"],
        mlp_sums[0:1],
        sums["shift0"],
        sums["shift1"],
        mlp_sums[1:2],
        sums["bias0"],
        sums["bias1"],
        sums["bias2"],
        mlp_sums[2:3],
        sums["time0"],
        sums["time2"],
        sums["space0"],
        sums["space2"],
    ]
    for number, value in enumerate(names):
        vectors[0, number : number + 1] = value
    vectors[0, len(names) : len(names) + blocks] = hidden_sums[...]
    vectors[0, len(names) + blocks :] = jnp.zeros(
        (vectors.shape[1] - len(names) - blocks, width), FLOAT
    )
    run("V")
    run("v")

    need(mixed)

    def over_blocks(left, right):
        total = None
        for block in range(blocks):
            spot = slice(block * frames, (block + 1) * frames)
            term = t_mm(left[spot].reshape(flat), right(block, spot))
            total = term if total is None else total + term
        return total

    def put_time(kind, result):
        result = result.astype(HALF)
        lanes = slice(kind * own_width, (kind + 1) * own_width)
        for part in range(cuts):
            time_data[(0,) + spread_index(clip, part, cuts, rest_size, cut) + (lanes,)] = (
                place_rows(part, result)
            )

    def columns(kind):
        first = kind * wide
        return lambda block, spot: qkv[spot, :, first : first + wide].reshape(
            frames * rows, wide
        )

    put_time(0, over_blocks(proj_back, lambda block, spot: by_rows(mixed[block], frames)))
    put_time(1, over_blocks(normed, columns(0))[:, :own_width])
    run("T")
    run("t1")
    put_time(2, over_blocks(normed, columns(1))[:, :own_width])
    run("t2")
    put_time(3, over_blocks(normed, columns(2))[:, :own_width])
    run("U")
    run("t3")

    tokens = jnp.swapaxes(tokens_in[...], 0, 1)
    back_near.wait_recv()
    run("rx")
    back_far.wait_recv()
    for frame in range(frames):
        unit, inverse = normalize(tokens[frame].astype(FLOAT))
        incoming = (
            outer_grad[frame, :patches].astype(FLOAT)
            + near_landing[1, frame, :patches].astype(FLOAT)
            + far_landing[frame, :patches].astype(FLOAT)
        )
        patch_out[frame] = grad[frame, :patches] + normalize_back(
            incoming * gains[0], unit, inverse
        )
    for copy in class_copies:
        copy.wait_recv()
    unit, inverse = normalize(class_token[...].astype(FLOAT))
    incoming = class_parts[0]
    for place in range(1, blocks):
        incoming = incoming + class_parts[place]
    result = class_state_grad + normalize_back(incoming * gains[1], unit, inverse)
    class_out[...] = own_lanes(result, head, blocks)

    run("fin")
    run("tail")
    while True:
        for item in chains.values():
            if item.idle:
                item.launch()
        live = [item for item in chains.values() if item.copy is not None]
        if not live:
            break
        for item in live:
            item.land()
    wires.finish()


def deliver_kernel(index, patch_first, patch_second, mixer, *refs):
    count = (len(refs) - 3) // 2
    first, second, mixer_out = refs[count : count + 3]
    first[...] = jnp.swapaxes(patch_first[...], 0, 1)
    second[...] = jnp.swapaxes(patch_second[...], 0, 1)
    share = mixer_out.shape[0]
    total = jnp.zeros(mixer_out.shape, FLOAT)
    head = index[0]
    for block in range(mixer.shape[0] // share):
        total = jnp.where(head == block, mixer[block * share : (block + 1) * share], total)
    mixer_out[...] = total
    for source, dest in zip(refs[:count], refs[count + 3 :]):
        dest[...] = source[...]


VMEM = pl.BlockSpec(memory_space=pltpu.VMEM)
ANY = pl.BlockSpec(memory_space=pl.ANY)
WIRES = 96
LIMIT = 125 * 2**19


def shape(dims, kind=HALF):
    return jax.ShapeDtypeStruct(tuple(dims), kind)


def room(dims, kind=HALF):
    return pltpu.VMEM(tuple(dims), kind)


def landing_rooms(axes, start, rest, cut, columns, begun):
    extent = list(start) + [rest]
    found = []
    for axis in axes:
        if axis is not None:
            extent[axis] //= 2
        first = [1] if begun and not found else extent[:1]
        found.append(room(first + extent[1:] + [cut, columns]))
    return found


def on_device(
    patch_tokens,
    class_token,
    keep_mask,
    patch_grad,
    class_grad,
    norm_gain,
    norm_bias,
    input_weight,
    input_bias,
    output_weight,
    time_mixer,
    output_bias,
    hidden_weight,
    hidden_bias,
    return_weight,
):
    blocks = lax.axis_size("head")
    clips = lax.axis_size("clip")
    head_index = lax.axis_index("head")
    clip_index = lax.axis_index("clip")
    _, frames, patches, width = patch_tokens.shape
    all_frames = keep_mask.shape[1]
    own_width = input_weight.shape[-1]
    heads = own_width // HEAD_DIM
    all_heads = heads * blocks
    hidden = hidden_weight.shape[-1]
    rows = round_up(patches + 1, TILE)
    groups = rows // TILE
    group_rows = all_frames * TILE
    wide = round_up(own_width, PAIR)
    cut = width // clips
    dense = 1
    while cut * dense % TILE:
        dense *= 2
    block_rows = cut * dense
    rest = clips // (4 * dense)
    tokens = frames * rows
    biases = output_bias[0]
    patch_state = jnp.transpose(patch_tokens[0], (1, 0, 2))
    patch_back = jnp.transpose(patch_grad[0], (1, 0, 2))

    projections = jnp.transpose(input_weight[0], (0, 2, 3, 1))
    gains = jnp.transpose(norm_gain, (1, 0, 2))
    shifts = jnp.transpose(norm_bias, (1, 0, 2))

    full = (frames, rows, width)
    everything = (all_frames, rows, width)
    qkv_dims = (all_frames, rows, 3 * wide)
    time_soft_dims = (groups, heads, group_rows, group_rows)
    mixed_dims = (blocks, rows, frames * own_width)
    space_soft_dims = (frames, all_heads, rows, rows)
    bundle_dims = (blocks, 5 * own_width, width)
    halves = (2, 2, 2, rest, block_rows, 2 * hidden)
    kept_outs = [
        shape(everything),
        shape(qkv_dims),
        shape(time_soft_dims),
        shape(mixed_dims),
        shape(full, FLOAT),
        shape(full),
        shape(full),
        shape((3,) + full),
        shape(space_soft_dims),
        shape(full),
        shape(bundle_dims),
        shape(full, FLOAT),
        shape(halves),
    ]
    direct_outs = [
        shape((frames, patches, width), FLOAT),
        shape((1, width // blocks), FLOAT),
        shape((8, width), FLOAT),
        shape((blocks, hidden), FLOAT),
    ]
    sems = [pltpu.SemaphoreType.DMA((WIRES,))] * 3
    (
        normed, qkv, time_soft, mixed, state, proj, space_normed, space_qkv, space_soft, spread,
        bundles, grads, whole, patch_out, class_out, mlp_sums, hidden_sums,
    ) = pl.pallas_call(
        functools.partial(forward_kernel, heads, clips),
        out_shape=kept_outs + direct_outs,
        in_specs=[VMEM] * 9 + [ANY] * 6,
        out_specs=[ANY] * len(kept_outs) + [VMEM] * len(direct_outs),
        scratch_shapes=[
            room(everything),
            room(qkv_dims),
            room(time_soft_dims),
            room(mixed_dims),
            room(mixed_dims),
            room(full, FLOAT),
            room(full),
            room(full),
            room((3,) + full),
            room(space_soft_dims),
            room(full),
            room((width, width)),
            room((frames, rows, rows), FLOAT),
            room(bundle_dims),
            room((blocks, width, hidden)),
            room((blocks, hidden, width)),
            room((blocks, 1, 4 * own_width + hidden), FLOAT),
            room((rows, all_frames), FLOAT),
            room((3 * wide, width)),
            room((width, width)),
            room((patches, frames, width)),
            room((blocks, 1, width), FLOAT),
            room(full, FLOAT),
            room((tokens, width)),
            room((tokens, width)),
            room((2, 2, rest, block_rows, tokens)),
            room((2, 2, rest, block_rows, tokens)),
            room((tokens, width), FLOAT),
            room((tokens, width), FLOAT),
            room(halves[1:]),
            room(halves),
            room(halves),
        ]
        + [
            room((2, rest, block_rows, count))
            for name, (_, count) in column_groups(2 * hidden).items()
            if HOPS[name][0] in "yz"
        ]
        + sems,
        cost_estimate=pl.CostEstimate(
            flops=int(30e9), bytes_accessed=int(40e6), transcendentals=0
        ),
        compiler_params=pltpu.CompilerParams(
            vmem_limit_bytes=LIMIT, collective_id=0, has_side_effects=True
        ),
        name="forward",
    )(
        patch_state,
        class_token,
        class_grad,
        keep_mask[0],
        input_bias[0],
        hidden_bias,
        gains,
        shifts,
        biases,
        patch_back,
        projections,
        output_weight[0],
        time_mixer[0],
        hidden_weight[0],
        return_weight[0],
    )

    clip_bits = clips.bit_length() - 1
    later = [3 if 1 << number < rest else None for number in range(clip_bits - 2)]
    steps = {"x": [0], "y": [1], "z": [2], "w": later}
    vector_rows = round_up(14 + blocks, 8)
    vector_hops = 2 + clip_bits
    pieces = [
        (name, 2, count, HOPS[name][0] != "x")
        for name, (_, count) in column_groups(2 * hidden).items()
    ]
    middle = 2 * own_width
    pieces += [("S", 2, middle, False), ("R", 2, middle, False)]
    pieces += [("T", 1, middle, False), ("U", 1, middle, False)]
    landings = []
    for name, across, columns, begun in pieces:
        axes = [axis for code in HOPS[name] for axis in steps[code]]
        landings += landing_rooms(axes, (across, 2, 2), rest, block_rows, columns, begun)
    axes = [axis for code in HOPS["X"] for axis in steps[code]]
    half_width = width // 2
    landings += landing_rooms(axes, (1, 2, 2), rest, block_rows, half_width, False)
    landings.append(room((1, 2, 2, rest, block_rows, half_width)))
    landings.append(room((1, 1, 1, 1, block_rows, half_width)))
    landings.append(room((block_rows, half_width)))
    part = width // (clips * blocks)
    hidden_part = hidden // clips
    (
        patch_input_grad, class_input_grad, inputs_total, outputs_total, mixer_total,
        hidden_total, return_total, gain_grad, shift_grad, bias_grad, input_bias_grad,
        hidden_bias_grad,
    ) = pl.pallas_call(
        functools.partial(backward_kernel, heads, clips),
        out_shape=[
            shape((frames, patches, width), FLOAT),
            shape((1, width // blocks), FLOAT),
            shape((2, 3, block_rows, own_width), FLOAT),
            shape((2, own_width, block_rows), FLOAT),
            shape((block_rows, width), FLOAT),
            shape((block_rows, hidden), FLOAT),
            shape((block_rows, hidden), FLOAT),
            shape((3, 1, part), FLOAT),
            shape((3, 1, part), FLOAT),
            shape((4, part), FLOAT),
            shape((2, 2, part), FLOAT),
            shape((1, hidden_part), FLOAT),
        ],
        in_specs=[VMEM] * 6 + [ANY] * 15,
        out_specs=[VMEM] * 12,
        scratch_shapes=[
            room(full, FLOAT),
            room((blocks, 4 * own_width, width)),
            room((own_width, width)),
            room((width, width)),
            room(everything),
            room(qkv_dims),
            room(time_soft_dims),
            room(mixed_dims),
            room(full, FLOAT),
            room(full),
            room(full),
            room((3,) + full),
            room(space_soft_dims),
            room(full),
            room((width, width)),
            room(full),
            room(full),
            room(everything),
            room((all_frames, rows, wide)),
            room((2,) + full),
            room(full),
            room((blocks, 1, width), FLOAT),
            room(halves),
            room((2, 2, 2, 2, rest, block_rows, 4 * own_width)),
            room((2, 2, 2, rest, block_rows, 4 * own_width)),
            room((1, 2, 2, rest, block_rows, 4 * own_width)),
            room((1, 2, 2, rest, block_rows, width)),
            room((vector_hops, vector_rows, width), FLOAT),
            room((vector_hops, vector_rows, width), FLOAT),
        ]
        + landings
        + sems,
        cost_estimate=pl.CostEstimate(
            flops=int(20e9), bytes_accessed=int(40e6), transcendentals=0
        ),
        compiler_params=pltpu.CompilerParams(
            vmem_limit_bytes=LIMIT, collective_id=1, has_side_effects=True
        ),
        name="backward",
    )(
        patch_state,
        class_token,
        gains,
        shifts,
        mlp_sums,
        hidden_sums,
        grads,
        bundles,
        projections,
        time_mixer[0],
        normed,
        qkv,
        time_soft,
        mixed,
        state,
        proj,
        space_normed,
        space_qkv,
        space_soft,
        spread,
        whole,
    )

    if dense > 1:
        start = lax.div(clip_index, clips // dense) * cut
        inputs_total = lax.dynamic_slice_in_dim(inputs_total, start, cut, 2)
        outputs_total = lax.dynamic_slice_in_dim(outputs_total, start, cut, 2)
        mixer_total, hidden_total, return_total = [
            lax.dynamic_slice_in_dim(total, start, cut, 0)
            for total in (mixer_total, hidden_total, return_total)
        ]
    share = cut // blocks
    small = [
        class_out,
        class_input_grad,
        gain_grad,
        shift_grad,
        inputs_total,
        input_bias_grad,
        outputs_total,
        bias_grad,
        hidden_total,
        hidden_bias_grad,
        return_total,
    ]
    whole_patch = shape((patches, frames, width), FLOAT)
    (
        patch_out, patch_input_grad, mixer_grad, class_out, class_input_grad, gain_grad,
        shift_grad, inputs_total, input_bias_grad, outputs_total, bias_grad, hidden_total,
        hidden_bias_grad, return_total,
    ) = pl.pallas_call(
        deliver_kernel,
        out_shape=[whole_patch, whole_patch, shape((share, width), FLOAT)]
        + [shape(a.shape, FLOAT) for a in small],
        in_specs=[pl.BlockSpec(memory_space=pltpu.SMEM)] + [VMEM] * (3 + len(small)),
        out_specs=[VMEM] * (3 + len(small)),
        compiler_params=pltpu.CompilerParams(vmem_limit_bytes=LIMIT),
        name="deliver",
    )(head_index.astype(jnp.int32)[None], patch_out, patch_input_grad, mixer_total, *small)
    return (
        jnp.transpose(patch_out, (1, 0, 2))[None],
        class_out,
        jnp.transpose(patch_input_grad, (1, 0, 2))[None],
        class_input_grad,
        jnp.transpose(gain_grad, (1, 0, 2)),
        jnp.transpose(shift_grad, (1, 0, 2)),
        jnp.transpose(inputs_total, (0, 2, 1, 3))[None],
        input_bias_grad[None],
        outputs_total[None],
        mixer_grad[None],
        bias_grad[None],
        hidden_total[None],
        hidden_bias_grad,
        return_total.T[None],
    )


def solution(mesh):
    in_specs = (
        P("clip", "head", None, None),
        P("clip", None),
        P("clip", None, None),
        P("clip", "head", None, None),
        P("clip", None),
        P(),
        P(),
        P(None, None, None, None, "head"),
        P(None, None, None, "head"),
        P(None, None, "head", None),
        P(),
        P(),
        P(None, None, "head"),
        P(None, "head"),
        P(None, "head", None),
    )
    out_specs = (
        P("clip", "head", None, None),
        P("clip", "head"),
        P("clip", "head", None, None),
        P("clip", "head"),
        P(None, None, ("clip", "head")),
        P(None, None, ("clip", "head")),
        P(None, None, "clip", None, "head"),
        P(None, None, None, ("head", "clip")),
        P(None, None, "head", "clip"),
        P(None, ("clip", "head"), None),
        P(None, None, ("clip", "head")),
        P(None, "clip", "head"),
        P(None, ("head", "clip")),
        P(None, "head", "clip"),
    )
    return jax.shard_map(
        on_device, mesh=mesh, in_specs=in_specs, out_specs=out_specs, check_vma=False
    )
```

```python
import functools

import jax
import jax.numpy as jnp
from jax import lax
from jax.experimental import pallas as pl
from jax.experimental.pallas import tpu as pltpu
from jax.sharding import PartitionSpec as P

HEAD_DIM = 64
PAIR = 2 * HEAD_DIM
TILE = 16
EPSILON = 1e-06
MASKED = -1e30
FLOAT = jnp.float32
HALF = jnp.bfloat16
ROW_ROW = (((1,), (1,)), ((), ()))
COL_COL = (((0,), (0,)), ((), ()))
ROOT_HALF = 0.7071067811865476
ROOT_TWO_PI = 0.3989422804014327


HOPS = {
    "A": "yzxw",
    "B": "zxyw",
    "C": "xyzw",
    "S": "yzxw",
    "R": "zxyw",
    "T": "yzw",
    "U": "yzw",
    "X": "yzw",
}
SHARES = (5, 4, 3)
SCHEDULE = {
    "begin": ("A+", "B+", "C+",),
    "sw": ("A-", "A+", "C-", "C+",),
    "X": ("X+",),
    "x1": ("B-",),
    "S": ("S+",),
    "c2": ("C-", "C+",),
    "R": ("R+",),
    "c3": ("X-", "X+",),
    "ag0": ("A-",),
    "ag2": ("B+", "A+",),
    "p0": ("C-", "C+",),
    "rc0": ("C-",),
    "rn": ("A-", "A+", "X-", "X+",),
    "V": ("V+",),
    "T": ("T+",),
    "t1": ("V-", "V+", "S-", "S+", "R-", "R+",),
    "U": ("U+",),
    "rx": ("X-", "X+", "A-", "V-", "V+", "T-", "T+", "B-", "B+", "V-", "V+", "X-", "X+", "S-", "S+", "U-", "U+", "V-", "V+", "T-", "T+", "R-", "R+", "B-", "B+", "X-", "X+", "U-", "U+", "X-", "S-", "S+", "R-", "R+",),
    "tail": ("V-", "T-", "U-", "S-", "R-", "B-",),
}
FORWARD = {
    "pre": ("O+", "P+", "Q+",),
    "after0": ("J+",),
    "afterto2": ("K+",),
    "f0": ("Os", "Ot", "Ps", "Qs", "On",),
    "f1": ("Pt", "Qt",),
    "c": ("Pn", "Qn",),
    "to": ("Js",),
    "e": ("Jt",),
    "i": ("Jn", "Ks",),
    "m2": ("Kt",),
    "cs0": ("Kn",),
}


def column_groups(total):
    found, start = {}, 0
    for name, share in zip("ABC", SHARES):
        count = total * share // sum(SHARES)
        if count:
            found[name] = (start, count)
        start += count
    return found


def round_up(value, unit):
    return -(-value // unit) * unit


def mm(left, right):
    return jnp.dot(left, right, preferred_element_type=FLOAT)


def mm_t(left, right):
    return lax.dot_general(left, right, ROW_ROW, preferred_element_type=FLOAT)


def t_mm(left, right):
    return lax.dot_general(left, right, COL_COL, preferred_element_type=FLOAT)


def normalize(values):
    average = jnp.mean(values, axis=-1, keepdims=True)
    centred = values - average
    spread = jnp.mean(centred * centred, axis=-1, keepdims=True)
    inverse = lax.rsqrt(spread + EPSILON)
    return centred * inverse, inverse


def normalize_back(scaled, unit, inverse):
    first = jnp.mean(scaled, axis=-1, keepdims=True)
    second = jnp.mean(scaled * unit, axis=-1, keepdims=True)
    return (scaled - first - unit * second) * inverse


def rows_iota(shape):
    return lax.broadcasted_iota(jnp.int32, shape, 0)


def lanes_iota(shape):
    return lax.broadcasted_iota(jnp.int32, shape, 1)


def half_masks():
    lanes = lanes_iota((1, PAIR))
    first = (lanes < HEAD_DIM).astype(HALF)
    return first, (1 - first).astype(HALF)


def softmax_columns(scores):
    top = jnp.max(scores, axis=0, keepdims=True)
    exponent = jnp.exp(scores - top)
    total = jnp.sum(exponent, axis=0, keepdims=True)
    return exponent * (1.0 / total)


def gelu_parts(values):
    size = jnp.abs(values)
    density = jnp.exp(-0.5 * values * values)
    step = 1.0 / (1.0 + (0.3275911 * ROOT_HALF) * size)
    tail = step * (
        0.5 * 0.254829592
        + step
        * (
            0.5 * -0.284496736
            + step * (0.5 * 1.421413741 + step * (0.5 * -1.453152027 + step * (0.5 * 1.061405429)))
        )
    )
    tail = tail * density
    return jnp.where(values < 0.0, tail, 1.0 - tail), density * ROOT_TWO_PI


def flip(value, mask):
    return value + mask - 2 * mask * lax.rem(lax.div(value, mask), 2)


def flip_all(value, number, size):
    total, bit = 0, 1
    while bit < size:
        mine = lax.rem(lax.div(value, bit), 2)
        total = total + bit * ((1 - mine) if number & bit else mine)
        bit *= 2
    return total


def spread_index(clip, part, cuts, rest, cut):
    bits = []
    bit = 1
    while bit < 4 * rest:
        mine = lax.rem(lax.div(clip, bit), 2)
        bits.append(1 - mine if part & bit else mine)
        bit *= 2
    inner = 0
    for value in bits[2:]:
        inner = 2 * inner + value
    outer = part // (4 * rest)
    return bits[0], bits[1], inner, pl.ds(outer * cut, cut)


class Wires:
    def __init__(self, send, recv, local):
        self.send, self.recv, self.local = send, recv, local
        self.sent, self.moved, self.done = [], [], []

    def to(self, peer, source, dest):
        slot = len(self.sent)
        copy = pltpu.make_async_remote_copy(
            src_ref=source,
            dst_ref=dest,
            send_sem=self.send.at[slot],
            recv_sem=self.recv.at[slot],
            device_id=peer,
            device_id_type=pl.DeviceIdType.MESH,
        )
        copy.start()
        self.sent.append(copy)
        return copy

    def drain(self, copy):
        copy.wait_send()
        self.done.append(copy)

    def finish(self):
        for copy in self.sent:
            if all(copy is not other for other in self.done):
                copy.wait_send()

    def move(self, source, dest):
        copy = pltpu.make_async_copy(source, dest, self.local.at[len(self.moved)])
        copy.start()
        self.moved.append(copy)
        return copy


def greet(peers):
    barrier = pltpu.get_barrier_semaphore()
    for peer in peers:
        pl.semaphore_signal(
            barrier, inc=1, device_id=peer, device_id_type=pl.DeviceIdType.MESH
        )
    pl.semaphore_wait(barrier, len(peers))


def by_rows(packed, frames):
    width = packed.shape[1] // frames
    return jnp.concatenate(
        [packed[:, frame * width : (frame + 1) * width] for frame in range(frames)], axis=0
    )


def own_lanes(row, head, blocks):
    part = row.shape[1] // blocks
    total = jnp.zeros((row.shape[0], part), FLOAT)
    for block in range(blocks):
        total = jnp.where(head == block, row[:, block * part : (block + 1) * part], total)
    return total


def pick(rows, first, count):
    lane = rows_iota((rows.shape[1], count))
    chosen = lane == lanes_iota((rows.shape[1], count)) + first
    return lax.dot_general(
        rows,
        chosen.astype(FLOAT),
        (((1,), (0,)), ((), ())),
        precision=lax.Precision.HIGHEST,
        preferred_element_type=FLOAT,
    )


def load_wide(wires, projections, dest, own_width):
    wide = dest.shape[0] // 3
    copies = []
    for kind in range(3):
        start = kind * wide
        copies.append(wires.move(projections.at[0, kind], dest.at[pl.ds(start, own_width)]))
        dest[start + own_width : start + wide] = jnp.zeros(
            (wide - own_width, dest.shape[1]), HALF
        )
    return copies


class Gather:
    def __init__(self, wires, peers, clip, head, sources, dest, first=0):
        self.wires, self.peers, self.dest, self.head, self.first = wires, peers, dest, head, first
        self.own, start = [], first
        for source in sources:
            count = source.shape[0]
            self.own.append(wires.move(source, dest.at[head, pl.ds(start, count)]))
            start += count
        self.rows = start - first
        self.piece = self.rows // 4
        self.half = round_up(self.piece // 2, TILE)
        self.mine = lax.rem(clip, 4)
        self.far = flip(head, 2)

    def settle(self):
        for copy in self.own:
            copy.wait()

    def spot(self, piece, first=0, count=None):
        start = pl.multiple_of(self.first + piece * self.piece + first, TILE)
        return pl.ds(start, self.piece if count is None else count)

    def begin(self):
        here = self.dest.at[self.head, self.spot(self.mine)]
        self.cross = self.wires.to(self.peers["far"], here, here)

    def begin_near(self):
        here = self.dest.at[self.head, pl.ds(self.first, self.rows)]
        self.near = self.wires.to(self.peers["near"], here, here)

    def share(self):
        self.cross.wait_recv()
        here = self.dest.at[self.far, self.spot(self.mine)]
        self.one = self.wires.to(self.peers["one"], here, here)
        self.two = self.wires.to(self.peers["two"], here, here)

    def share_again(self):
        self.two.wait_recv()
        here = self.dest.at[self.far, self.spot(flip(self.mine, 2), 0, self.half)]
        third = self.wires.to(self.peers["one"], here, here)
        self.one.wait_recv()
        here = self.dest.at[
            self.far, self.spot(flip(self.mine, 1), self.half, self.piece - self.half)
        ]
        self.rest = [third, self.wires.to(self.peers["two"], here, here)]

    def pass_on(self):
        for copy in self.rest:
            copy.wait_recv()
        here = self.dest.at[self.far, pl.ds(self.first, self.rows)]
        self.last = self.wires.to(self.peers["near"], here, here)

    def finish(self):
        self.near.wait_recv()
        self.last.wait_recv()


def time_groups(heads, groups, qkv, keep_t, weights_out, out, masks, same, equal):
    frames = qkv.shape[0]
    wide = qkv.shape[2] // 3
    total_rows = frames * TILE
    work = []
    for group in groups:
        spot = pl.ds(pl.multiple_of(group * TILE, TILE), TILE)
        piece = qkv[:, spot, :].reshape(total_rows, 3 * wide)
        kept = keep_t[spot, :]
        kept = jnp.concatenate(
            [jnp.broadcast_to(kept[:, f : f + 1], (TILE, total_rows)) for f in range(frames)],
            axis=0,
        )
        blocked = jnp.where(same & ((kept > 0.5) | equal), 0.0, MASKED)
        scores = []
        for head in range(heads):
            left = (head // 2) * PAIR
            query = piece[:, left : left + PAIR]
            key = piece[:, wide + left : wide + left + PAIR]
            scores.append(mm_t(key * masks[head % 2], query) + blocked)
        work.append((group, spot, piece, scores))
    softs = []
    for group, spot, piece, scores in work:
        found = [softmax_columns(s).astype(HALF) for s in scores]
        for head in range(heads):
            weights_out[group, head] = found[head]
        softs.append(found)
    for (group, spot, piece, _), found in zip(work, softs):
        results = []
        for pair in range(wide // PAIR):
            left = 2 * wide + pair * PAIR
            value = piece[:, left : left + PAIR]
            total = t_mm(found[2 * pair], value * masks[0])
            if 2 * pair + 1 < heads:
                total = total + t_mm(found[2 * pair + 1], value * masks[1])
            results.append(total.astype(HALF))
        joined = jnp.concatenate(results, axis=1)[:, : heads * HEAD_DIM]
        joined = joined.reshape(frames, TILE, heads * HEAD_DIM)
        local = frames // out.shape[0]
        for block in range(out.shape[0]):
            own = [joined[block * local + frame] for frame in range(local)]
            out[block, spot, :] = jnp.concatenate(own, axis=1)


def forward_kernel(
    heads,
    cuts,
    tokens_in,
    class_token,
    class_grad,
    keep,
    input_bias,
    hidden_bias,
    gains,
    shifts,
    biases,
    grads_in,
    projections,
    outputs_in,
    mixer_in,
    first_in,
    second_in,
    normed_o,
    qkv_o,
    time_soft_o,
    mixed_o,
    state_o,
    proj_o,
    space_normed_o,
    space_qkv_o,
    space_soft_o,
    spread_o,
    bundles_o,
    grad_o,
    whole_o,
    patch_out,
    class_out,
    sums_out,
    hidden_sums,
    normed,
    qkv,
    time_soft,
    mixed,
    mixed_here,
    state,
    proj,
    space_normed,
    space_qkv,
    space_soft,
    spread,
    joint,
    blocked,
    bundles,
    first,
    second,
    smalls,
    keep_t,
    time_weight,
    mixer,
    grads,
    class_parts,
    grad,
    mlp_normed,
    grads_half,
    normed_t,
    grads_t,
    total,
    normed_back,
    found,
    core_landing,
    whole,
    *rest_refs,
):
    send_sems, recv_sems, local_sems = rest_refs[-3:]
    landings = list(rest_refs[:-3])
    clip, head = lax.axis_index("clip"), lax.axis_index("head")
    patches, frames, width = tokens_in.shape
    all_frames, rows, _ = normed.shape
    blocks = all_frames // frames
    own_width = mixed.shape[2] // frames
    wide = qkv.shape[2] // 3
    flat = (frames * rows, width)
    shaped = (frames, rows, width)
    rest, block_rows = normed_t.shape[2:4]
    cut = width // cuts
    hidden = first.shape[2]
    peers = {
        "near": (clip, flip(head, 1)),
        "far": (clip, flip(head, 2)),
        "cross": (clip, flip(flip(head, 1), 2)),
        "one": (flip(clip, 1), head),
        "two": (flip(clip, 2), head),
    }
    others = [peers["near"], peers["far"], peers["cross"]]
    wires = Wires(send_sems, recv_sems, local_sems)
    gathers = {
        "O": Gather(wires, peers, clip, head, [outputs_in.at[0]], bundles),
        "P": Gather(
            wires,
            peers,
            clip,
            head,
            [projections.at[1, 0], projections.at[1, 1]],
            bundles,
            own_width,
        ),
        "Q": Gather(
            wires,
            peers,
            clip,
            head,
            [projections.at[1, 2], outputs_in.at[1]],
            bundles,
            3 * own_width,
        ),
    }
    weight_copies = load_wide(wires, projections, time_weight, own_width)
    mixer_copy = wires.move(mixer_in, mixer)
    grads_copy = wires.move(grads_in, grads)
    gathers["J"] = Gather(wires, peers, clip, head, [first_in], first)
    gathers["K"] = Gather(wires, peers, clip, head, [second_in], second)

    def run(place):
        for event in FORWARD.get(place, ()):
            item = gathers[event[0]]
            steps = {"+": item.begin, "s": item.share, "t": item.share_again, "n": item.pass_on}
            steps[event[1]]()

    for number in range(4):
        smalls[head, :, number * own_width : (number + 1) * own_width] = input_bias[
            number // 2, number % 2 : number % 2 + 1
        ]
    smalls[head, :, 4 * own_width :] = hidden_bias[...]
    keep_t[:patches] = keep[...].astype(FLOAT).T
    keep_t[patches:] = jnp.zeros((rows - patches, all_frames), FLOAT)
    greet(list(peers.values()))

    for item in gathers.values():
        item.settle()
    run("pre")
    small_copies = [wires.to(peer, smalls.at[head], smalls.at[head]) for peer in others]

    tokens = jnp.swapaxes(tokens_in[...], 0, 1)
    mine = pl.multiple_of(head * frames, frames)
    for frame in range(frames):
        unit, _ = normalize(tokens[frame].astype(FLOAT))
        normed[mine + frame, :patches] = (unit * gains[0] + shifts[0]).astype(HALF)
        normed[mine + frame, patches:] = jnp.zeros((rows - patches, width), HALF)
    own_part = normed.at[pl.ds(mine, frames)]
    near_copy = wires.to(peers["near"], own_part, own_part)
    far_copies = [wires.to(peers["far"], normed.at[mine], normed.at[mine])]

    for copy in small_copies:
        copy.wait_recv()
    bias_row = smalls[head]
    bias_gap = jnp.zeros((1, wide - own_width), FLOAT)
    query_bias = jnp.concatenate([bias_row[:, :own_width], bias_gap], axis=1)
    value_bias = jnp.concatenate([bias_row[:, own_width : 2 * own_width], bias_gap], axis=1)
    for copy in weight_copies:
        copy.wait()

    def project(block):
        start = pl.multiple_of(block * frames, frames)
        raw = mm_t(normed[pl.ds(start, frames)].reshape(flat), time_weight[...])
        query = (raw[:, :wide] + query_bias).astype(HALF) * (HEAD_DIM**-0.5)
        value = (raw[:, 2 * wide :] + value_bias).astype(HALF)
        joined = jnp.concatenate(
            [query.astype(HALF), raw[:, wide : 2 * wide].astype(HALF), value], axis=1
        )
        qkv[pl.ds(start, frames)] = joined.reshape(frames, rows, 3 * wide)

    row = rows_iota((frames * rows, 1))
    lead = (head == 0).astype(FLOAT)
    is_class = row == patches
    is_real = (lax.rem(row, rows) < patches) | is_class
    keep_all = keep_t[...]

    def prepare_grads():
        grads_copy.wait()
        back_rows = jnp.swapaxes(grads[...], 0, 1)
        for frame in range(frames):
            chosen = lanes_iota(keep_all.shape) == mine + frame
            kept = jnp.sum(jnp.where(chosen, keep_all, 0.0), axis=1, keepdims=True)
            grad[frame, :patches] = back_rows[frame].astype(FLOAT) * kept[:patches]
            grad[frame, patches:] = jnp.zeros((rows - patches, width), FLOAT)
        grad[0, patches : patches + 1] = class_grad[...].astype(FLOAT)
        values = grad[...].reshape(flat)
        grads_half[...] = values.astype(HALF)
        turned = jnp.where(is_class, values * lead, values)
        sums_out[2:3] = jnp.sum(turned, axis=0, keepdims=True)
        turned = turned.astype(HALF).T
        for part in range(cuts):
            grads_t[spread_index(clip, part, cuts, rest, cut)] = turned[part * cut : (part + 1) * cut]

    project(head)
    near_copy.wait_recv()
    project(flip(head, 1))
    run("a")
    for frame in range(1, frames):
        here = normed.at[mine + frame]
        far_copies.append(wires.to(peers["far"], here, here))
    for name in "OPQ":
        gathers[name].begin_near()
    prepare_grads()
    far_start = pl.multiple_of(flip(head, 2) * frames, frames)
    passed = []
    for frame in range(frames):
        run("f%d" % min(frame, 1))
        far_copies[frame].wait_recv()
        here = normed.at[far_start + frame]
        passed.append(wires.to(peers["near"], here, here))
        run("after%d" % min(frame, 1))
    project(flip(head, 2))
    run("p")
    for copy in passed:
        copy.wait_recv()
    project(flip(flip(head, 1), 2))
    run("b")
    saved = [wires.move(normed, normed_o), wires.move(qkv, qkv_o)]

    masks = half_masks()
    square = (all_frames * TILE,) * 2
    key_index, query_index = rows_iota(square), lanes_iota(square)
    same = lax.rem(key_index, TILE) == lax.rem(query_index, TILE)
    equal = key_index == query_index
    groups = rows // TILE
    batch = 3
    middle = (groups // batch) // 2

    def attend(start, stop):
        def body(step, carry):
            time_groups(
                heads,
                [step * batch + i for i in range(batch)],
                qkv,
                keep_t,
                time_soft,
                mixed,
                masks,
                same,
                equal,
            )
            return carry

        lax.fori_loop(start, stop, body, 0)

    def exchange(first_row, count):
        spot = pl.ds(first_row, count)
        copies = []
        for peer in others:
            copies.append(
                wires.to(peer, mixed.at[peer[1], spot], mixed_here.at[head, spot])
            )
        return copies

    cut_row = middle * batch * TILE
    attend(0, middle)
    exchanged = exchange(0, cut_row)
    run("c")
    attend(middle, groups // batch)
    for group in range(groups // batch * batch, groups):
        time_groups(heads, [group], qkv, keep_t, time_soft, mixed, masks, same, equal)
    exchanged = exchanged + exchange(cut_row, rows - cut_row)
    run("d")
    for name in "JK":
        gathers[name].begin_near()
    run("afterto")
    mixed_here[head] = mixed[head]
    saved = saved + [wires.move(time_soft, time_soft_o), wires.move(mixed, mixed_o)]
    key_index, query_index = rows_iota((rows, rows)), lanes_iota((rows, rows))
    for frame in range(frames):
        chosen = lanes_iota(keep_all.shape) == mine + frame
        kept = jnp.sum(jnp.where(chosen, keep_all, 0.0), axis=1, keepdims=True)
        allowed = (kept > 0.5) | (key_index == patches) | (key_index == query_index)
        blocked[frame] = jnp.where(allowed, 0.0, MASKED)
    mixer_copy.wait()
    run("to")
    for copy in exchanged:
        copy.wait_recv()
    run("afterto2")
    run("F1b!")
    gathers["O"].finish()
    sum_here = jnp.zeros(flat, FLOAT)
    for place in range(blocks):
        sum_here = sum_here + mm(
            by_rows(mixed_here[place], frames), bundles[place, :own_width]
        )
    half = (sum_here + biases[0:1, :]).astype(HALF)
    proj[...] = half.reshape(shaped)
    added = (mm(half, mixer[...]) + biases[1:2, :]).reshape(shaped)
    tokens = jnp.swapaxes(tokens_in[...], 0, 1)
    for frame in range(frames):
        state[frame, :patches] = tokens[frame].astype(FLOAT) + added[frame, :patches]
        state[frame, patches : patches + 1] = class_token[...].astype(FLOAT)
        state[frame, patches + 1 :] = jnp.zeros((rows - patches - 1, width), FLOAT)
    saved.append(wires.move(proj, proj_o))
    state_copy = wires.move(state, state_o)
    run("f1b")

    unit, _ = normalize(state[...].reshape(flat))
    real = lax.rem(row, rows) <= patches
    half = jnp.where(real, unit * gains[1] + shifts[1], 0.0).astype(HALF)
    space_normed[...] = half.reshape(shaped)
    run("e")
    run("q!")
    gathers["P"].finish()
    start_bias = 2 * own_width
    for kind in range(3):
        if kind == 2:
            run("f")
            run("v!")
            gathers["Q"].finish()
            saved.append(wires.move(bundles, bundles_o))
        for place in range(blocks):
            joint[place * own_width : (place + 1) * own_width] = bundles[
                place, (1 + kind) * own_width : (2 + kind) * own_width
            ]
        raw = mm_t(space_normed[...].reshape(flat), joint[...])
        if kind != 1:
            begin = start_bias + (kind // 2) * own_width
            bias = jnp.concatenate(
                [smalls[place][:, begin : begin + own_width] for place in range(blocks)], axis=1
            )
            raw = raw + bias
        raw = raw.astype(HALF)
        if kind == 0:
            raw = (raw * (HEAD_DIM**-0.5)).astype(HALF)
        space_qkv[kind] = raw.reshape(shaped)
    saved = saved + [wires.move(space_normed, space_normed_o), wires.move(space_qkv, space_qkv_o)]
    run("g")

    def one_frame(frame, carry):
        softs = []
        for pair in range(width // PAIR):
            spot = slice(pair * PAIR, (pair + 1) * PAIR)
            query, key = space_qkv[0, frame, :, spot], space_qkv[1, frame, :, spot]
            for side in range(2):
                scores = mm_t(key * masks[side], query) + blocked[frame]
                softs.append(softmax_columns(scores).astype(HALF))
                space_soft[frame, 2 * pair + side] = softs[-1]
        for pair in range(width // PAIR):
            spot = slice(pair * PAIR, (pair + 1) * PAIR)
            value = space_qkv[2, frame, :, spot]
            result = t_mm(softs[2 * pair], value * masks[0]) + t_mm(
                softs[2 * pair + 1], value * masks[1]
            )
            spread[frame, :, spot] = result.astype(HALF)
        return carry

    lax.fori_loop(0, frames, one_frame, 0)
    run("h")
    run("i")
    saved = saved + [wires.move(space_soft, space_soft_o), wires.move(spread, spread_o)]
    for place in range(blocks):
        joint[place * own_width : (place + 1) * own_width] = bundles[place, 4 * own_width :]
    added = mm(spread[...].reshape(flat), joint[...]).reshape(shaped)
    part = added[0, patches : patches + 1]
    for frame in range(1, frames):
        part = part + added[frame, patches : patches + 1]
    class_parts[head] = part * (1.0 / all_frames)
    class_copies = [
        wires.to(peer, class_parts.at[head], class_parts.at[head]) for peer in others
    ]
    state_copy.wait()
    full = state
    full[...] = state[...] + added + biases[2:3, :]
    run("cl")

    for copy in class_copies:
        copy.wait_recv()
    class_state = class_token[...].astype(FLOAT) + biases[2:3, :]
    for place in range(blocks):
        class_state = class_state + class_parts[place]
    full[0, patches : patches + 1] = class_state
    unit, _ = normalize(full[...].reshape(flat))
    values = jnp.where(is_real, unit * gains[2] + shifts[2], 0.0)
    mlp_normed[...] = values.astype(HALF)
    turned = jnp.where(is_class, values * lead, values).astype(HALF).T
    for part in range(cuts):
        normed_t[spread_index(clip, part, cuts, rest, cut)] = turned[part * cut : (part + 1) * cut]
    class_row = jnp.where(is_class, lead, 1.0)
    run("m0")
    sends, firsts = [], []
    half_lanes = [pl.ds(0, hidden), pl.ds(hidden, hidden)]
    for number, block in enumerate((1, 0, 3, 2)):
        place = flip_all(head, block, blocks)
        if number == 0:
            gathers["J"].near.wait_recv()
            gathers["K"].near.wait_recv()
        if number == 2:
            run("m4")
            run("W1!")
            gathers["J"].last.wait_recv()
            run("W2!")
            gathers["K"].last.wait_recv()
        inner = mm(mlp_normed[...], first[place]) + smalls[place][:, 4 * own_width :]
        outer = mm_t(grads_half[...], second[place])
        chance, density = gelu_parts(inner)
        active = (inner * chance).astype(HALF)
        back = (outer * (chance + inner * density)).astype(HALF)
        hidden_sums[pl.ds(place, 1)] = jnp.sum(
            back.astype(FLOAT) * class_row, axis=0, keepdims=True
        )
        if number < 2:
            run(("m1", "m3")[number])
        forward = mm(active, second[place])
        backward = mm_t(back, first[place])
        if number == 0:
            total[...] = forward
            normed_back[...] = backward
        else:
            total[...] += forward
            normed_back[...] += backward
        factors = [(normed_t, back), (grads_t, active)]
        across = number // 2
        if number % 2 == 0:
            for copy in sends:
                wires.drain(copy)
            sends = []
            for lanes, (turned, factor) in zip(half_lanes, factors):
                piece = mm(turned[...].reshape(width, frames * rows), factor)
                found[:, :, :, :, lanes] = piece.astype(HALF).reshape(
                    2, 2, rest, block_rows, hidden
                )
                sends.append(
                    wires.to(
                        peers["near"],
                        found.at[:, :, :, :, lanes],
                        core_landing.at[across, :, :, :, :, lanes],
                    )
                )
            if number == 0:
                run("m2")
            continue
        if number == 1:
            run("cs0")
        for copy, lanes, (turned, factor) in zip(sends, half_lanes, factors):
            piece = mm(turned[...].reshape(width, frames * rows), factor)
            copy.wait_recv()
            landed = core_landing[across, :, :, :, :, lanes].astype(FLOAT)
            whole[across, :, :, :, :, lanes] = (
                piece.reshape(2, 2, rest, block_rows, hidden) + landed
            ).astype(HALF)
        if across == 0:
            for name, (start, count) in column_groups(2 * hidden).items():
                lanes = pl.ds(start, count)
                landing = landings.pop(0) if HOPS[name][0] in "yz" else None
                if HOPS[name][0] == "y":
                    source, peer = whole.at[0, 1, :, :, :, lanes], peers["one"]
                elif HOPS[name][0] == "z":
                    source, peer = whole.at[0, :, 1, :, :, lanes], peers["two"]
                else:
                    continue
                firsts.append((wires.to(peer, source, landing), landing, name, lanes))
        else:
            saved.append(wires.move(whole.at[1], whole_o.at[1]))
    result = (full[...].reshape(flat) + total[...] + biases[3:4, :]).reshape(shaped)
    for frame in range(frames):
        chosen = lanes_iota(keep_all.shape) == mine + frame
        kept = jnp.sum(jnp.where(chosen, keep_all, 0.0), axis=1, keepdims=True)
        patch_out[frame] = result[frame, :patches] * kept[:patches]
    class_out[...] = own_lanes(result[0, patches : patches + 1], head, blocks)
    unit, inverse = normalize(full[...].reshape(flat))
    incoming = normed_back[...]
    weighted = jnp.where(is_class, incoming * lead, incoming)
    sums_out[0:1] = jnp.sum(weighted * unit, axis=0, keepdims=True)
    sums_out[1:2] = jnp.sum(weighted, axis=0, keepdims=True)
    sums_out[3:] = jnp.zeros((sums_out.shape[0] - 3, width), FLOAT)
    change = normalize_back(incoming * gains[2], unit, inverse)
    change = jnp.where(is_real, change, 0.0)
    grad[...] += change.reshape(shaped)
    saved.append(wires.move(grad, grad_o))
    for copy, *_ in firsts:
        copy.wait_recv()

    def add_first(index, carry):
        for _, landing, name, lanes in firsts:
            for outer in range(2):
                place = (0, 0, outer) if HOPS[name][0] == "y" else (0, outer, 0)
                spot = place + (index, slice(None), lanes)
                whole[spot] = (
                    whole[spot].astype(FLOAT) + landing[outer, index].astype(FLOAT)
                ).astype(HALF)
        return carry

    lax.fori_loop(0, rest, add_first, 0)
    wires.finish()
    saved.append(wires.move(whole.at[0], whole_o.at[0]))
    for copy in saved:
        copy.wait()


class Reduce:
    def __init__(self, wires, data, lanes, landings, hops, out, across=2, begun=None):
        self.wires, self.data, self.lanes = wires, data, lanes
        self.landings, self.hops, self.out, self.begun = landings, hops, out, begun
        self.extent = [across, 2, 2, data.shape[3]]
        self.at, self.copy = 0, None

    @property
    def idle(self):
        return self.copy is None and self.at < len(self.hops)

    def launch(self):
        axis, peer = self.hops[self.at]
        places = [pl.ds(0, size) for size in self.extent]
        if axis is not None:
            half = self.extent[axis] // 2
            places[axis] = pl.ds(half, half)
            self.extent[axis] = half
        self.first = [0, 0]
        source = self.data
        if self.begun is not None and self.at == 0:
            source = self.begun
            if axis != 0:
                places[0] = pl.ds(1, 1)
                self.first = [1, 0]
        self.copy = self.wires.to(
            peer,
            source.at[tuple(places) + (slice(None), self.lanes)],
            self.landings[self.at],
        )

    def wait(self):
        self.copy.wait_recv()
        if self.hops[self.at][0] is None:
            self.wires.drain(self.copy)
        self.copy = None

    def land(self):
        self.wait()
        landing = self.landings[self.at]
        self.at += 1
        tail = (slice(None), self.lanes)
        if self.at == len(self.hops):
            self.out(
                self.data[(0, 0, 0, 0) + tail].astype(FLOAT)
                + landing[0, 0, 0, 0].astype(FLOAT)
            )
            return
        start = self.first[0]
        _, second, third, rest = self.extent
        for place in [
            (a, b, c)
            for a in range(start, self.extent[0])
            for b in range(second)
            for c in range(third)
        ]:

            def add(index, carry):
                spot = place + (index,) + tail
                landed = landing[place[0] - start, place[1], place[2], index]
                self.data[spot] = (
                    self.data[spot].astype(FLOAT) + landed.astype(FLOAT)
                ).astype(HALF)
                return carry

            lax.fori_loop(0, rest, add, 0)


class Mixer(Reduce):
    def __init__(self, wires, data, head, near, far, landings, hops, out):
        half = data.shape[5] // 2
        bit = lax.rem(head, 2)
        super().__init__(
            wires,
            data,
            pl.ds(pl.multiple_of(bit * half, PAIR), half),
            landings,
            [None] + hops + [(None, far), None],
            out,
            1,
        )
        self.near = near
        self.other = pl.ds(pl.multiple_of((1 - bit) * half, PAIR), half)

    def launch(self):
        if self.at == 0:
            source = self.data.at[:, :, :, :, :, self.other]
        elif self.at == len(self.hops) - 1:
            source = self.data.at[0, 0, 0, 0, :, self.lanes]
        else:
            super().launch()
            return
        self.copy = self.wires.to(self.near, source, self.landings[self.at])

    def land(self):
        if 0 < self.at < len(self.hops) - 1:
            super().land()
            return
        self.copy.wait_recv()
        self.copy = None
        landing = self.landings[self.at]
        self.at += 1
        if self.at == len(self.hops):
            self.out[:, self.lanes] = self.data[0, 0, 0, 0, :, self.lanes].astype(FLOAT)
            self.out[:, self.other] = landing[...].astype(FLOAT)
            return
        for place in [(0, a, b) for a in range(2) for b in range(2)]:

            def add(index, carry):
                spot = place + (index, slice(None), self.lanes)
                self.data[spot] = (
                    self.data[spot].astype(FLOAT) + landing[place + (index,)].astype(FLOAT)
                ).astype(HALF)
                return carry

            lax.fori_loop(0, self.data.shape[3], add, 0)


class Vectors:
    def __init__(self, wires, sums, landing, peers, out):
        self.wires, self.sums, self.landing, self.peers, self.out = wires, sums, landing, peers, out
        self.at, self.copy = 0, None

    @property
    def idle(self):
        return self.copy is None and self.at < len(self.peers)

    def launch(self):
        self.copy = self.wires.to(
            self.peers[self.at], self.sums.at[self.at], self.landing.at[self.at]
        )

    def land(self):
        self.copy.wait_recv()
        self.copy = None
        total = self.sums[self.at] + self.landing[self.at]
        self.at += 1
        if self.at == len(self.peers):
            self.out(total)
        else:
            self.sums[self.at] = total


def backward_kernel(
    heads,
    cuts,
    tokens_in,
    class_token,
    gains,
    shifts,
    mlp_sums,
    hidden_sums,
    grad_in,
    bundles_in,
    projections,
    mixer_in,
    normed_in,
    qkv_in,
    time_soft_in,
    mixed_in,
    state_in,
    proj_in,
    space_normed_in,
    space_qkv_in,
    space_soft_in,
    spread_in,
    whole_in,
    patch_out,
    class_out,
    inputs_out,
    outputs_out,
    mixer_out,
    hidden_out,
    return_out,
    gains_out,
    shifts_out,
    biases_out,
    input_bias_out,
    hidden_bias_out,
    grad,
    bundles,
    time_output,
    weight,
    normed,
    qkv,
    time_soft,
    mixed,
    state,
    proj,
    space_normed,
    space_qkv,
    space_soft,
    spread,
    joint,
    outer_grad,
    mixed_back,
    proj_back,
    time_back,
    near_landing,
    far_landing,
    class_parts,
    mlp,
    space,
    space_landing,
    time_data,
    mixer_data,
    vectors,
    vector_landing,
    *rest,
):
    send_sems, recv_sems, local_sems = rest[-3:]
    landings = list(rest[:-3])
    clip, head = lax.axis_index("clip"), lax.axis_index("head")
    patches, frames, width = tokens_in.shape
    all_frames, rows, _ = normed.shape
    blocks = all_frames // frames
    own_width = mixed.shape[2] // frames
    wide = qkv.shape[2] // 3
    flat = (frames * rows, width)
    shaped = (frames, rows, width)
    cut = width // cuts
    rest_size = mlp.shape[3]
    hidden = mlp.shape[5] // 2
    near, far = flip(head, 1), flip(head, 2)
    cross = flip(near, 2)
    near_peer, far_peer, cross_peer = (clip, near), (clip, far), (clip, cross)
    others = [near_peer, far_peer, cross_peer]
    clip_peers = []
    bit = 1
    while bit < cuts:
        clip_peers.append((flip(clip, bit), head))
        bit *= 2
    wires = Wires(send_sems, recv_sems, local_sems)
    order = [
        (grad_in, grad),
        (bundles_in.at[:, pl.ds(own_width, 4 * own_width)], bundles),
        (space_soft_in, space_soft),
        (space_qkv_in, space_qkv),
        (state_in, state),
        (mixer_in, weight),
    ]
    order_later = [
        (whole_in, mlp),
        (space_normed_in, space_normed),
        (spread_in, spread),
        (proj_in, proj),
        (qkv_in, qkv),
        (time_soft_in, time_soft),
        (bundles_in.at[head, pl.ds(0, own_width)], time_output),
        (normed_in, normed),
        (mixed_in, mixed),
    ]
    ready = {id(dest): wires.move(source, dest) for source, dest in order}

    def need(*refs):
        for ref in refs:
            ready[id(ref)].wait()

    greet(others + clip_peers)
    clip_hops = [
        (3 if 1 << number < rest_size else None, peer)
        for number, peer in enumerate(clip_peers[2:])
    ]
    steps = {
        "x": [(0, far_peer)],
        "y": [(1, clip_peers[0])],
        "z": [(2, clip_peers[1])],
        "w": clip_hops,
    }
    chains = {}

    def take(name):
        hops = [hop for code in HOPS[name] for hop in steps[code]]
        return hops, [landings.pop(0) for _ in hops]

    def chain(name, data, lanes, out, across=2, begun=None):
        hops, mine = take(name)
        chains[name] = Reduce(wires, data, lanes, mine, hops, out, across, begun)

    def run(place):
        for event in SCHEDULE.get(place, ()):
            if event[-1] == "+":
                chains[event[:-1]].launch()
            else:
                chains[event[:-1]].land()

    def put_inputs(layer, first, second):
        def write(value):
            for number, kind in enumerate((first, second)):
                piece = value[:, number * own_width : (number + 1) * own_width]
                if kind == 3:
                    outputs_out[layer] = piece.T
                else:
                    inputs_out[layer, kind] = piece

        return write

    def put_hidden(start, count):
        def write(value):
            inner = max(0, min(count, hidden - start))
            if inner:
                hidden_out[:, start : start + inner] = value[:, :inner]
            if count > inner:
                first = start + inner - hidden
                return_out[:, first : first + count - inner] = value[:, inner:]

        return write

    middle = 2 * own_width
    left, right = pl.ds(0, middle), pl.ds(middle, middle)
    for name, (start, count) in column_groups(2 * hidden).items():
        chain(
            name,
            mlp,
            pl.ds(start, count),
            put_hidden(start, count),
            2,
            whole_in,
        )
    chain("S", space.at[0], left, put_inputs(1, 0, 1))
    chain("R", space.at[0], right, put_inputs(1, 2, 3))
    chain("T", time_data, left, put_inputs(0, 3, 0), 1)
    chain("U", time_data, right, put_inputs(0, 1, 2), 1)
    hops, mine = take("X")
    mine = [landings.pop(0)] + mine + [landings.pop(0), landings.pop(0)]
    chains["X"] = Mixer(wires, mixer_data, head, near_peer, far_peer, mine, hops, mixer_out)

    def put_vectors(total):
        part = width // (blocks * cuts)
        shared = pick(total[:10], (clip * blocks + head) * part, part)
        for place in range(3):
            gains_out[place] = shared[place : place + 1]
            shifts_out[place] = shared[3 + place : 4 + place]
        biases_out[...] = shared[6:10]
        other = pick(total[10:14], (head * cuts + clip) * part, part)
        input_bias_out[0] = other[0:2]
        input_bias_out[1] = other[2:4]
        chosen = rows_iota((blocks, 1)) == head
        row = jnp.sum(jnp.where(chosen, total[14 : 14 + blocks], 0.0), axis=0, keepdims=True)
        hidden_bias_out[...] = pick(row, clip * (hidden // cuts), hidden // cuts)

    chains["V"] = Vectors(
        wires, vectors, vector_landing, [near_peer, far_peer] + clip_peers, put_vectors
    )
    run("begin")

    need(grad)
    lead = (head == 0).astype(FLOAT)
    row = lax.rem(rows_iota((frames * rows, 1)), rows)
    is_patch = row < patches
    class_grad = grad[0, patches : patches + 1]
    values = grad[...].reshape(flat)
    sums = {}
    sums["bias2"] = (
        jnp.sum(jnp.where(is_patch, values, 0.0), axis=0, keepdims=True) + lead * class_grad
    )
    values = jnp.where(
        is_patch, values, jnp.where(row == patches, class_grad * (1.0 / all_frames), 0.0)
    )
    half = values.astype(HALF)
    outer_grad[...] = half.reshape(shaped)
    ready.update({id(dest): wires.move(source, dest) for source, dest in order_later})
    need(bundles)
    for place in range(blocks):
        joint[place * own_width : (place + 1) * own_width] = bundles[place, 3 * own_width :]
    mixed_back[...] = mm_t(outer_grad[...].reshape(flat), joint[...]).astype(HALF).reshape(shaped)

    need(space_soft, space_qkv)
    masks = half_masks()

    def one_frame(frame, carry):
        pairs = width // PAIR
        for group in range(2):
            chosen = range(group * pairs // 2, (group + 1) * pairs // 2)
            backs, mines = [], []
            for pair in chosen:
                spot = slice(pair * PAIR, (pair + 1) * PAIR)
                value = space_qkv[2, frame, :, spot]
                for side in range(2):
                    mine = mixed_back[frame, :, spot] * masks[side]
                    mines.append(mine)
                    backs.append(mm_t(value, mine))
            scores = []
            for number, pair in enumerate(chosen):
                for side in range(2):
                    soft = space_soft[frame, 2 * pair + side].astype(FLOAT)
                    product = soft * backs[2 * number + side]
                    score = product - soft * jnp.sum(product, axis=0, keepdims=True)
                    scores.append(score.astype(HALF))
            for number, pair in enumerate(chosen):
                spot = slice(pair * PAIR, (pair + 1) * PAIR)
                query, key = space_qkv[0, frame, :, spot], space_qkv[1, frame, :, spot]
                left, right = scores[2 * number], scores[2 * number + 1]
                value_back = mm(space_soft[frame, 2 * pair], mines[2 * number]) + mm(
                    space_soft[frame, 2 * pair + 1], mines[2 * number + 1]
                )
                key_back = mm(left, query * masks[0]) + mm(right, query * masks[1])
                query_back = t_mm(left, key * masks[0]) + t_mm(right, key * masks[1])
                space_qkv[0, frame, :, spot] = (query_back * (HEAD_DIM**-0.5)).astype(HALF)
                space_qkv[1, frame, :, spot] = key_back.astype(HALF)
                space_qkv[2, frame, :, spot] = value_back.astype(HALF)
        return carry

    lax.fori_loop(0, frames, one_frame, 0)
    incoming = jnp.zeros(flat, FLOAT)
    for kind in range(3):
        for place in range(blocks):
            joint[place * own_width : (place + 1) * own_width] = bundles[
                place, kind * own_width : (1 + kind) * own_width
            ]
        piece = space_qkv[kind].reshape(flat)
        incoming = incoming + mm(piece, joint[...])
        if kind != 1:
            sums["space%d" % kind] = jnp.sum(piece.astype(FLOAT), axis=0, keepdims=True)
    need(state)
    unit, inverse = normalize(state[...].reshape(flat))
    sums["gain1"] = jnp.sum(incoming * unit, axis=0, keepdims=True)
    sums["shift1"] = jnp.sum(incoming, axis=0, keepdims=True)
    by_frame = incoming.reshape(shaped)
    part = by_frame[0, patches : patches + 1]
    for frame in range(1, frames):
        part = part + by_frame[frame, patches : patches + 1]
    class_parts[head] = part
    class_state_grad = class_grad
    change = normalize_back(incoming * gains[1], unit, inverse)
    result = jnp.where(is_patch, grad[...].reshape(flat) + change, 0.0)
    grad[...] = result.reshape(shaped)
    need(mlp)
    run("b")
    sums["bias1"] = jnp.sum(result, axis=0, keepdims=True)
    half = result.astype(HALF)
    time_grad = mixed_back
    time_grad[...] = half.reshape(shaped)
    need(weight)
    back = mm_t(time_grad[...].reshape(flat), weight[...]).astype(HALF)
    mine = pl.multiple_of(head * frames, frames)
    proj_back[pl.ds(mine, frames)] = back.reshape(shaped)
    far_copies = [
        wires.to(far_peer, proj_back.at[mine + frame], proj_back.at[mine + frame])
        for frame in range(frames)
    ]
    own_part = proj_back.at[pl.ds(mine, frames)]
    near_copy = wires.to(near_peer, own_part, own_part)
    class_copies = [
        wires.to(peer, class_parts.at[head], class_parts.at[head]) for peer in others
    ]
    sums["bias0"] = jnp.sum(back.astype(FLOAT), axis=0, keepdims=True)

    weight_copies = load_wide(wires, projections, weight, own_width)

    need(space_normed, spread, proj)

    def place_rows(part, result):
        return result[part * cut : (part + 1) * cut]

    def send_core(lanes):
        return wires.to(
            near_peer,
            space.at[1, :, :, :, :, :, lanes],
            space_landing.at[:, :, :, :, :, lanes],
        )

    core_copies = []
    turned = space_normed[...].reshape(flat).T
    for kind in range(4):
        if kind == 2:
            core_copies.append(send_core(left))
            run("sw")
        if kind == 3:
            turned = outer_grad[...].reshape(flat).T
            result = mm(turned, spread[...].reshape(flat)).astype(HALF)
        else:
            result = mm(turned, space_qkv[kind].reshape(flat)).astype(HALF)
        for block in range(blocks):
            relative = flip_all(head, block, blocks)
            core, across = lax.rem(relative, 2), lax.div(relative, 2)
            for part in range(cuts):
                space[
                    (core, across)
                    + spread_index(clip, part, cuts, rest_size, cut)
                    + (slice(kind * own_width, (kind + 1) * own_width),)
                ] = place_rows(part, result)[:, block * own_width : (block + 1) * own_width]
    core_copies.append(send_core(right))
    turned = proj[...].reshape(flat).T
    result = mm(turned, time_grad[...].reshape(flat)).astype(HALF)
    for part in range(cuts):
        mixer_data[(0,) + spread_index(clip, part, cuts, rest_size, cut)] = place_rows(part, result)
    run("X")
    run("x1")

    need(qkv, time_soft, time_output)
    for copy in weight_copies:
        copy.wait()

    def outer(block):
        start = pl.multiple_of(block * frames, frames)
        back = mm_t(proj_back[pl.ds(start, frames)].reshape(flat), time_output[...])
        back = back.astype(HALF)
        gap = jnp.zeros((frames * rows, wide - own_width), HALF)
        time_back[pl.ds(start, frames)] = jnp.concatenate([back, gap], axis=1).reshape(
            frames, rows, wide
        )

    outer(head)
    near_copy.wait_recv()
    outer(near)
    run("x2")

    def add_core(lanes):
        for place in [(a, b, c) for a in range(2) for b in range(2) for c in range(2)]:

            def add(index, carry):
                spot = place + (index, slice(None), lanes)
                space[(0,) + spot] = (
                    space[(0,) + spot].astype(FLOAT) + space_landing[spot].astype(FLOAT)
                ).astype(HALF)
                return carry

            lax.fori_loop(0, rest_size, add, 0)

    for number, lanes in enumerate((left, right)):
        run(("c1", "c2")[number])
        core_copies[number].wait_recv()
        add_core(lanes)
        run(("S", "R")[number])
    run("c3")
    passed = []
    for frame in range(frames):
        run(("ag0", "ag1")[min(frame, 1)])
        far_copies[frame].wait_recv()
        here = proj_back.at[far * frames + frame]
        passed.append(wires.to(near_peer, here, here))
    run("ag2")
    outer(far)
    for frame in range(frames):
        run(("p0", "p1")[min(frame, 1)])
        passed[frame].wait_recv()
    outer(cross)
    total_rows = all_frames * TILE
    groups = rows // TILE
    batch = 3

    def time_backward(chosen):
        work = []
        for group in chosen:
            spot = pl.ds(pl.multiple_of(group * TILE, TILE), TILE)
            piece = qkv[:, spot, :].reshape(total_rows, 3 * wide)
            outers = time_back[:, spot, :].reshape(total_rows, wide)
            backs, mines = [], []
            for number in range(heads):
                left = (number // 2) * PAIR
                own = outers[:, left : left + PAIR] * masks[number % 2]
                mines.append(own)
                backs.append(mm_t(piece[:, 2 * wide + left : 2 * wide + left + PAIR], own))
            work.append((group, spot, piece, mines, backs))
        for group, spot, piece, mines, backs in work:
            parts = [[], [], []]
            for pair in range(wide // PAIR):
                left = pair * PAIR
                query = piece[:, left : left + PAIR]
                key = piece[:, wide + left : wide + left + PAIR]
                found = None
                for side in range(2):
                    number = 2 * pair + side
                    if number >= heads:
                        continue
                    soft = time_soft[group, number]
                    large = soft.astype(FLOAT)
                    product = large * backs[number]
                    score = product - large * jnp.sum(product, axis=0, keepdims=True)
                    score = score.astype(HALF)
                    terms = [
                        t_mm(score, key * masks[side]),
                        mm(score, query * masks[side]),
                        mm(soft, mines[number]),
                    ]
                    found = terms if found is None else [x + y for x, y in zip(found, terms)]
                for kind, scale in enumerate((HEAD_DIM**-0.5, 1.0, 1.0)):
                    parts[kind].append((found[kind] * scale).astype(HALF))
            joined = jnp.concatenate(parts[0] + parts[1] + parts[2], axis=1)
            qkv[:, spot, :] = joined.reshape(all_frames, TILE, 3 * wide)

    def body(step, carry):
        time_backward([step * batch + i for i in range(batch)])
        return carry

    lax.fori_loop(0, groups // batch, body, 0)
    for group in range(groups // batch * batch, groups):
        time_backward([group])

    need(normed)
    run("at")
    norm_sums = [jnp.zeros((1, width), FLOAT), jnp.zeros((1, width), FLOAT)]
    bias_sums = jnp.zeros((1, 3 * wide), FLOAT)

    def inner(block):
        start = pl.multiple_of(block * frames, frames)
        piece = qkv[pl.ds(start, frames)].reshape(frames * rows, 3 * wide)
        result = mm(piece, weight[...])
        values = normed[pl.ds(start, frames)].reshape(flat).astype(FLOAT)
        norm_sums[0] = norm_sums[0] + jnp.sum(result * values, axis=0, keepdims=True)
        norm_sums[1] = norm_sums[1] + jnp.sum(result, axis=0, keepdims=True)
        return result, jnp.sum(piece.astype(FLOAT), axis=0, keepdims=True)

    result, more = inner(cross)
    bias_sums = bias_sums + more
    space_qkv[0] = result.astype(HALF).reshape(shaped)
    back_cross = wires.to(near_peer, space_qkv.at[0], near_landing.at[0])
    result, more = inner(far)
    bias_sums = bias_sums + more
    run("rc0")
    back_cross.wait_recv()
    result = result + near_landing[0].reshape(flat).astype(FLOAT)
    space_qkv[1] = result.astype(HALF).reshape(shaped)
    back_far = wires.to(far_peer, space_qkv.at[1], far_landing)
    result, more = inner(near)
    bias_sums = bias_sums + more
    space_qkv[2] = result.astype(HALF).reshape(shaped)
    back_near = wires.to(near_peer, space_qkv.at[2], near_landing.at[1])
    run("rn")
    result, more = inner(head)
    bias_sums = bias_sums + more
    outer_grad[...] = result.astype(HALF).reshape(shaped)

    sums["gain0"] = (norm_sums[0] - norm_sums[1] * shifts[0]) / gains[0]
    sums["shift0"] = norm_sums[1]
    lane = lanes_iota((1, width))
    here = (lane >= head * own_width) & (lane < (head + 1) * own_width)
    for kind in (0, 2):
        own = bias_sums[:, kind * wide : kind * wide + own_width]
        repeated = jnp.concatenate([own] * blocks, axis=1)
        sums["time%d" % kind] = jnp.where(here, repeated, 0.0)
    names = [
        sums["gain0"],
        sums["gain1"],
        mlp_sums[0:1],
        sums["shift0"],
        sums["shift1"],
        mlp_sums[1:2],
        sums["bias0"],
        sums["bias1"],
        sums["bias2"],
        mlp_sums[2:3],
        sums["time0"],
        sums["time2"],
        sums["space0"],
        sums["space2"],
    ]
    for number, value in enumerate(names):
        vectors[0, number : number + 1] = value
    vectors[0, len(names) : len(names) + blocks] = hidden_sums[...]
    vectors[0, len(names) + blocks :] = jnp.zeros(
        (vectors.shape[1] - len(names) - blocks, width), FLOAT
    )
    run("V")
    run("v")

    need(mixed)

    def over_blocks(left, right):
        total = None
        for block in range(blocks):
            spot = slice(block * frames, (block + 1) * frames)
            term = t_mm(left[spot].reshape(flat), right(block, spot))
            total = term if total is None else total + term
        return total

    def put_time(kind, result):
        result = result.astype(HALF)
        lanes = slice(kind * own_width, (kind + 1) * own_width)
        for part in range(cuts):
            time_data[(0,) + spread_index(clip, part, cuts, rest_size, cut) + (lanes,)] = (
                place_rows(part, result)
            )

    def columns(kind):
        first = kind * wide
        return lambda block, spot: qkv[spot, :, first : first + wide].reshape(
            frames * rows, wide
        )

    put_time(0, over_blocks(proj_back, lambda block, spot: by_rows(mixed[block], frames)))
    put_time(1, over_blocks(normed, columns(0))[:, :own_width])
    run("T")
    run("t1")
    put_time(2, over_blocks(normed, columns(1))[:, :own_width])
    run("t2")
    put_time(3, over_blocks(normed, columns(2))[:, :own_width])
    run("U")
    run("t3")

    tokens = jnp.swapaxes(tokens_in[...], 0, 1)
    back_near.wait_recv()
    run("rx")
    back_far.wait_recv()
    for frame in range(frames):
        unit, inverse = normalize(tokens[frame].astype(FLOAT))
        incoming = (
            outer_grad[frame, :patches].astype(FLOAT)
            + near_landing[1, frame, :patches].astype(FLOAT)
            + far_landing[frame, :patches].astype(FLOAT)
        )
        patch_out[frame] = grad[frame, :patches] + normalize_back(
            incoming * gains[0], unit, inverse
        )
    for copy in class_copies:
        copy.wait_recv()
    unit, inverse = normalize(class_token[...].astype(FLOAT))
    incoming = class_parts[0]
    for place in range(1, blocks):
        incoming = incoming + class_parts[place]
    result = class_state_grad + normalize_back(incoming * gains[1], unit, inverse)
    class_out[...] = own_lanes(result, head, blocks)

    run("fin")
    run("tail")
    while True:
        for item in chains.values():
            if item.idle:
                item.launch()
        live = [item for item in chains.values() if item.copy is not None]
        if not live:
            break
        for item in live:
            item.land()
    wires.finish()


def deliver_kernel(index, patch_first, patch_second, mixer, *refs):
    count = (len(refs) - 3) // 2
    first, second, mixer_out = refs[count : count + 3]
    first[...] = jnp.swapaxes(patch_first[...], 0, 1)
    second[...] = jnp.swapaxes(patch_second[...], 0, 1)
    share = mixer_out.shape[0]
    total = jnp.zeros(mixer_out.shape, FLOAT)
    head = index[0]
    for block in range(mixer.shape[0] // share):
        total = jnp.where(head == block, mixer[block * share : (block + 1) * share], total)
    mixer_out[...] = total
    for source, dest in zip(refs[:count], refs[count + 3 :]):
        dest[...] = source[...]


VMEM = pl.BlockSpec(memory_space=pltpu.VMEM)
ANY = pl.BlockSpec(memory_space=pl.ANY)
WIRES = 96
LIMIT = 125 * 2**19


def shape(dims, kind=HALF):
    return jax.ShapeDtypeStruct(tuple(dims), kind)


def room(dims, kind=HALF):
    return pltpu.VMEM(tuple(dims), kind)


def landing_rooms(axes, start, rest, cut, columns, begun):
    extent = list(start) + [rest]
    found = []
    for axis in axes:
        if axis is not None:
            extent[axis] //= 2
        first = [1] if begun and not found else extent[:1]
        found.append(room(first + extent[1:] + [cut, columns]))
    return found


def on_device(
    patch_tokens,
    class_token,
    keep_mask,
    patch_grad,
    class_grad,
    norm_gain,
    norm_bias,
    input_weight,
    input_bias,
    output_weight,
    time_mixer,
    output_bias,
    hidden_weight,
    hidden_bias,
    return_weight,
):
    blocks = lax.axis_size("head")
    clips = lax.axis_size("clip")
    head_index = lax.axis_index("head")
    clip_index = lax.axis_index("clip")
    _, frames, patches, width = patch_tokens.shape
    all_frames = keep_mask.shape[1]
    own_width = input_weight.shape[-1]
    heads = own_width // HEAD_DIM
    all_heads = heads * blocks
    hidden = hidden_weight.shape[-1]
    rows = round_up(patches + 1, TILE)
    groups = rows // TILE
    group_rows = all_frames * TILE
    wide = round_up(own_width, PAIR)
    cut = width // clips
    dense = 1
    while cut * dense % TILE:
        dense *= 2
    block_rows = cut * dense
    rest = clips // (4 * dense)
    tokens = frames * rows
    biases = output_bias[0]
    patch_state = jnp.transpose(patch_tokens[0], (1, 0, 2))
    patch_back = jnp.transpose(patch_grad[0], (1, 0, 2))

    projections = jnp.transpose(input_weight[0], (0, 2, 3, 1))
    gains = jnp.transpose(norm_gain, (1, 0, 2))
    shifts = jnp.transpose(norm_bias, (1, 0, 2))

    full = (frames, rows, width)
    everything = (all_frames, rows, width)
    qkv_dims = (all_frames, rows, 3 * wide)
    time_soft_dims = (groups, heads, group_rows, group_rows)
    mixed_dims = (blocks, rows, frames * own_width)
    space_soft_dims = (frames, all_heads, rows, rows)
    bundle_dims = (blocks, 5 * own_width, width)
    halves = (2, 2, 2, rest, block_rows, 2 * hidden)
    kept_outs = [
        shape(everything),
        shape(qkv_dims),
        shape(time_soft_dims),
        shape(mixed_dims),
        shape(full, FLOAT),
        shape(full),
        shape(full),
        shape((3,) + full),
        shape(space_soft_dims),
        shape(full),
        shape(bundle_dims),
        shape(full, FLOAT),
        shape(halves),
    ]
    direct_outs = [
        shape((frames, patches, width), FLOAT),
        shape((1, width // blocks), FLOAT),
        shape((8, width), FLOAT),
        shape((blocks, hidden), FLOAT),
    ]
    sems = [pltpu.SemaphoreType.DMA((WIRES,))] * 3
    (
        normed, qkv, time_soft, mixed, state, proj, space_normed, space_qkv, space_soft, spread,
        bundles, grads, whole, patch_out, class_out, mlp_sums, hidden_sums,
    ) = pl.pallas_call(
        functools.partial(forward_kernel, heads, clips),
        out_shape=kept_outs + direct_outs,
        in_specs=[VMEM] * 9 + [ANY] * 6,
        out_specs=[ANY] * len(kept_outs) + [VMEM] * len(direct_outs),
        scratch_shapes=[
            room(everything),
            room(qkv_dims),
            room(time_soft_dims),
            room(mixed_dims),
            room(mixed_dims),
            room(full, FLOAT),
            room(full),
            room(full),
            room((3,) + full),
            room(space_soft_dims),
            room(full),
            room((width, width)),
            room((frames, rows, rows), FLOAT),
            room(bundle_dims),
            room((blocks, width, hidden)),
            room((blocks, hidden, width)),
            room((blocks, 1, 4 * own_width + hidden), FLOAT),
            room((rows, all_frames), FLOAT),
            room((3 * wide, width)),
            room((width, width)),
            room((patches, frames, width)),
            room((blocks, 1, width), FLOAT),
            room(full, FLOAT),
            room((tokens, width)),
            room((tokens, width)),
            room((2, 2, rest, block_rows, tokens)),
            room((2, 2, rest, block_rows, tokens)),
            room((tokens, width), FLOAT),
            room((tokens, width), FLOAT),
            room(halves[1:]),
            room(halves),
            room(halves),
        ]
        + [
            room((2, rest, block_rows, count))
            for name, (_, count) in column_groups(2 * hidden).items()
            if HOPS[name][0] in "yz"
        ]
        + sems,
        cost_estimate=pl.CostEstimate(
            flops=int(30e9), bytes_accessed=int(40e6), transcendentals=0
        ),
        compiler_params=pltpu.CompilerParams(
            vmem_limit_bytes=LIMIT, collective_id=0, has_side_effects=True
        ),
        name="forward",
    )(
        patch_state,
        class_token,
        class_grad,
        keep_mask[0],
        input_bias[0],
        hidden_bias,
        gains,
        shifts,
        biases,
        patch_back,
        projections,
        output_weight[0],
        time_mixer[0],
        hidden_weight[0],
        return_weight[0],
    )

    clip_bits = clips.bit_length() - 1
    later = [3 if 1 << number < rest else None for number in range(clip_bits - 2)]
    steps = {"x": [0], "y": [1], "z": [2], "w": later}
    vector_rows = round_up(14 + blocks, 8)
    vector_hops = 2 + clip_bits
    pieces = [
        (name, 2, count, HOPS[name][0] != "x")
        for name, (_, count) in column_groups(2 * hidden).items()
    ]
    middle = 2 * own_width
    pieces += [("S", 2, middle, False), ("R", 2, middle, False)]
    pieces += [("T", 1, middle, False), ("U", 1, middle, False)]
    landings = []
    for name, across, columns, begun in pieces:
        axes = [axis for code in HOPS[name] for axis in steps[code]]
        landings += landing_rooms(axes, (across, 2, 2), rest, block_rows, columns, begun)
    axes = [axis for code in HOPS["X"] for axis in steps[code]]
    half_width = width // 2
    landings += landing_rooms(axes, (1, 2, 2), rest, block_rows, half_width, False)
    landings.append(room((1, 2, 2, rest, block_rows, half_width)))
    landings.append(room((1, 1, 1, 1, block_rows, half_width)))
    landings.append(room((block_rows, half_width)))
    part = width // (clips * blocks)
    hidden_part = hidden // clips
    (
        patch_input_grad, class_input_grad, inputs_total, outputs_total, mixer_total,
        hidden_total, return_total, gain_grad, shift_grad, bias_grad, input_bias_grad,
        hidden_bias_grad,
    ) = pl.pallas_call(
        functools.partial(backward_kernel, heads, clips),
        out_shape=[
            shape((frames, patches, width), FLOAT),
            shape((1, width // blocks), FLOAT),
            shape((2, 3, block_rows, own_width), FLOAT),
            shape((2, own_width, block_rows), FLOAT),
            shape((block_rows, width), FLOAT),
            shape((block_rows, hidden), FLOAT),
            shape((block_rows, hidden), FLOAT),
            shape((3, 1, part), FLOAT),
            shape((3, 1, part), FLOAT),
            shape((4, part), FLOAT),
            shape((2, 2, part), FLOAT),
            shape((1, hidden_part), FLOAT),
        ],
        in_specs=[VMEM] * 6 + [ANY] * 15,
        out_specs=[VMEM] * 12,
        scratch_shapes=[
            room(full, FLOAT),
            room((blocks, 4 * own_width, width)),
            room((own_width, width)),
            room((width, width)),
            room(everything),
            room(qkv_dims),
            room(time_soft_dims),
            room(mixed_dims),
            room(full, FLOAT),
            room(full),
            room(full),
            room((3,) + full),
            room(space_soft_dims),
            room(full),
            room((width, width)),
            room(full),
            room(full),
            room(everything),
            room((all_frames, rows, wide)),
            room((2,) + full),
            room(full),
            room((blocks, 1, width), FLOAT),
            room(halves),
            room((2, 2, 2, 2, rest, block_rows, 4 * own_width)),
            room((2, 2, 2, rest, block_rows, 4 * own_width)),
            room((1, 2, 2, rest, block_rows, 4 * own_width)),
            room((1, 2, 2, rest, block_rows, width)),
            room((vector_hops, vector_rows, width), FLOAT),
            room((vector_hops, vector_rows, width), FLOAT),
        ]
        + landings
        + sems,
        cost_estimate=pl.CostEstimate(
            flops=int(20e9), bytes_accessed=int(40e6), transcendentals=0
        ),
        compiler_params=pltpu.CompilerParams(
            vmem_limit_bytes=LIMIT, collective_id=1, has_side_effects=True
        ),
        name="backward",
    )(
        patch_state,
        class_token,
        gains,
        shifts,
        mlp_sums,
        hidden_sums,
        grads,
        bundles,
        projections,
        time_mixer[0],
        normed,
        qkv,
        time_soft,
        mixed,
        state,
        proj,
        space_normed,
        space_qkv,
        space_soft,
        spread,
        whole,
    )

    if dense > 1:
        start = lax.div(clip_index, clips // dense) * cut
        inputs_total = lax.dynamic_slice_in_dim(inputs_total, start, cut, 2)
        outputs_total = lax.dynamic_slice_in_dim(outputs_total, start, cut, 2)
        mixer_total, hidden_total, return_total = [
            lax.dynamic_slice_in_dim(total, start, cut, 0)
            for total in (mixer_total, hidden_total, return_total)
        ]
    share = cut // blocks
    small = [
        class_out,
        class_input_grad,
        gain_grad,
        shift_grad,
        inputs_total,
        input_bias_grad,
        outputs_total,
        bias_grad,
        hidden_total,
        hidden_bias_grad,
        return_total,
    ]
    whole_patch = shape((patches, frames, width), FLOAT)
    (
        patch_out, patch_input_grad, mixer_grad, class_out, class_input_grad, gain_grad,
        shift_grad, inputs_total, input_bias_grad, outputs_total, bias_grad, hidden_total,
        hidden_bias_grad, return_total,
    ) = pl.pallas_call(
        deliver_kernel,
        out_shape=[whole_patch, whole_patch, shape((share, width), FLOAT)]
        + [shape(a.shape, FLOAT) for a in small],
        in_specs=[pl.BlockSpec(memory_space=pltpu.SMEM)] + [VMEM] * (3 + len(small)),
        out_specs=[VMEM] * (3 + len(small)),
        compiler_params=pltpu.CompilerParams(vmem_limit_bytes=LIMIT),
        name="deliver",
    )(head_index.astype(jnp.int32)[None], patch_out, patch_input_grad, mixer_total, *small)
    return (
        jnp.transpose(patch_out, (1, 0, 2))[None],
        class_out,
        jnp.transpose(patch_input_grad, (1, 0, 2))[None],
        class_input_grad,
        jnp.transpose(gain_grad, (1, 0, 2)),
        jnp.transpose(shift_grad, (1, 0, 2)),
        jnp.transpose(inputs_total, (0, 2, 1, 3))[None],
        input_bias_grad[None],
        outputs_total[None],
        mixer_grad[None],
        bias_grad[None],
        hidden_total[None],
        hidden_bias_grad,
        return_total.T[None],
    )


def solution(mesh):
    in_specs = (
        P("clip", "head", None, None),
        P("clip", None),
        P("clip", None, None),
        P("clip", "head", None, None),
        P("clip", None),
        P(),
        P(),
        P(None, None, None, None, "head"),
        P(None, None, None, "head"),
        P(None, None, "head", None),
        P(),
        P(),
        P(None, None, "head"),
        P(None, "head"),
        P(None, "head", None),
    )
    out_specs = (
        P("clip", "head", None, None),
        P("clip", "head"),
        P("clip", "head", None, None),
        P("clip", "head"),
        P(None, None, ("clip", "head")),
        P(None, None, ("clip", "head")),
        P(None, None, "clip", None, "head"),
        P(None, None, None, ("head", "clip")),
        P(None, None, "head", "clip"),
        P(None, ("clip", "head"), None),
        P(None, None, ("clip", "head")),
        P(None, "clip", "head"),
        P(None, ("head", "clip")),
        P(None, "head", "clip"),
    )
    return jax.shard_map(
        on_device, mesh=mesh, in_specs=in_specs, out_specs=out_specs, check_vma=False
    )
```

```python
import functools

import jax
import jax.numpy as jnp
from jax import lax
from jax.experimental import pallas as pl
from jax.experimental.pallas import tpu as pltpu
from jax.sharding import PartitionSpec as P

HEAD_DIM = 64
PAIR = 2 * HEAD_DIM
TILE = 16
EPSILON = 1e-06
MASKED = -1e30
FLOAT = jnp.float32
HALF = jnp.bfloat16
ROW_ROW = (((1,), (1,)), ((), ()))
COL_COL = (((0,), (0,)), ((), ()))
ROOT_HALF = 0.7071067811865476
ROOT_TWO_PI = 0.3989422804014327


HOPS = {
    "A": "yzxw",
    "B": "zxyw",
    "C": "xyzw",
    "S": "yzxw",
    "R": "zxyw",
    "T": "ywz",
    "U": "yzw",
    "X": "yzw",
}
SHARES = (5, 4, 3)
SCHEDULE = {
    "begin": ("A+", "B+", "C+",),
    "sw": ("A-", "A+", "C-", "C+",),
    "X": ("X+",),
    "x1": ("B-",),
    "S": ("S+",),
    "c2": ("C-", "C+",),
    "R": ("R+",),
    "c3": ("X-", "X+",),
    "ag0": (),
    "ag2": ("B+",),
    "p0": ("C-", "C+",),
    "rc0": ("C-",),
    "rn": ("A-", "A+",),
    "V": ("V+",),
    "T": ("T+",),
    "t1": ("X-", "X+", "V-", "V+", "S-", "S+", "R-", "R+",),
    "U": ("U+",),
    "rx": ("X-", "X+", "A-", "V-", "V+", "T-", "T+", "B-", "B+", "V-", "V+", "X-", "X+", "S-", "S+", "U-", "U+", "V-", "V+", "T-", "T+", "R-", "R+", "B-", "B+", "X-", "X+", "U-", "U+", "X-", "S-", "S+", "R-", "R+",),
    "tail": ("V-", "T-", "U-", "S-", "R-", "B-",),
    "p1": ("A-", "A+",),
}
FORWARD = {
    "pre": ("O+", "P+", "Q+",),
    "after0": ("J+",),
    "afterto2": ("K+",),
    "f0": ("Os", "Ot", "Ps", "Qs", "On",),
    "f1": ("Pt", "Qt",),
    "c": ("Pn", "Qn",),
    "to": ("Js",),
    "e": ("Jt",),
    "i": ("Jn", "Ks",),
    "m2": ("Kt",),
    "cs0": ("Kn",),
}


def column_groups(total):
    found, start = {}, 0
    for name, share in zip("ABC", SHARES):
        count = total * share // sum(SHARES)
        if count:
            found[name] = (start, count)
        start += count
    return found


def round_up(value, unit):
    return -(-value // unit) * unit


def mm(left, right):
    return jnp.dot(left, right, preferred_element_type=FLOAT)


def mm_t(left, right):
    return lax.dot_general(left, right, ROW_ROW, preferred_element_type=FLOAT)


def t_mm(left, right):
    return lax.dot_general(left, right, COL_COL, preferred_element_type=FLOAT)


def normalize(values):
    average = jnp.mean(values, axis=-1, keepdims=True)
    centred = values - average
    spread = jnp.mean(centred * centred, axis=-1, keepdims=True)
    inverse = lax.rsqrt(spread + EPSILON)
    return centred * inverse, inverse


def normalize_back(scaled, unit, inverse):
    first = jnp.mean(scaled, axis=-1, keepdims=True)
    second = jnp.mean(scaled * unit, axis=-1, keepdims=True)
    return (scaled - first - unit * second) * inverse


def rows_iota(shape):
    return lax.broadcasted_iota(jnp.int32, shape, 0)


def lanes_iota(shape):
    return lax.broadcasted_iota(jnp.int32, shape, 1)


def half_masks():
    lanes = lanes_iota((1, PAIR))
    first = (lanes < HEAD_DIM).astype(HALF)
    return first, (1 - first).astype(HALF)


def softmax_columns(scores):
    top = jnp.max(scores, axis=0, keepdims=True)
    exponent = jnp.exp(scores - top)
    total = jnp.sum(exponent, axis=0, keepdims=True)
    return exponent * (1.0 / total)


def gelu_parts(values):
    size = jnp.abs(values)
    density = jnp.exp(-0.5 * values * values)
    step = 1.0 / (1.0 + (0.3275911 * ROOT_HALF) * size)
    tail = step * (
        0.5 * 0.254829592
        + step
        * (
            0.5 * -0.284496736
            + step * (0.5 * 1.421413741 + step * (0.5 * -1.453152027 + step * (0.5 * 1.061405429)))
        )
    )
    tail = tail * density
    return jnp.where(values < 0.0, tail, 1.0 - tail), density * ROOT_TWO_PI


def flip(value, mask):
    return value + mask - 2 * mask * lax.rem(lax.div(value, mask), 2)


def flip_all(value, number, size):
    total, bit = 0, 1
    while bit < size:
        mine = lax.rem(lax.div(value, bit), 2)
        total = total + bit * ((1 - mine) if number & bit else mine)
        bit *= 2
    return total


def spread_index(clip, part, cuts, rest, cut):
    bits = []
    bit = 1
    while bit < 4 * rest:
        mine = lax.rem(lax.div(clip, bit), 2)
        bits.append(1 - mine if part & bit else mine)
        bit *= 2
    inner = 0
    for value in bits[2:]:
        inner = 2 * inner + value
    outer = part // (4 * rest)
    return bits[0], bits[1], inner, pl.ds(outer * cut, cut)


class Wires:
    def __init__(self, send, recv, local):
        self.send, self.recv, self.local = send, recv, local
        self.sent, self.moved, self.done = [], [], []

    def to(self, peer, source, dest):
        slot = len(self.sent)
        copy = pltpu.make_async_remote_copy(
            src_ref=source,
            dst_ref=dest,
            send_sem=self.send.at[slot],
            recv_sem=self.recv.at[slot],
            device_id=peer,
            device_id_type=pl.DeviceIdType.MESH,
        )
        copy.start()
        self.sent.append(copy)
        return copy

    def drain(self, copy):
        copy.wait_send()
        self.done.append(copy)

    def finish(self):
        for copy in self.sent:
            if all(copy is not other for other in self.done):
                copy.wait_send()

    def move(self, source, dest):
        copy = pltpu.make_async_copy(source, dest, self.local.at[len(self.moved)])
        copy.start()
        self.moved.append(copy)
        return copy


def greet(peers):
    barrier = pltpu.get_barrier_semaphore()
    for peer in peers:
        pl.semaphore_signal(
            barrier, inc=1, device_id=peer, device_id_type=pl.DeviceIdType.MESH
        )
    pl.semaphore_wait(barrier, len(peers))


def by_rows(packed, frames):
    width = packed.shape[1] // frames
    return jnp.concatenate(
        [packed[:, frame * width : (frame + 1) * width] for frame in range(frames)], axis=0
    )


def own_lanes(row, head, blocks):
    part = row.shape[1] // blocks
    total = jnp.zeros((row.shape[0], part), FLOAT)
    for block in range(blocks):
        total = jnp.where(head == block, row[:, block * part : (block + 1) * part], total)
    return total


def pick(rows, first, count):
    lane = rows_iota((rows.shape[1], count))
    chosen = lane == lanes_iota((rows.shape[1], count)) + first
    return lax.dot_general(
        rows,
        chosen.astype(FLOAT),
        (((1,), (0,)), ((), ())),
        precision=lax.Precision.HIGHEST,
        preferred_element_type=FLOAT,
    )


def load_wide(wires, projections, dest, own_width):
    wide = dest.shape[0] // 3
    copies = []
    for kind in range(3):
        start = kind * wide
        copies.append(wires.move(projections.at[0, kind], dest.at[pl.ds(start, own_width)]))
        dest[start + own_width : start + wide] = jnp.zeros(
            (wide - own_width, dest.shape[1]), HALF
        )
    return copies


class Gather:
    def __init__(self, wires, peers, clip, head, sources, dest, first=0):
        self.wires, self.peers, self.dest, self.head, self.first = wires, peers, dest, head, first
        self.own, start = [], first
        for source in sources:
            count = source.shape[0]
            self.own.append(wires.move(source, dest.at[head, pl.ds(start, count)]))
            start += count
        self.rows = start - first
        self.piece = self.rows // 4
        self.half = round_up(self.piece // 2, TILE)
        self.mine = lax.rem(clip, 4)
        self.far = flip(head, 2)

    def settle(self):
        for copy in self.own:
            copy.wait()

    def spot(self, piece, first=0, count=None):
        start = pl.multiple_of(self.first + piece * self.piece + first, TILE)
        return pl.ds(start, self.piece if count is None else count)

    def begin(self):
        here = self.dest.at[self.head, self.spot(self.mine)]
        self.cross = self.wires.to(self.peers["far"], here, here)

    def begin_near(self):
        here = self.dest.at[self.head, pl.ds(self.first, self.rows)]
        self.near = self.wires.to(self.peers["near"], here, here)

    def share(self):
        self.cross.wait_recv()
        here = self.dest.at[self.far, self.spot(self.mine)]
        self.one = self.wires.to(self.peers["one"], here, here)
        self.two = self.wires.to(self.peers["two"], here, here)

    def share_again(self):
        self.two.wait_recv()
        here = self.dest.at[self.far, self.spot(flip(self.mine, 2), 0, self.half)]
        third = self.wires.to(self.peers["one"], here, here)
        self.one.wait_recv()
        here = self.dest.at[
            self.far, self.spot(flip(self.mine, 1), self.half, self.piece - self.half)
        ]
        self.rest = [third, self.wires.to(self.peers["two"], here, here)]

    def pass_on(self):
        for copy in self.rest:
            copy.wait_recv()
        here = self.dest.at[self.far, pl.ds(self.first, self.rows)]
        self.last = self.wires.to(self.peers["near"], here, here)

    def finish(self):
        self.near.wait_recv()
        self.last.wait_recv()


def time_groups(heads, groups, qkv, keep_t, weights_out, out, masks, same, equal):
    frames = qkv.shape[0]
    wide = qkv.shape[2] // 3
    total_rows = frames * TILE
    work = []
    for group in groups:
        spot = pl.ds(pl.multiple_of(group * TILE, TILE), TILE)
        piece = qkv[:, spot, :].reshape(total_rows, 3 * wide)
        kept = keep_t[spot, :]
        kept = jnp.concatenate(
            [jnp.broadcast_to(kept[:, f : f + 1], (TILE, total_rows)) for f in range(frames)],
            axis=0,
        )
        blocked = jnp.where(same & ((kept > 0.5) | equal), 0.0, MASKED)
        scores = []
        for head in range(heads):
            left = (head // 2) * PAIR
            query = piece[:, left : left + PAIR]
            key = piece[:, wide + left : wide + left + PAIR]
            scores.append(mm_t(key * masks[head % 2], query) + blocked)
        work.append((group, spot, piece, scores))
    softs = []
    for group, spot, piece, scores in work:
        found = [softmax_columns(s).astype(HALF) for s in scores]
        for head in range(heads):
            weights_out[group, head] = found[head]
        softs.append(found)
    for (group, spot, piece, _), found in zip(work, softs):
        results = []
        for pair in range(wide // PAIR):
            left = 2 * wide + pair * PAIR
            value = piece[:, left : left + PAIR]
            total = t_mm(found[2 * pair], value * masks[0])
            if 2 * pair + 1 < heads:
                total = total + t_mm(found[2 * pair + 1], value * masks[1])
            results.append(total.astype(HALF))
        joined = jnp.concatenate(results, axis=1)[:, : heads * HEAD_DIM]
        joined = joined.reshape(frames, TILE, heads * HEAD_DIM)
        local = frames // out.shape[0]
        for block in range(out.shape[0]):
            own = [joined[block * local + frame] for frame in range(local)]
            out[block, spot, :] = jnp.concatenate(own, axis=1)


def forward_kernel(
    heads,
    cuts,
    tokens_in,
    class_token,
    class_grad,
    keep,
    input_bias,
    hidden_bias,
    gains,
    shifts,
    biases,
    grads_in,
    projections,
    outputs_in,
    mixer_in,
    first_in,
    second_in,
    normed_o,
    qkv_o,
    time_soft_o,
    mixed_o,
    state_o,
    proj_o,
    space_normed_o,
    space_qkv_o,
    space_soft_o,
    spread_o,
    bundles_o,
    grad_o,
    whole_o,
    patch_out,
    class_out,
    sums_out,
    hidden_sums,
    normed,
    qkv,
    time_soft,
    mixed,
    mixed_here,
    state,
    proj,
    space_normed,
    space_qkv,
    space_soft,
    spread,
    joint,
    blocked,
    bundles,
    first,
    second,
    smalls,
    keep_t,
    time_weight,
    mixer,
    grads,
    class_parts,
    grad,
    mlp_normed,
    grads_half,
    normed_t,
    grads_t,
    total,
    normed_back,
    found,
    core_landing,
    whole,
    *rest_refs,
):
    send_sems, recv_sems, local_sems = rest_refs[-3:]
    landings = list(rest_refs[:-3])
    clip, head = lax.axis_index("clip"), lax.axis_index("head")
    patches, frames, width = tokens_in.shape
    all_frames, rows, _ = normed.shape
    blocks = all_frames // frames
    own_width = mixed.shape[2] // frames
    wide = qkv.shape[2] // 3
    flat = (frames * rows, width)
    shaped = (frames, rows, width)
    rest, block_rows = normed_t.shape[2:4]
    cut = width // cuts
    hidden = first.shape[2]
    peers = {
        "near": (clip, flip(head, 1)),
        "far": (clip, flip(head, 2)),
        "cross": (clip, flip(flip(head, 1), 2)),
        "one": (flip(clip, 1), head),
        "two": (flip(clip, 2), head),
    }
    others = [peers["near"], peers["far"], peers["cross"]]
    wires = Wires(send_sems, recv_sems, local_sems)
    gathers = {
        "O": Gather(wires, peers, clip, head, [outputs_in.at[0]], bundles),
        "P": Gather(
            wires,
            peers,
            clip,
            head,
            [projections.at[1, 0], projections.at[1, 1]],
            bundles,
            own_width,
        ),
        "Q": Gather(
            wires,
            peers,
            clip,
            head,
            [projections.at[1, 2], outputs_in.at[1]],
            bundles,
            3 * own_width,
        ),
    }
    weight_copies = load_wide(wires, projections, time_weight, own_width)
    mixer_copy = wires.move(mixer_in, mixer)
    grads_copy = wires.move(grads_in, grads)
    gathers["J"] = Gather(wires, peers, clip, head, [first_in], first)
    gathers["K"] = Gather(wires, peers, clip, head, [second_in], second)

    def run(place):
        for event in FORWARD.get(place, ()):
            item = gathers[event[0]]
            steps = {"+": item.begin, "s": item.share, "t": item.share_again, "n": item.pass_on}
            steps[event[1]]()

    for number in range(4):
        smalls[head, :, number * own_width : (number + 1) * own_width] = input_bias[
            number // 2, number % 2 : number % 2 + 1
        ]
    smalls[head, :, 4 * own_width :] = hidden_bias[...]
    keep_t[:patches] = keep[...].astype(FLOAT).T
    keep_t[patches:] = jnp.zeros((rows - patches, all_frames), FLOAT)
    greet(list(peers.values()))

    for item in gathers.values():
        item.settle()
    run("pre")
    small_copies = [wires.to(peer, smalls.at[head], smalls.at[head]) for peer in others]

    tokens = jnp.swapaxes(tokens_in[...], 0, 1)
    mine = pl.multiple_of(head * frames, frames)
    for frame in range(frames):
        unit, _ = normalize(tokens[frame].astype(FLOAT))
        normed[mine + frame, :patches] = (unit * gains[0] + shifts[0]).astype(HALF)
        normed[mine + frame, patches:] = jnp.zeros((rows - patches, width), HALF)
    own_part = normed.at[pl.ds(mine, frames)]
    near_copy = wires.to(peers["near"], own_part, own_part)
    far_copies = [wires.to(peers["far"], normed.at[mine], normed.at[mine])]

    for copy in small_copies:
        copy.wait_recv()
    bias_row = smalls[head]
    bias_gap = jnp.zeros((1, wide - own_width), FLOAT)
    query_bias = jnp.concatenate([bias_row[:, :own_width], bias_gap], axis=1)
    value_bias = jnp.concatenate([bias_row[:, own_width : 2 * own_width], bias_gap], axis=1)
    for copy in weight_copies:
        copy.wait()

    def project(block):
        start = pl.multiple_of(block * frames, frames)
        raw = mm_t(normed[pl.ds(start, frames)].reshape(flat), time_weight[...])
        query = (raw[:, :wide] + query_bias).astype(HALF) * (HEAD_DIM**-0.5)
        value = (raw[:, 2 * wide :] + value_bias).astype(HALF)
        joined = jnp.concatenate(
            [query.astype(HALF), raw[:, wide : 2 * wide].astype(HALF), value], axis=1
        )
        qkv[pl.ds(start, frames)] = joined.reshape(frames, rows, 3 * wide)

    row = rows_iota((frames * rows, 1))
    lead = (head == 0).astype(FLOAT)
    is_class = row == patches
    is_real = (lax.rem(row, rows) < patches) | is_class
    keep_all = keep_t[...]

    def prepare_grads():
        grads_copy.wait()
        back_rows = jnp.swapaxes(grads[...], 0, 1)
        for frame in range(frames):
            chosen = lanes_iota(keep_all.shape) == mine + frame
            kept = jnp.sum(jnp.where(chosen, keep_all, 0.0), axis=1, keepdims=True)
            grad[frame, :patches] = back_rows[frame].astype(FLOAT) * kept[:patches]
            grad[frame, patches:] = jnp.zeros((rows - patches, width), FLOAT)
        grad[0, patches : patches + 1] = class_grad[...].astype(FLOAT)
        values = grad[...].reshape(flat)
        grads_half[...] = values.astype(HALF)
        turned = jnp.where(is_class, values * lead, values)
        sums_out[2:3] = jnp.sum(turned, axis=0, keepdims=True)
        turned = turned.astype(HALF).T
        for part in range(cuts):
            grads_t[spread_index(clip, part, cuts, rest, cut)] = turned[part * cut : (part + 1) * cut]

    project(head)
    near_copy.wait_recv()
    project(flip(head, 1))
    run("a")
    for frame in range(1, frames):
        here = normed.at[mine + frame]
        far_copies.append(wires.to(peers["far"], here, here))
    for name in "OPQ":
        gathers[name].begin_near()
    prepare_grads()
    far_start = pl.multiple_of(flip(head, 2) * frames, frames)
    passed = []
    for frame in range(frames):
        run("f%d" % min(frame, 1))
        far_copies[frame].wait_recv()
        here = normed.at[far_start + frame]
        passed.append(wires.to(peers["near"], here, here))
        run("after%d" % min(frame, 1))
    project(flip(head, 2))
    run("p")
    for copy in passed:
        copy.wait_recv()
    project(flip(flip(head, 1), 2))
    run("b")
    saved = [wires.move(normed, normed_o), wires.move(qkv, qkv_o)]

    masks = half_masks()
    square = (all_frames * TILE,) * 2
    key_index, query_index = rows_iota(square), lanes_iota(square)
    same = lax.rem(key_index, TILE) == lax.rem(query_index, TILE)
    equal = key_index == query_index
    groups = rows // TILE
    batch = 3
    middle = (groups // batch) // 2

    def attend(start, stop):
        def body(step, carry):
            time_groups(
                heads,
                [step * batch + i for i in range(batch)],
                qkv,
                keep_t,
                time_soft,
                mixed,
                masks,
                same,
                equal,
            )
            return carry

        lax.fori_loop(start, stop, body, 0)

    def exchange(first_row, count):
        spot = pl.ds(first_row, count)
        copies = []
        for peer in others:
            copies.append(
                wires.to(peer, mixed.at[peer[1], spot], mixed_here.at[head, spot])
            )
        return copies

    cut_row = middle * batch * TILE
    attend(0, middle)
    exchanged = exchange(0, cut_row)
    run("c")
    attend(middle, groups // batch)
    for group in range(groups // batch * batch, groups):
        time_groups(heads, [group], qkv, keep_t, time_soft, mixed, masks, same, equal)
    exchanged = exchanged + exchange(cut_row, rows - cut_row)
    run("d")
    for name in "JK":
        gathers[name].begin_near()
    run("afterto")
    mixed_here[head] = mixed[head]
    saved = saved + [wires.move(time_soft, time_soft_o), wires.move(mixed, mixed_o)]
    key_index, query_index = rows_iota((rows, rows)), lanes_iota((rows, rows))
    for frame in range(frames):
        chosen = lanes_iota(keep_all.shape) == mine + frame
        kept = jnp.sum(jnp.where(chosen, keep_all, 0.0), axis=1, keepdims=True)
        allowed = (kept > 0.5) | (key_index == patches) | (key_index == query_index)
        blocked[frame] = jnp.where(allowed, 0.0, MASKED)
    mixer_copy.wait()
    run("to")
    for copy in exchanged:
        copy.wait_recv()
    run("afterto2")
    run("F1b!")
    gathers["O"].finish()
    sum_here = jnp.zeros(flat, FLOAT)
    for place in range(blocks):
        sum_here = sum_here + mm(
            by_rows(mixed_here[place], frames), bundles[place, :own_width]
        )
    half = (sum_here + biases[0:1, :]).astype(HALF)
    proj[...] = half.reshape(shaped)
    added = (mm(half, mixer[...]) + biases[1:2, :]).reshape(shaped)
    tokens = jnp.swapaxes(tokens_in[...], 0, 1)
    for frame in range(frames):
        state[frame, :patches] = tokens[frame].astype(FLOAT) + added[frame, :patches]
        state[frame, patches : patches + 1] = class_token[...].astype(FLOAT)
        state[frame, patches + 1 :] = jnp.zeros((rows - patches - 1, width), FLOAT)
    saved.append(wires.move(proj, proj_o))
    state_copy = wires.move(state, state_o)
    run("f1b")

    unit, _ = normalize(state[...].reshape(flat))
    real = lax.rem(row, rows) <= patches
    half = jnp.where(real, unit * gains[1] + shifts[1], 0.0).astype(HALF)
    space_normed[...] = half.reshape(shaped)
    run("e")
    run("q!")
    gathers["P"].finish()
    start_bias = 2 * own_width
    for kind in range(3):
        if kind == 2:
            run("f")
            run("v!")
            gathers["Q"].finish()
            saved.append(wires.move(bundles, bundles_o))
        for place in range(blocks):
            joint[place * own_width : (place + 1) * own_width] = bundles[
                place, (1 + kind) * own_width : (2 + kind) * own_width
            ]
        raw = mm_t(space_normed[...].reshape(flat), joint[...])
        if kind != 1:
            begin = start_bias + (kind // 2) * own_width
            bias = jnp.concatenate(
                [smalls[place][:, begin : begin + own_width] for place in range(blocks)], axis=1
            )
            raw = raw + bias
        raw = raw.astype(HALF)
        if kind == 0:
            raw = (raw * (HEAD_DIM**-0.5)).astype(HALF)
        space_qkv[kind] = raw.reshape(shaped)
    saved = saved + [wires.move(space_normed, space_normed_o), wires.move(space_qkv, space_qkv_o)]
    run("g")

    def one_frame(frame, carry):
        softs = []
        for pair in range(width // PAIR):
            spot = slice(pair * PAIR, (pair + 1) * PAIR)
            query, key = space_qkv[0, frame, :, spot], space_qkv[1, frame, :, spot]
            for side in range(2):
                scores = mm_t(key * masks[side], query) + blocked[frame]
                softs.append(softmax_columns(scores).astype(HALF))
                space_soft[frame, 2 * pair + side] = softs[-1]
        for pair in range(width // PAIR):
            spot = slice(pair * PAIR, (pair + 1) * PAIR)
            value = space_qkv[2, frame, :, spot]
            result = t_mm(softs[2 * pair], value * masks[0]) + t_mm(
                softs[2 * pair + 1], value * masks[1]
            )
            spread[frame, :, spot] = result.astype(HALF)
        return carry

    lax.fori_loop(0, frames, one_frame, 0)
    run("h")
    run("i")
    saved = saved + [wires.move(space_soft, space_soft_o), wires.move(spread, spread_o)]
    for place in range(blocks):
        joint[place * own_width : (place + 1) * own_width] = bundles[place, 4 * own_width :]
    added = mm(spread[...].reshape(flat), joint[...]).reshape(shaped)
    part = added[0, patches : patches + 1]
    for frame in range(1, frames):
        part = part + added[frame, patches : patches + 1]
    class_parts[head] = part * (1.0 / all_frames)
    class_copies = [
        wires.to(peer, class_parts.at[head], class_parts.at[head]) for peer in others
    ]
    state_copy.wait()
    full = state
    full[...] = state[...] + added + biases[2:3, :]
    run("cl")

    for copy in class_copies:
        copy.wait_recv()
    class_state = class_token[...].astype(FLOAT) + biases[2:3, :]
    for place in range(blocks):
        class_state = class_state + class_parts[place]
    full[0, patches : patches + 1] = class_state
    unit, _ = normalize(full[...].reshape(flat))
    values = jnp.where(is_real, unit * gains[2] + shifts[2], 0.0)
    mlp_normed[...] = values.astype(HALF)
    turned = jnp.where(is_class, values * lead, values).astype(HALF).T
    for part in range(cuts):
        normed_t[spread_index(clip, part, cuts, rest, cut)] = turned[part * cut : (part + 1) * cut]
    class_row = jnp.where(is_class, lead, 1.0)
    run("m0")
    sends, firsts = [], []
    half_lanes = [pl.ds(0, hidden), pl.ds(hidden, hidden)]
    for number, block in enumerate((1, 0, 3, 2)):
        place = flip_all(head, block, blocks)
        if number == 0:
            gathers["J"].near.wait_recv()
            gathers["K"].near.wait_recv()
        if number == 2:
            run("m4")
            run("W1!")
            gathers["J"].last.wait_recv()
            run("W2!")
            gathers["K"].last.wait_recv()
        inner = mm(mlp_normed[...], first[place]) + smalls[place][:, 4 * own_width :]
        outer = mm_t(grads_half[...], second[place])
        chance, density = gelu_parts(inner)
        active = (inner * chance).astype(HALF)
        back = (outer * (chance + inner * density)).astype(HALF)
        hidden_sums[pl.ds(place, 1)] = jnp.sum(
            back.astype(FLOAT) * class_row, axis=0, keepdims=True
        )
        if number < 2:
            run(("m1", "m3")[number])
        forward = mm(active, second[place])
        backward = mm_t(back, first[place])
        if number == 0:
            total[...] = forward
            normed_back[...] = backward
        else:
            total[...] += forward
            normed_back[...] += backward
        factors = [(normed_t, back), (grads_t, active)]
        across = number // 2
        if number % 2 == 0:
            for copy in sends:
                wires.drain(copy)
            sends = []
            for lanes, (turned, factor) in zip(half_lanes, factors):
                piece = mm(turned[...].reshape(width, frames * rows), factor)
                found[:, :, :, :, lanes] = piece.astype(HALF).reshape(
                    2, 2, rest, block_rows, hidden
                )
                sends.append(
                    wires.to(
                        peers["near"],
                        found.at[:, :, :, :, lanes],
                        core_landing.at[across, :, :, :, :, lanes],
                    )
                )
            if number == 0:
                run("m2")
            continue
        if number == 1:
            run("cs0")
        for copy, lanes, (turned, factor) in zip(sends, half_lanes, factors):
            piece = mm(turned[...].reshape(width, frames * rows), factor)
            copy.wait_recv()
            landed = core_landing[across, :, :, :, :, lanes].astype(FLOAT)
            whole[across, :, :, :, :, lanes] = (
                piece.reshape(2, 2, rest, block_rows, hidden) + landed
            ).astype(HALF)
        if across == 0:
            for name, (start, count) in column_groups(2 * hidden).items():
                lanes = pl.ds(start, count)
                landing = landings.pop(0) if HOPS[name][0] in "yz" else None
                if HOPS[name][0] == "y":
                    source, peer = whole.at[0, 1, :, :, :, lanes], peers["one"]
                elif HOPS[name][0] == "z":
                    source, peer = whole.at[0, :, 1, :, :, lanes], peers["two"]
                else:
                    continue
                firsts.append((wires.to(peer, source, landing), landing, name, lanes))
        else:
            saved.append(wires.move(whole.at[1], whole_o.at[1]))
    result = (full[...].reshape(flat) + total[...] + biases[3:4, :]).reshape(shaped)
    for frame in range(frames):
        chosen = lanes_iota(keep_all.shape) == mine + frame
        kept = jnp.sum(jnp.where(chosen, keep_all, 0.0), axis=1, keepdims=True)
        patch_out[frame] = result[frame, :patches] * kept[:patches]
    class_out[...] = own_lanes(result[0, patches : patches + 1], head, blocks)
    unit, inverse = normalize(full[...].reshape(flat))
    incoming = normed_back[...]
    weighted = jnp.where(is_class, incoming * lead, incoming)
    sums_out[0:1] = jnp.sum(weighted * unit, axis=0, keepdims=True)
    sums_out[1:2] = jnp.sum(weighted, axis=0, keepdims=True)
    sums_out[3:] = jnp.zeros((sums_out.shape[0] - 3, width), FLOAT)
    change = normalize_back(incoming * gains[2], unit, inverse)
    change = jnp.where(is_real, change, 0.0)
    grad[...] += change.reshape(shaped)
    saved.append(wires.move(grad, grad_o))
    for copy, *_ in firsts:
        copy.wait_recv()

    def add_first(index, carry):
        for _, landing, name, lanes in firsts:
            for outer in range(2):
                place = (0, 0, outer) if HOPS[name][0] == "y" else (0, outer, 0)
                spot = place + (index, slice(None), lanes)
                whole[spot] = (
                    whole[spot].astype(FLOAT) + landing[outer, index].astype(FLOAT)
                ).astype(HALF)
        return carry

    lax.fori_loop(0, rest, add_first, 0)
    wires.finish()
    saved.append(wires.move(whole.at[0], whole_o.at[0]))
    for copy in saved:
        copy.wait()


class Reduce:
    def __init__(self, wires, data, lanes, landings, hops, out, across=2, begun=None):
        self.wires, self.data, self.lanes = wires, data, lanes
        self.landings, self.hops, self.out, self.begun = landings, hops, out, begun
        self.extent = [across, 2, 2, data.shape[3]]
        self.at, self.copy = 0, None

    @property
    def idle(self):
        return self.copy is None and self.at < len(self.hops)

    def launch(self):
        axis, peer = self.hops[self.at]
        places = [pl.ds(0, size) for size in self.extent]
        if axis is not None:
            half = self.extent[axis] // 2
            places[axis] = pl.ds(half, half)
            self.extent[axis] = half
        self.first = [0, 0]
        source = self.data
        if self.begun is not None and self.at == 0:
            source = self.begun
            if axis != 0:
                places[0] = pl.ds(1, 1)
                self.first = [1, 0]
        self.copy = self.wires.to(
            peer,
            source.at[tuple(places) + (slice(None), self.lanes)],
            self.landings[self.at],
        )

    def wait(self):
        self.copy.wait_recv()
        if self.hops[self.at][0] is None:
            self.wires.drain(self.copy)
        self.copy = None

    def land(self):
        self.wait()
        landing = self.landings[self.at]
        self.at += 1
        tail = (slice(None), self.lanes)
        if self.at == len(self.hops):
            self.out(
                self.data[(0, 0, 0, 0) + tail].astype(FLOAT)
                + landing[0, 0, 0, 0].astype(FLOAT)
            )
            return
        start = self.first[0]
        _, second, third, rest = self.extent
        for place in [
            (a, b, c)
            for a in range(start, self.extent[0])
            for b in range(second)
            for c in range(third)
        ]:

            def add(index, carry):
                spot = place + (index,) + tail
                landed = landing[place[0] - start, place[1], place[2], index]
                self.data[spot] = (
                    self.data[spot].astype(FLOAT) + landed.astype(FLOAT)
                ).astype(HALF)
                return carry

            lax.fori_loop(0, rest, add, 0)


class Mixer(Reduce):
    def __init__(self, wires, data, head, near, far, landings, hops, out):
        half = data.shape[5] // 2
        bit = lax.rem(head, 2)
        super().__init__(
            wires,
            data,
            pl.ds(pl.multiple_of(bit * half, PAIR), half),
            landings,
            [None] + hops + [(None, far), None],
            out,
            1,
        )
        self.near = near
        self.other = pl.ds(pl.multiple_of((1 - bit) * half, PAIR), half)

    def launch(self):
        if self.at == 0:
            source = self.data.at[:, :, :, :, :, self.other]
        elif self.at == len(self.hops) - 1:
            source = self.data.at[0, 0, 0, 0, :, self.lanes]
        else:
            super().launch()
            return
        self.copy = self.wires.to(self.near, source, self.landings[self.at])

    def land(self):
        if 0 < self.at < len(self.hops) - 1:
            super().land()
            return
        self.copy.wait_recv()
        self.copy = None
        landing = self.landings[self.at]
        self.at += 1
        if self.at == len(self.hops):
            self.out[:, self.lanes] = self.data[0, 0, 0, 0, :, self.lanes].astype(FLOAT)
            self.out[:, self.other] = landing[...].astype(FLOAT)
            return
        for place in [(0, a, b) for a in range(2) for b in range(2)]:

            def add(index, carry):
                spot = place + (index, slice(None), self.lanes)
                self.data[spot] = (
                    self.data[spot].astype(FLOAT) + landing[place + (index,)].astype(FLOAT)
                ).astype(HALF)
                return carry

            lax.fori_loop(0, self.data.shape[3], add, 0)


class Vectors:
    def __init__(self, wires, sums, landing, peers, out):
        self.wires, self.sums, self.landing, self.peers, self.out = wires, sums, landing, peers, out
        self.at, self.copy = 0, None

    @property
    def idle(self):
        return self.copy is None and self.at < len(self.peers)

    def launch(self):
        self.copy = self.wires.to(
            self.peers[self.at], self.sums.at[self.at], self.landing.at[self.at]
        )

    def land(self):
        self.copy.wait_recv()
        self.copy = None
        total = self.sums[self.at] + self.landing[self.at]
        self.at += 1
        if self.at == len(self.peers):
            self.out(total)
        else:
            self.sums[self.at] = total


def backward_kernel(
    heads,
    cuts,
    tokens_in,
    class_token,
    gains,
    shifts,
    mlp_sums,
    hidden_sums,
    grad_in,
    bundles_in,
    projections,
    mixer_in,
    normed_in,
    qkv_in,
    time_soft_in,
    mixed_in,
    state_in,
    proj_in,
    space_normed_in,
    space_qkv_in,
    space_soft_in,
    spread_in,
    whole_in,
    patch_out,
    class_out,
    inputs_out,
    outputs_out,
    mixer_out,
    hidden_out,
    return_out,
    gains_out,
    shifts_out,
    biases_out,
    input_bias_out,
    hidden_bias_out,
    grad,
    bundles,
    time_output,
    weight,
    normed,
    qkv,
    time_soft,
    mixed,
    state,
    proj,
    space_normed,
    space_qkv,
    space_soft,
    spread,
    joint,
    outer_grad,
    mixed_back,
    proj_back,
    time_back,
    near_landing,
    far_landing,
    class_parts,
    mlp,
    space,
    space_landing,
    time_data,
    mixer_data,
    vectors,
    vector_landing,
    *rest,
):
    send_sems, recv_sems, local_sems = rest[-3:]
    landings = list(rest[:-3])
    clip, head = lax.axis_index("clip"), lax.axis_index("head")
    patches, frames, width = tokens_in.shape
    all_frames, rows, _ = normed.shape
    blocks = all_frames // frames
    own_width = mixed.shape[2] // frames
    wide = qkv.shape[2] // 3
    flat = (frames * rows, width)
    shaped = (frames, rows, width)
    cut = width // cuts
    rest_size = mlp.shape[3]
    hidden = mlp.shape[5] // 2
    near, far = flip(head, 1), flip(head, 2)
    cross = flip(near, 2)
    near_peer, far_peer, cross_peer = (clip, near), (clip, far), (clip, cross)
    others = [near_peer, far_peer, cross_peer]
    clip_peers = []
    bit = 1
    while bit < cuts:
        clip_peers.append((flip(clip, bit), head))
        bit *= 2
    wires = Wires(send_sems, recv_sems, local_sems)
    order = [
        (grad_in, grad),
        (bundles_in.at[:, pl.ds(own_width, 4 * own_width)], bundles),
        (space_soft_in, space_soft),
        (space_qkv_in, space_qkv),
        (state_in, state),
        (mixer_in, weight),
    ]
    order_later = [
        (whole_in, mlp),
        (space_normed_in, space_normed),
        (spread_in, spread),
        (proj_in, proj),
        (qkv_in, qkv),
        (time_soft_in, time_soft),
        (bundles_in.at[head, pl.ds(0, own_width)], time_output),
        (normed_in, normed),
        (mixed_in, mixed),
    ]
    ready = {id(dest): wires.move(source, dest) for source, dest in order}

    def need(*refs):
        for ref in refs:
            ready[id(ref)].wait()

    greet(others + clip_peers)
    clip_hops = [
        (3 if 1 << number < rest_size else None, peer)
        for number, peer in enumerate(clip_peers[2:])
    ]
    steps = {
        "x": [(0, far_peer)],
        "y": [(1, clip_peers[0])],
        "z": [(2, clip_peers[1])],
        "w": clip_hops,
    }
    chains = {}

    def take(name):
        hops = [hop for code in HOPS[name] for hop in steps[code]]
        return hops, [landings.pop(0) for _ in hops]

    def chain(name, data, lanes, out, across=2, begun=None):
        hops, mine = take(name)
        chains[name] = Reduce(wires, data, lanes, mine, hops, out, across, begun)

    def run(place):
        for event in SCHEDULE.get(place, ()):
            if event[-1] == "+":
                chains[event[:-1]].launch()
            else:
                chains[event[:-1]].land()

    def put_inputs(layer, first, second):
        def write(value):
            for number, kind in enumerate((first, second)):
                piece = value[:, number * own_width : (number + 1) * own_width]
                if kind == 3:
                    outputs_out[layer] = piece.T
                else:
                    inputs_out[layer, kind] = piece

        return write

    def put_hidden(start, count):
        def write(value):
            inner = max(0, min(count, hidden - start))
            if inner:
                hidden_out[:, start : start + inner] = value[:, :inner]
            if count > inner:
                first = start + inner - hidden
                return_out[:, first : first + count - inner] = value[:, inner:]

        return write

    middle = 2 * own_width
    left, right = pl.ds(0, middle), pl.ds(middle, middle)
    for name, (start, count) in column_groups(2 * hidden).items():
        chain(
            name,
            mlp,
            pl.ds(start, count),
            put_hidden(start, count),
            2,
            whole_in,
        )
    chain("S", space.at[0], left, put_inputs(1, 0, 1))
    chain("R", space.at[0], right, put_inputs(1, 2, 3))
    chain("T", time_data, left, put_inputs(0, 3, 0), 1)
    chain("U", time_data, right, put_inputs(0, 1, 2), 1)
    hops, mine = take("X")
    mine = [landings.pop(0)] + mine + [landings.pop(0), landings.pop(0)]
    chains["X"] = Mixer(wires, mixer_data, head, near_peer, far_peer, mine, hops, mixer_out)

    def put_vectors(total):
        part = width // (blocks * cuts)
        shared = pick(total[:10], (clip * blocks + head) * part, part)
        for place in range(3):
            gains_out[place] = shared[place : place + 1]
            shifts_out[place] = shared[3 + place : 4 + place]
        biases_out[...] = shared[6:10]
        other = pick(total[10:14], (head * cuts + clip) * part, part)
        input_bias_out[0] = other[0:2]
        input_bias_out[1] = other[2:4]
        chosen = rows_iota((blocks, 1)) == head
        row = jnp.sum(jnp.where(chosen, total[14 : 14 + blocks], 0.0), axis=0, keepdims=True)
        hidden_bias_out[...] = pick(row, clip * (hidden // cuts), hidden // cuts)

    chains["V"] = Vectors(
        wires, vectors, vector_landing, [near_peer, far_peer] + clip_peers, put_vectors
    )
    run("begin")

    need(grad)
    lead = (head == 0).astype(FLOAT)
    row = lax.rem(rows_iota((frames * rows, 1)), rows)
    is_patch = row < patches
    class_grad = grad[0, patches : patches + 1]
    values = grad[...].reshape(flat)
    sums = {}
    sums["bias2"] = (
        jnp.sum(jnp.where(is_patch, values, 0.0), axis=0, keepdims=True) + lead * class_grad
    )
    values = jnp.where(
        is_patch, values, jnp.where(row == patches, class_grad * (1.0 / all_frames), 0.0)
    )
    half = values.astype(HALF)
    outer_grad[...] = half.reshape(shaped)
    ready.update({id(dest): wires.move(source, dest) for source, dest in order_later})
    need(bundles)
    for place in range(blocks):
        joint[place * own_width : (place + 1) * own_width] = bundles[place, 3 * own_width :]
    mixed_back[...] = mm_t(outer_grad[...].reshape(flat), joint[...]).astype(HALF).reshape(shaped)

    need(space_soft, space_qkv)
    masks = half_masks()

    def one_frame(frame, carry):
        pairs = width // PAIR
        for group in range(2):
            chosen = range(group * pairs // 2, (group + 1) * pairs // 2)
            backs, mines = [], []
            for pair in chosen:
                spot = slice(pair * PAIR, (pair + 1) * PAIR)
                value = space_qkv[2, frame, :, spot]
                for side in range(2):
                    mine = mixed_back[frame, :, spot] * masks[side]
                    mines.append(mine)
                    backs.append(mm_t(value, mine))
            scores = []
            for number, pair in enumerate(chosen):
                for side in range(2):
                    soft = space_soft[frame, 2 * pair + side].astype(FLOAT)
                    product = soft * backs[2 * number + side]
                    score = product - soft * jnp.sum(product, axis=0, keepdims=True)
                    scores.append(score.astype(HALF))
            for number, pair in enumerate(chosen):
                spot = slice(pair * PAIR, (pair + 1) * PAIR)
                query, key = space_qkv[0, frame, :, spot], space_qkv[1, frame, :, spot]
                left, right = scores[2 * number], scores[2 * number + 1]
                value_back = mm(space_soft[frame, 2 * pair], mines[2 * number]) + mm(
                    space_soft[frame, 2 * pair + 1], mines[2 * number + 1]
                )
                key_back = mm(left, query * masks[0]) + mm(right, query * masks[1])
                query_back = t_mm(left, key * masks[0]) + t_mm(right, key * masks[1])
                space_qkv[0, frame, :, spot] = (query_back * (HEAD_DIM**-0.5)).astype(HALF)
                space_qkv[1, frame, :, spot] = key_back.astype(HALF)
                space_qkv[2, frame, :, spot] = value_back.astype(HALF)
        return carry

    lax.fori_loop(0, frames, one_frame, 0)
    incoming = jnp.zeros(flat, FLOAT)
    for kind in range(3):
        for place in range(blocks):
            joint[place * own_width : (place + 1) * own_width] = bundles[
                place, kind * own_width : (1 + kind) * own_width
            ]
        piece = space_qkv[kind].reshape(flat)
        incoming = incoming + mm(piece, joint[...])
        if kind != 1:
            sums["space%d" % kind] = jnp.sum(piece.astype(FLOAT), axis=0, keepdims=True)
    need(state)
    unit, inverse = normalize(state[...].reshape(flat))
    sums["gain1"] = jnp.sum(incoming * unit, axis=0, keepdims=True)
    sums["shift1"] = jnp.sum(incoming, axis=0, keepdims=True)
    by_frame = incoming.reshape(shaped)
    part = by_frame[0, patches : patches + 1]
    for frame in range(1, frames):
        part = part + by_frame[frame, patches : patches + 1]
    class_parts[head] = part
    class_state_grad = class_grad
    change = normalize_back(incoming * gains[1], unit, inverse)
    result = jnp.where(is_patch, grad[...].reshape(flat) + change, 0.0)
    grad[...] = result.reshape(shaped)
    need(mlp)
    run("b")
    sums["bias1"] = jnp.sum(result, axis=0, keepdims=True)
    half = result.astype(HALF)
    time_grad = mixed_back
    time_grad[...] = half.reshape(shaped)
    need(weight)
    back = mm_t(time_grad[...].reshape(flat), weight[...]).astype(HALF)
    mine = pl.multiple_of(head * frames, frames)
    proj_back[pl.ds(mine, frames)] = back.reshape(shaped)
    far_copies = [
        wires.to(far_peer, proj_back.at[mine + frame], proj_back.at[mine + frame])
        for frame in range(frames)
    ]
    own_part = proj_back.at[pl.ds(mine, frames)]
    near_copy = wires.to(near_peer, own_part, own_part)
    class_copies = [
        wires.to(peer, class_parts.at[head], class_parts.at[head]) for peer in others
    ]
    sums["bias0"] = jnp.sum(back.astype(FLOAT), axis=0, keepdims=True)

    weight_copies = load_wide(wires, projections, weight, own_width)

    need(space_normed, spread, proj)

    def place_rows(part, result):
        return result[part * cut : (part + 1) * cut]

    def send_core(lanes):
        return wires.to(
            near_peer,
            space.at[1, :, :, :, :, :, lanes],
            space_landing.at[:, :, :, :, :, lanes],
        )

    core_copies = []
    turned = space_normed[...].reshape(flat).T
    for kind in range(4):
        if kind == 2:
            core_copies.append(send_core(left))
            run("sw")
        if kind == 3:
            turned = outer_grad[...].reshape(flat).T
            result = mm(turned, spread[...].reshape(flat)).astype(HALF)
        else:
            result = mm(turned, space_qkv[kind].reshape(flat)).astype(HALF)
        for block in range(blocks):
            relative = flip_all(head, block, blocks)
            core, across = lax.rem(relative, 2), lax.div(relative, 2)
            for part in range(cuts):
                space[
                    (core, across)
                    + spread_index(clip, part, cuts, rest_size, cut)
                    + (slice(kind * own_width, (kind + 1) * own_width),)
                ] = place_rows(part, result)[:, block * own_width : (block + 1) * own_width]
    core_copies.append(send_core(right))
    turned = proj[...].reshape(flat).T
    result = mm(turned, time_grad[...].reshape(flat)).astype(HALF)
    for part in range(cuts):
        mixer_data[(0,) + spread_index(clip, part, cuts, rest_size, cut)] = place_rows(part, result)
    run("X")
    run("x1")

    need(qkv, time_soft, time_output)
    for copy in weight_copies:
        copy.wait()

    def outer(block):
        start = pl.multiple_of(block * frames, frames)
        back = mm_t(proj_back[pl.ds(start, frames)].reshape(flat), time_output[...])
        back = back.astype(HALF)
        gap = jnp.zeros((frames * rows, wide - own_width), HALF)
        time_back[pl.ds(start, frames)] = jnp.concatenate([back, gap], axis=1).reshape(
            frames, rows, wide
        )

    outer(head)
    near_copy.wait_recv()
    outer(near)
    run("x2")

    def add_core(lanes):
        for place in [(a, b, c) for a in range(2) for b in range(2) for c in range(2)]:

            def add(index, carry):
                spot = place + (index, slice(None), lanes)
                space[(0,) + spot] = (
                    space[(0,) + spot].astype(FLOAT) + space_landing[spot].astype(FLOAT)
                ).astype(HALF)
                return carry

            lax.fori_loop(0, rest_size, add, 0)

    for number, lanes in enumerate((left, right)):
        run(("c1", "c2")[number])
        core_copies[number].wait_recv()
        add_core(lanes)
        run(("S", "R")[number])
    run("c3")
    passed = []
    for frame in range(frames):
        run(("ag0", "ag1")[min(frame, 1)])
        far_copies[frame].wait_recv()
        here = proj_back.at[far * frames + frame]
        passed.append(wires.to(near_peer, here, here))
    run("ag2")
    outer(far)
    for frame in range(frames):
        run(("p0", "p1")[min(frame, 1)])
        passed[frame].wait_recv()
    outer(cross)
    total_rows = all_frames * TILE
    groups = rows // TILE
    batch = 3

    def time_backward(chosen):
        work = []
        for group in chosen:
            spot = pl.ds(pl.multiple_of(group * TILE, TILE), TILE)
            piece = qkv[:, spot, :].reshape(total_rows, 3 * wide)
            outers = time_back[:, spot, :].reshape(total_rows, wide)
            backs, mines = [], []
            for number in range(heads):
                left = (number // 2) * PAIR
                own = outers[:, left : left + PAIR] * masks[number % 2]
                mines.append(own)
                backs.append(mm_t(piece[:, 2 * wide + left : 2 * wide + left + PAIR], own))
            work.append((group, spot, piece, mines, backs))
        for group, spot, piece, mines, backs in work:
            parts = [[], [], []]
            for pair in range(wide // PAIR):
                left = pair * PAIR
                query = piece[:, left : left + PAIR]
                key = piece[:, wide + left : wide + left + PAIR]
                found = None
                for side in range(2):
                    number = 2 * pair + side
                    if number >= heads:
                        continue
                    soft = time_soft[group, number]
                    large = soft.astype(FLOAT)
                    product = large * backs[number]
                    score = product - large * jnp.sum(product, axis=0, keepdims=True)
                    score = score.astype(HALF)
                    terms = [
                        t_mm(score, key * masks[side]),
                        mm(score, query * masks[side]),
                        mm(soft, mines[number]),
                    ]
                    found = terms if found is None else [x + y for x, y in zip(found, terms)]
                for kind, scale in enumerate((HEAD_DIM**-0.5, 1.0, 1.0)):
                    parts[kind].append((found[kind] * scale).astype(HALF))
            joined = jnp.concatenate(parts[0] + parts[1] + parts[2], axis=1)
            qkv[:, spot, :] = joined.reshape(all_frames, TILE, 3 * wide)

    def body(step, carry):
        time_backward([step * batch + i for i in range(batch)])
        return carry

    lax.fori_loop(0, groups // batch, body, 0)
    for group in range(groups // batch * batch, groups):
        time_backward([group])

    need(normed)
    run("at")
    norm_sums = [jnp.zeros((1, width), FLOAT), jnp.zeros((1, width), FLOAT)]
    bias_sums = jnp.zeros((1, 3 * wide), FLOAT)

    def inner(block):
        start = pl.multiple_of(block * frames, frames)
        piece = qkv[pl.ds(start, frames)].reshape(frames * rows, 3 * wide)
        result = mm(piece, weight[...])
        values = normed[pl.ds(start, frames)].reshape(flat).astype(FLOAT)
        norm_sums[0] = norm_sums[0] + jnp.sum(result * values, axis=0, keepdims=True)
        norm_sums[1] = norm_sums[1] + jnp.sum(result, axis=0, keepdims=True)
        return result, jnp.sum(piece.astype(FLOAT), axis=0, keepdims=True)

    result, more = inner(cross)
    bias_sums = bias_sums + more
    space_qkv[0] = result.astype(HALF).reshape(shaped)
    back_cross = wires.to(near_peer, space_qkv.at[0], near_landing.at[0])
    result, more = inner(far)
    bias_sums = bias_sums + more
    run("rc0")
    back_cross.wait_recv()
    result = result + near_landing[0].reshape(flat).astype(FLOAT)
    space_qkv[1] = result.astype(HALF).reshape(shaped)
    back_far = wires.to(far_peer, space_qkv.at[1], far_landing)
    result, more = inner(near)
    bias_sums = bias_sums + more
    space_qkv[2] = result.astype(HALF).reshape(shaped)
    back_near = wires.to(near_peer, space_qkv.at[2], near_landing.at[1])
    run("rn")
    result, more = inner(head)
    bias_sums = bias_sums + more
    outer_grad[...] = result.astype(HALF).reshape(shaped)

    sums["gain0"] = (norm_sums[0] - norm_sums[1] * shifts[0]) / gains[0]
    sums["shift0"] = norm_sums[1]
    lane = lanes_iota((1, width))
    here = (lane >= head * own_width) & (lane < (head + 1) * own_width)
    for kind in (0, 2):
        own = bias_sums[:, kind * wide : kind * wide + own_width]
        repeated = jnp.concatenate([own] * blocks, axis=1)
        sums["time%d" % kind] = jnp.where(here, repeated, 0.0)
    names = [
        sums["gain0"],
        sums["gain1"],
        mlp_sums[0:1],
        sums["shift0"],
        sums["shift1"],
        mlp_sums[1:2],
        sums["bias0"],
        sums["bias1"],
        sums["bias2"],
        mlp_sums[2:3],
        sums["time0"],
        sums["time2"],
        sums["space0"],
        sums["space2"],
    ]
    for number, value in enumerate(names):
        vectors[0, number : number + 1] = value
    vectors[0, len(names) : len(names) + blocks] = hidden_sums[...]
    vectors[0, len(names) + blocks :] = jnp.zeros(
        (vectors.shape[1] - len(names) - blocks, width), FLOAT
    )
    run("V")
    run("v")

    need(mixed)

    def over_blocks(left, right):
        total = None
        for block in range(blocks):
            spot = slice(block * frames, (block + 1) * frames)
            term = t_mm(left[spot].reshape(flat), right(block, spot))
            total = term if total is None else total + term
        return total

    def put_time(kind, result):
        result = result.astype(HALF)
        lanes = slice(kind * own_width, (kind + 1) * own_width)
        for part in range(cuts):
            time_data[(0,) + spread_index(clip, part, cuts, rest_size, cut) + (lanes,)] = (
                place_rows(part, result)
            )

    def columns(kind):
        first = kind * wide
        return lambda block, spot: qkv[spot, :, first : first + wide].reshape(
            frames * rows, wide
        )

    put_time(0, over_blocks(proj_back, lambda block, spot: by_rows(mixed[block], frames)))
    put_time(1, over_blocks(normed, columns(0))[:, :own_width])
    run("T")
    run("t1")
    put_time(2, over_blocks(normed, columns(1))[:, :own_width])
    run("t2")
    put_time(3, over_blocks(normed, columns(2))[:, :own_width])
    run("U")
    run("t3")

    tokens = jnp.swapaxes(tokens_in[...], 0, 1)
    back_near.wait_recv()
    run("rx")
    back_far.wait_recv()
    for frame in range(frames):
        unit, inverse = normalize(tokens[frame].astype(FLOAT))
        incoming = (
            outer_grad[frame, :patches].astype(FLOAT)
            + near_landing[1, frame, :patches].astype(FLOAT)
            + far_landing[frame, :patches].astype(FLOAT)
        )
        patch_out[frame] = grad[frame, :patches] + normalize_back(
            incoming * gains[0], unit, inverse
        )
    for copy in class_copies:
        copy.wait_recv()
    unit, inverse = normalize(class_token[...].astype(FLOAT))
    incoming = class_parts[0]
    for place in range(1, blocks):
        incoming = incoming + class_parts[place]
    result = class_state_grad + normalize_back(incoming * gains[1], unit, inverse)
    class_out[...] = own_lanes(result, head, blocks)

    run("fin")
    run("tail")
    while True:
        for item in chains.values():
            if item.idle:
                item.launch()
        live = [item for item in chains.values() if item.copy is not None]
        if not live:
            break
        for item in live:
            item.land()
    wires.finish()


def deliver_kernel(index, patch_first, patch_second, mixer, *refs):
    count = (len(refs) - 3) // 2
    first, second, mixer_out = refs[count : count + 3]
    first[...] = jnp.swapaxes(patch_first[...], 0, 1)
    second[...] = jnp.swapaxes(patch_second[...], 0, 1)
    share = mixer_out.shape[0]
    total = jnp.zeros(mixer_out.shape, FLOAT)
    head = index[0]
    for block in range(mixer.shape[0] // share):
        total = jnp.where(head == block, mixer[block * share : (block + 1) * share], total)
    mixer_out[...] = total
    for source, dest in zip(refs[:count], refs[count + 3 :]):
        dest[...] = source[...]


VMEM = pl.BlockSpec(memory_space=pltpu.VMEM)
ANY = pl.BlockSpec(memory_space=pl.ANY)
WIRES = 96
LIMIT = 125 * 2**19


def shape(dims, kind=HALF):
    return jax.ShapeDtypeStruct(tuple(dims), kind)


def room(dims, kind=HALF):
    return pltpu.VMEM(tuple(dims), kind)


def landing_rooms(axes, start, rest, cut, columns, begun):
    extent = list(start) + [rest]
    found = []
    for axis in axes:
        if axis is not None:
            extent[axis] //= 2
        first = [1] if begun and not found else extent[:1]
        found.append(room(first + extent[1:] + [cut, columns]))
    return found


def on_device(
    patch_tokens,
    class_token,
    keep_mask,
    patch_grad,
    class_grad,
    norm_gain,
    norm_bias,
    input_weight,
    input_bias,
    output_weight,
    time_mixer,
    output_bias,
    hidden_weight,
    hidden_bias,
    return_weight,
):
    blocks = lax.axis_size("head")
    clips = lax.axis_size("clip")
    head_index = lax.axis_index("head")
    clip_index = lax.axis_index("clip")
    _, frames, patches, width = patch_tokens.shape
    all_frames = keep_mask.shape[1]
    own_width = input_weight.shape[-1]
    heads = own_width // HEAD_DIM
    all_heads = heads * blocks
    hidden = hidden_weight.shape[-1]
    rows = round_up(patches + 1, TILE)
    groups = rows // TILE
    group_rows = all_frames * TILE
    wide = round_up(own_width, PAIR)
    cut = width // clips
    dense = 1
    while cut * dense % TILE:
        dense *= 2
    block_rows = cut * dense
    rest = clips // (4 * dense)
    tokens = frames * rows
    biases = output_bias[0]
    patch_state = jnp.transpose(patch_tokens[0], (1, 0, 2))
    patch_back = jnp.transpose(patch_grad[0], (1, 0, 2))

    projections = jnp.transpose(input_weight[0], (0, 2, 3, 1))
    gains = jnp.transpose(norm_gain, (1, 0, 2))
    shifts = jnp.transpose(norm_bias, (1, 0, 2))

    full = (frames, rows, width)
    everything = (all_frames, rows, width)
    qkv_dims = (all_frames, rows, 3 * wide)
    time_soft_dims = (groups, heads, group_rows, group_rows)
    mixed_dims = (blocks, rows, frames * own_width)
    space_soft_dims = (frames, all_heads, rows, rows)
    bundle_dims = (blocks, 5 * own_width, width)
    halves = (2, 2, 2, rest, block_rows, 2 * hidden)
    kept_outs = [
        shape(everything),
        shape(qkv_dims),
        shape(time_soft_dims),
        shape(mixed_dims),
        shape(full, FLOAT),
        shape(full),
        shape(full),
        shape((3,) + full),
        shape(space_soft_dims),
        shape(full),
        shape(bundle_dims),
        shape(full, FLOAT),
        shape(halves),
    ]
    direct_outs = [
        shape((frames, patches, width), FLOAT),
        shape((1, width // blocks), FLOAT),
        shape((8, width), FLOAT),
        shape((blocks, hidden), FLOAT),
    ]
    sems = [pltpu.SemaphoreType.DMA((WIRES,))] * 3
    (
        normed, qkv, time_soft, mixed, state, proj, space_normed, space_qkv, space_soft, spread,
        bundles, grads, whole, patch_out, class_out, mlp_sums, hidden_sums,
    ) = pl.pallas_call(
        functools.partial(forward_kernel, heads, clips),
        out_shape=kept_outs + direct_outs,
        in_specs=[VMEM] * 9 + [ANY] * 6,
        out_specs=[ANY] * len(kept_outs) + [VMEM] * len(direct_outs),
        scratch_shapes=[
            room(everything),
            room(qkv_dims),
            room(time_soft_dims),
            room(mixed_dims),
            room(mixed_dims),
            room(full, FLOAT),
            room(full),
            room(full),
            room((3,) + full),
            room(space_soft_dims),
            room(full),
            room((width, width)),
            room((frames, rows, rows), FLOAT),
            room(bundle_dims),
            room((blocks, width, hidden)),
            room((blocks, hidden, width)),
            room((blocks, 1, 4 * own_width + hidden), FLOAT),
            room((rows, all_frames), FLOAT),
            room((3 * wide, width)),
            room((width, width)),
            room((patches, frames, width)),
            room((blocks, 1, width), FLOAT),
            room(full, FLOAT),
            room((tokens, width)),
            room((tokens, width)),
            room((2, 2, rest, block_rows, tokens)),
            room((2, 2, rest, block_rows, tokens)),
            room((tokens, width), FLOAT),
            room((tokens, width), FLOAT),
            room(halves[1:]),
            room(halves),
            room(halves),
        ]
        + [
            room((2, rest, block_rows, count))
            for name, (_, count) in column_groups(2 * hidden).items()
            if HOPS[name][0] in "yz"
        ]
        + sems,
        cost_estimate=pl.CostEstimate(
            flops=int(30e9), bytes_accessed=int(40e6), transcendentals=0
        ),
        compiler_params=pltpu.CompilerParams(
            vmem_limit_bytes=LIMIT, collective_id=0, has_side_effects=True
        ),
        name="forward",
    )(
        patch_state,
        class_token,
        class_grad,
        keep_mask[0],
        input_bias[0],
        hidden_bias,
        gains,
        shifts,
        biases,
        patch_back,
        projections,
        output_weight[0],
        time_mixer[0],
        hidden_weight[0],
        return_weight[0],
    )

    clip_bits = clips.bit_length() - 1
    later = [3 if 1 << number < rest else None for number in range(clip_bits - 2)]
    steps = {"x": [0], "y": [1], "z": [2], "w": later}
    vector_rows = round_up(14 + blocks, 8)
    vector_hops = 2 + clip_bits
    pieces = [
        (name, 2, count, HOPS[name][0] != "x")
        for name, (_, count) in column_groups(2 * hidden).items()
    ]
    middle = 2 * own_width
    pieces += [("S", 2, middle, False), ("R", 2, middle, False)]
    pieces += [("T", 1, middle, False), ("U", 1, middle, False)]
    landings = []
    for name, across, columns, begun in pieces:
        axes = [axis for code in HOPS[name] for axis in steps[code]]
        landings += landing_rooms(axes, (across, 2, 2), rest, block_rows, columns, begun)
    axes = [axis for code in HOPS["X"] for axis in steps[code]]
    half_width = width // 2
    landings += landing_rooms(axes, (1, 2, 2), rest, block_rows, half_width, False)
    landings.append(room((1, 2, 2, rest, block_rows, half_width)))
    landings.append(room((1, 1, 1, 1, block_rows, half_width)))
    landings.append(room((block_rows, half_width)))
    part = width // (clips * blocks)
    hidden_part = hidden // clips
    (
        patch_input_grad, class_input_grad, inputs_total, outputs_total, mixer_total,
        hidden_total, return_total, gain_grad, shift_grad, bias_grad, input_bias_grad,
        hidden_bias_grad,
    ) = pl.pallas_call(
        functools.partial(backward_kernel, heads, clips),
        out_shape=[
            shape((frames, patches, width), FLOAT),
            shape((1, width // blocks), FLOAT),
            shape((2, 3, block_rows, own_width), FLOAT),
            shape((2, own_width, block_rows), FLOAT),
            shape((block_rows, width), FLOAT),
            shape((block_rows, hidden), FLOAT),
            shape((block_rows, hidden), FLOAT),
            shape((3, 1, part), FLOAT),
            shape((3, 1, part), FLOAT),
            shape((4, part), FLOAT),
            shape((2, 2, part), FLOAT),
            shape((1, hidden_part), FLOAT),
        ],
        in_specs=[VMEM] * 6 + [ANY] * 15,
        out_specs=[VMEM] * 12,
        scratch_shapes=[
            room(full, FLOAT),
            room((blocks, 4 * own_width, width)),
            room((own_width, width)),
            room((width, width)),
            room(everything),
            room(qkv_dims),
            room(time_soft_dims),
            room(mixed_dims),
            room(full, FLOAT),
            room(full),
            room(full),
            room((3,) + full),
            room(space_soft_dims),
            room(full),
            room((width, width)),
            room(full),
            room(full),
            room(everything),
            room((all_frames, rows, wide)),
            room((2,) + full),
            room(full),
            room((blocks, 1, width), FLOAT),
            room(halves),
            room((2, 2, 2, 2, rest, block_rows, 4 * own_width)),
            room((2, 2, 2, rest, block_rows, 4 * own_width)),
            room((1, 2, 2, rest, block_rows, 4 * own_width)),
            room((1, 2, 2, rest, block_rows, width)),
            room((vector_hops, vector_rows, width), FLOAT),
            room((vector_hops, vector_rows, width), FLOAT),
        ]
        + landings
        + sems,
        cost_estimate=pl.CostEstimate(
            flops=int(20e9), bytes_accessed=int(40e6), transcendentals=0
        ),
        compiler_params=pltpu.CompilerParams(
            vmem_limit_bytes=LIMIT, collective_id=1, has_side_effects=True
        ),
        name="backward",
    )(
        patch_state,
        class_token,
        gains,
        shifts,
        mlp_sums,
        hidden_sums,
        grads,
        bundles,
        projections,
        time_mixer[0],
        normed,
        qkv,
        time_soft,
        mixed,
        state,
        proj,
        space_normed,
        space_qkv,
        space_soft,
        spread,
        whole,
    )

    if dense > 1:
        start = lax.div(clip_index, clips // dense) * cut
        inputs_total = lax.dynamic_slice_in_dim(inputs_total, start, cut, 2)
        outputs_total = lax.dynamic_slice_in_dim(outputs_total, start, cut, 2)
        mixer_total, hidden_total, return_total = [
            lax.dynamic_slice_in_dim(total, start, cut, 0)
            for total in (mixer_total, hidden_total, return_total)
        ]
    share = cut // blocks
    small = [
        class_out,
        class_input_grad,
        gain_grad,
        shift_grad,
        inputs_total,
        input_bias_grad,
        outputs_total,
        bias_grad,
        hidden_total,
        hidden_bias_grad,
        return_total,
    ]
    whole_patch = shape((patches, frames, width), FLOAT)
    (
        patch_out, patch_input_grad, mixer_grad, class_out, class_input_grad, gain_grad,
        shift_grad, inputs_total, input_bias_grad, outputs_total, bias_grad, hidden_total,
        hidden_bias_grad, return_total,
    ) = pl.pallas_call(
        deliver_kernel,
        out_shape=[whole_patch, whole_patch, shape((share, width), FLOAT)]
        + [shape(a.shape, FLOAT) for a in small],
        in_specs=[pl.BlockSpec(memory_space=pltpu.SMEM)] + [VMEM] * (3 + len(small)),
        out_specs=[VMEM] * (3 + len(small)),
        compiler_params=pltpu.CompilerParams(vmem_limit_bytes=LIMIT),
        name="deliver",
    )(head_index.astype(jnp.int32)[None], patch_out, patch_input_grad, mixer_total, *small)
    return (
        jnp.transpose(patch_out, (1, 0, 2))[None],
        class_out,
        jnp.transpose(patch_input_grad, (1, 0, 2))[None],
        class_input_grad,
        jnp.transpose(gain_grad, (1, 0, 2)),
        jnp.transpose(shift_grad, (1, 0, 2)),
        jnp.transpose(inputs_total, (0, 2, 1, 3))[None],
        input_bias_grad[None],
        outputs_total[None],
        mixer_grad[None],
        bias_grad[None],
        hidden_total[None],
        hidden_bias_grad,
        return_total.T[None],
    )


def solution(mesh):
    in_specs = (
        P("clip", "head", None, None),
        P("clip", None),
        P("clip", None, None),
        P("clip", "head", None, None),
        P("clip", None),
        P(),
        P(),
        P(None, None, None, None, "head"),
        P(None, None, None, "head"),
        P(None, None, "head", None),
        P(),
        P(),
        P(None, None, "head"),
        P(None, "head"),
        P(None, "head", None),
    )
    out_specs = (
        P("clip", "head", None, None),
        P("clip", "head"),
        P("clip", "head", None, None),
        P("clip", "head"),
        P(None, None, ("clip", "head")),
        P(None, None, ("clip", "head")),
        P(None, None, "clip", None, "head"),
        P(None, None, None, ("head", "clip")),
        P(None, None, "head", "clip"),
        P(None, ("clip", "head"), None),
        P(None, None, ("clip", "head")),
        P(None, "clip", "head"),
        P(None, ("head", "clip")),
        P(None, "head", "clip"),
    )
    return jax.shard_map(
        on_device, mesh=mesh, in_specs=in_specs, out_specs=out_specs, check_vma=False
    )
```
